256 devices in a mesh: lon: 32 (over z, x), lat: 8 (over y, core).
Axes of the slice: x: 4, y: 4, z: 8, core: 2. Of those that a mesh axis runs over, the one named last changes fastest.
Arguments:
- warmth_deviation: float32 [10, 512, 4096], P(None, 'lat', 'lon'), may hold values from -6 to 6
- saltiness_deviation: float32 [10, 512, 4096], P(None, 'lat', 'lon'), may hold values from -6 to 6
- easterly_speed: float32 [10, 512, 4096], P(None, 'lat', 'lon'), may hold values from -6 to 6
- poleward_speed: float32 [10, 512, 4096], P(None, 'lat', 'lon'), may hold values from -6 to 6
- stratum_spans: float32 [10], replicated, may hold values from 0.5 to 2
- water_indicator: int32 [512, 4096], P('lat', 'lon'), may hold values 0 or 1
- opposite_counterpart: int32 [4096], P('lon'), may hold values from 0 to 4095, as said below
- elevation_weights: float32 [512, 4096], P('lat', 'lon'), may hold values from 0.2 to 2
- elevation_anomaly: float32 [512, 4096], P('lat', 'lon'), may hold values from -3 to 17
Outputs:
- new_temperature: float32 [10, 512, 4096], P(None, 'lat', 'lon')
- new_salinity: float32 [10, 512, 4096], P(None, 'lat', 'lon')
- new_zonal: float32 [10, 512, 4096], P(None, 'lat', 'lon')
- new_meridional: float32 [10, 512, 4096], P(None, 'lat', 'lon')
- new_surface: float32 [512, 4096], P('lat', 'lon')
The draws below stay inside these ranges and needn't reach their ends.
Inputs may be any that keep to these rules, and one draw needn't show every extreme that they name: opposite_counterpart[x] = (h - 1 - x) mod 4096 for a hinge column h chosen by the draw, so opposite_counterpart[opposite_counterpart[x]] = x.
All inputs are finite; a program needn't handle non-finite values. No bound on the sum of `water_indicator` on one device may be relied on, other than what follows from the above.
Results may differ from the reference program's by a relative error of at most 0.0001.
Values sent between devices are 32-bit elements; how exact they have to be, the bound alone decides.
A program may use at most 64 MiB of HBM per device.

```python
import math
import jax
import jax.numpy as jnp

STRATA_COUNT = 10
ITERS = 3
EASTWARD_CELLS = 4096
POLEWARD_CELLS = 512


def draw_opposite_counterpart(key, part):
    key = jax.random.fold_in(key, 11)
    hinge = jax.random.randint(key, (), 0, EASTWARD_CELLS)
    return jnp.mod(hinge - 1 - jnp.arange(EASTWARD_CELLS, dtype=jnp.int32), EASTWARD_CELLS).astype(jnp.int32)


def draw_elevation_anomaly(key, part):
    key = jax.random.fold_in(key, 23)
    rough = jnp.clip(jax.random.normal(key, (POLEWARD_CELLS, EASTWARD_CELLS), jnp.float32), -3.0, 3.0)
    return rough.astype(jnp.float32)


def place_ends(drawn, rng, least, largest):
    place = [jax.random.randint(jax.random.fold_in(rng, axis), (), 0, length) for axis, length in enumerate(drawn.shape)]
    main_axis = drawn.shape.index(max(drawn.shape))
    beside = place[:main_axis] + [(place[main_axis] + 1) % drawn.shape[main_axis]] + place[main_axis + 1:]
    return drawn.at[tuple(place)].set(least).at[tuple(beside)].set(largest)


def block_levels(own_key, extent, split, low, top_value):
    level = 1.0
    for dim, parts in split:
        steps = jax.random.uniform(jax.random.fold_in(jax.random.fold_in(own_key, 6), dim), (parts,), jnp.float32, low / len(split), top_value / len(split))
        level = level * jnp.repeat(jnp.exp(steps), extent[dim] // parts).reshape((-1,) + (1,) * (len(extent) - 1 - dim))
    return level


def noise(own_key, extent, scale, bound, shards=(), kind=jnp.bfloat16):
    drawn = scale * jax.random.normal(own_key, extent, jnp.float32)
    if shards:
        drawn = drawn * block_levels(own_key, extent, shards, -0.22, 0.18)
    return jnp.clip(drawn, -bound, bound).astype(kind)


def setup_inputs(seed: int = 0) -> dict:
    key_list = jax.random.split(jax.random.key(seed), 10)
    warmth_deviation = noise(key_list[0], (STRATA_COUNT, POLEWARD_CELLS, EASTWARD_CELLS), 1.0, 6.0, ((1, 8), (2, 32)), jnp.float32)
    saltiness_deviation = noise(key_list[1], (STRATA_COUNT, POLEWARD_CELLS, EASTWARD_CELLS), 1.0, 6.0, ((1, 8), (2, 32)), jnp.float32)
    easterly_speed = noise(key_list[2], (STRATA_COUNT, POLEWARD_CELLS, EASTWARD_CELLS), 1.0, 6.0, ((1, 8), (2, 32)), jnp.float32)
    poleward_speed = noise(key_list[3], (STRATA_COUNT, POLEWARD_CELLS, EASTWARD_CELLS), 1.0, 6.0, ((1, 8), (2, 32)), jnp.float32)
    stratum_spans = jnp.clip(jnp.exp(jax.random.uniform(key_list[4], (STRATA_COUNT,), jnp.float32, math.log(0.5), math.log(2.0))), 0.5, 2.0)
    water_indicator = place_ends((jax.random.randint(key_list[5], (POLEWARD_CELLS, EASTWARD_CELLS), 0, 4) < 3).astype(jnp.int32), jax.random.fold_in(key_list[5], 1), 0, 1)
    opposite_counterpart = draw_opposite_counterpart(jax.random.fold_in(key_list[9], 71), 0)
    elevation_weights = jnp.clip(jnp.exp(math.log(2.0) - 2.3025851 * jax.random.uniform(key_list[7], (POLEWARD_CELLS, EASTWARD_CELLS), jnp.float32) ** block_levels(key_list[7], (POLEWARD_CELLS, EASTWARD_CELLS), ((0, 8), (1, 32)), -0.2, 0.2)), 0.2, 2.0)
    elevation_anomaly = draw_elevation_anomaly(jax.random.fold_in(key_list[9], 71), 0)
    return dict(warmth_deviation=warmth_deviation, saltiness_deviation=saltiness_deviation, easterly_speed=easterly_speed, poleward_speed=poleward_speed, stratum_spans=stratum_spans, water_indicator=water_indicator, opposite_counterpart=opposite_counterpart, elevation_weights=elevation_weights, elevation_anomaly=elevation_anomaly)


LINEAR_HEAT = 1.0
SQUARE_HEAT = 0.3
SALT_COEF = 0.8
CROSS_COEF = 0.2
TIME_STEP = 0.1
MIXING = 0.1


def periodic(field, width):
    return jnp.concatenate([field[..., -width:], field, field[..., :width]], axis=-1)


def northward(field, opposite_counterpart, width, sign):
    rows = field.shape[-2]
    south = jnp.zeros(field.shape[:-2] + (width, field.shape[-1]), jnp.float32)
    folded = [sign * jnp.take(field[..., rows - 1 - offset, :], opposite_counterpart, axis=-1) for offset in range(width)]
    north = jnp.stack(folded, axis=-2)
    return jnp.concatenate([south, field, north], axis=-2)


def density(heat_part, salt_part):
    return -LINEAR_HEAT * heat_part - 0.5 * SQUARE_HEAT * heat_part * heat_part + SALT_COEF * salt_part - CROSS_COEF * heat_part * salt_part


def pressure(heat_part, salt_part, stratum_spans):
    layers = density(heat_part, salt_part) * stratum_spans[:, None, None]
    return jnp.cumsum(layers, axis=0) - 0.5 * layers


def reference(warmth_deviation, saltiness_deviation, easterly_speed, poleward_speed, stratum_spans, water_indicator, opposite_counterpart, elevation_weights, elevation_anomaly):
    wetness = water_indicator.astype(jnp.float32)
    advected_quantities = jnp.stack([warmth_deviation, saltiness_deviation])
    along = periodic(advected_quantities, 2)
    across = northward(advected_quantities, opposite_counterpart, 2, 1.0)
    east_one = along[..., 3:-1]
    west_one = along[..., 1:-3]
    east_two = along[..., 4:]
    west_two = along[..., :-4]
    north_one = across[..., 3:-1, :]
    south_one = across[..., 1:-3, :]
    north_two = across[..., 4:, :]
    south_two = across[..., :-4, :]
    grad_east = (8.0 * (east_one - west_one) - (east_two - west_two)) / 12.0
    grad_north = (8.0 * (north_one - south_one) - (north_two - south_two)) / 12.0
    laplace = east_one + west_one + north_one + south_one - 4.0 * advected_quantities
    tendency = -TIME_STEP * (easterly_speed * grad_east + poleward_speed * grad_north) + MIXING * laplace
    updated = advected_quantities + wetness * tendency
    press_east = pressure(along[0][..., 1:-1], along[1][..., 1:-1], stratum_spans)
    press_north = pressure(across[0][:, 1:-1, :], across[1][:, 1:-1, :], stratum_spans)
    slope_east = 0.5 * (press_east[..., 2:] - press_east[..., :-2])
    slope_north = 0.5 * (press_north[:, 2:, :] - press_north[:, :-2, :])
    new_zonal = wetness * (easterly_speed - TIME_STEP * slope_east)
    new_meridional = wetness * (poleward_speed - TIME_STEP * slope_north)
    east_flow = jnp.sum(stratum_spans[:, None, None] * new_zonal, axis=0)
    north_flow = jnp.sum(stratum_spans[:, None, None] * new_meridional, axis=0)
    transports = jnp.stack([east_flow, north_flow])
    flow_along = periodic(transports, 1)
    flow_across = northward(transports, opposite_counterpart, 1, -1.0)
    divergence = 0.5 * (flow_along[0][:, 2:] - flow_along[0][:, :-2] + flow_across[1][2:, :] - flow_across[1][:-2, :])
    right_side = wetness * (elevation_weights * elevation_anomaly - divergence)
    diagonal = 4.0 + elevation_weights

    def operate(field):
        cycle_ext = periodic(field, 1)
        row_ext = northward(field, opposite_counterpart, 1, 1.0)
        neighbours = cycle_ext[:, 2:] + cycle_ext[:, :-2] + row_ext[2:, :] + row_ext[:-2, :]
        return diagonal * field - wetness * neighbours

    solution = jnp.zeros_like(right_side)
    residual = right_side
    precond = residual / diagonal
    direction = precond
    norm_now = jnp.sum(residual * precond)
    for step in range(ITERS):
        image = operate(direction)
        alpha = norm_now / jnp.sum(direction * image)
        solution = solution + alpha * direction
        residual = residual - alpha * image
        precond = residual / diagonal
        norm_next = jnp.sum(residual * precond)
        direction = precond + (norm_next / norm_now) * direction
        norm_now = norm_next
    return updated[0], updated[1], new_zonal, new_meridional, solution
```

```python
import functools

import jax
import jax.numpy as jnp
from jax import lax
from jax.experimental import pallas as pl
from jax.experimental.pallas import tpu as pltpu
from jax.sharding import PartitionSpec as P

MESH = pl.DeviceIdType.MESH
LEVELS = 10
ROWS = 64
LANES = 128
EDGE = 8
NLON = 32
NLAT = 8
NX = 4
NZ = 8
SPAN2 = 10
SPAN3 = 4
FOLD2 = 20
FOLD3 = 4 * LEVELS


def density(t, s):
    return -t - 0.15 * t * t + 0.8 * s - 0.2 * t * s


def lane_iota(rows):
    return lax.broadcasted_iota(jnp.int32, (rows, LANES), 1)


def kernel(
    t_hbm, s_hbm, u_hbm, v_hbm, w_hbm, e_hbm, a_hbm, spans, opp,
    nt, ns, nu, nv, surf,
    ts, uv, wbuf, ebuf, x, pack, wide, pack3, wide3, own2, fold2, own3, fold3, press, vec, sums1, sums2,
    in_sem, side_send, side_recv, group_send, group_recv,
):
    lon = lax.axis_index("lon")
    lat = lax.axis_index("lat")
    lon_x = lax.rem(lon, NX)
    east = lax.rem(lon + 1, NLON)
    west = lax.rem(lon + NLON - 1, NLON)
    is_top = lat == NLAT - 1
    is_low = lat == 0
    not_top = lat < NLAT - 1
    not_low = lat > 0

    loads = [
        pltpu.make_async_copy(w_hbm, wbuf, in_sem.at[0]),
        pltpu.make_async_copy(e_hbm, ebuf.at[0], in_sem.at[1]),
        pltpu.make_async_copy(a_hbm, ebuf.at[1], in_sem.at[2]),
        pltpu.make_async_copy(t_hbm, ts.at[0, :, EDGE:EDGE + ROWS, :], in_sem.at[3]),
        pltpu.make_async_copy(s_hbm, ts.at[1, :, EDGE:EDGE + ROWS, :], in_sem.at[4]),
        pltpu.make_async_copy(u_hbm, uv.at[0], in_sem.at[5]),
        pltpu.make_async_copy(v_hbm, uv.at[1], in_sem.at[6]),
    ]
    for load in loads:
        load.start()

    barrier = pltpu.get_barrier_semaphore()

    def greet(dev):
        pl.semaphore_signal(barrier, inc=1, device_id=dev, device_id_type=MESH)

    near = []
    for dx in range(NX):
        for dy in range(NLAT):
            if dx or dy:
                near.append((lon - lon_x + lax.rem(lon_x + dx, NX), lax.rem(lat + dy, NLAT)))
    far = [(lax.rem(lon + NX * k, NLON), lat) for k in range(1, NZ)]
    ring = [(lax.rem(lon + k, NLON), lat) for k in range(1, NLON)]
    for dev in near + far + [(east, lat), (west, lat)]:
        greet(dev)

    @pl.when(not_top)
    def _():
        greet((east, lat + 1))
        greet((west, lat + 1))

    @pl.when(not_low)
    def _():
        greet((east, lat - 1))
        greet((west, lat - 1))

    @pl.when(is_top)
    def _():
        for dev in ring:
            greet(dev)

    for load in loads[:3]:
        load.wait()
    own = slice(EDGE, EDGE + ROWS)
    weights = ebuf[0]
    diagonal = 4.0 + weights
    wetness = wbuf[...].astype(jnp.float32)
    scale = wetness / diagonal
    x[3, 0, own, :] = scale
    x[4, 0, own, :] = scale * (weights * ebuf[1])

    for load in loads[3:]:
        load.wait()
    zero = jnp.zeros((ROWS, LANES), jnp.float32)
    below, press_sum, east_sum, north_sum = zero, zero, zero, zero
    for k in range(LEVELS):
        span = spans[k]
        layer = density(ts[0, k, own, :], ts[1, k, own, :]) * span
        press_sum = press_sum + span * (below + 0.5 * layer)
        below = below + layer
        east_sum = east_sum + span * uv[0, k]
        north_sum = north_sum + span * uv[1, k]
    x[0, 0, own, :] = press_sum
    x[1, 0, own, :] = east_sum
    x[2, 0, own, :] = north_sum

    lanes = lane_iota(ROWS)
    packed = zero
    for f in range(5):
        moved = pltpu.roll(x[f, 0, own, :], SPAN2 * f + 5, 1)
        packed = jnp.where((lanes >= SPAN2 * f) & (lanes < SPAN2 * (f + 1)), moved, packed)
    pack[...] = packed
    packed = zero
    for q in range(2 * LEVELS):
        moved = pltpu.roll(ts[q // LEVELS, q % LEVELS, own, :], SPAN3 * q + 2, 1)
        packed = jnp.where((lanes >= SPAN3 * q) & (lanes < SPAN3 * (q + 1)), moved, packed)
    pack3[...] = packed

    @pl.when(is_top)
    def _():
        row = 0
        for f, count in ((0, 5), (1, 3), (2, 4), (3, 4), (4, 4)):
            for r in range(count):
                last = EDGE + ROWS - 1 - r
                line = x[f, 0, last:last + 1, :]
                own2[row:row + 1, :] = -line if f in (1, 2) else line
                row += 1
        fold2[lon, 0:FOLD2, :] = own2[0:FOLD2, :]
        for q in range(2 * LEVELS):
            own3[2 * q:2 * q + 2, :] = ts[q // LEVELS, q % LEVELS, EDGE + ROWS - 2:EDGE + ROWS, :]
        fold3[lon] = own3[...]
        for f in range(5):
            x[f, 0, EDGE + ROWS:, :] = jnp.zeros((EDGE, LANES), jnp.float32)

    @pl.when(is_low)
    def _():
        for f in range(5):
            x[f, 0, 0:EDGE, :] = jnp.zeros((EDGE, LANES), jnp.float32)
        for q in range(2 * LEVELS):
            ts[q // LEVELS, q % LEVELS, 0:EDGE, :] = jnp.zeros((EDGE, LANES), jnp.float32)

    base = 31 + 7 + 2

    @pl.when(is_top)
    def _():
        pl.semaphore_wait(barrier, base + 2 + NLON - 1)

    @pl.when(is_low)
    def _():
        pl.semaphore_wait(barrier, base + 2)

    @pl.when(not_top & not_low)
    def _():
        pl.semaphore_wait(barrier, base + 4)

    def copy(src, dst, sem, dev):
        return pltpu.make_async_remote_copy(
            src_ref=src, dst_ref=dst, send_sem=side_send.at[sem], recv_sem=side_recv.at[sem],
            device_id=dev, device_id_type=MESH,
        )

    top_rows = slice(EDGE + ROWS, EDGE + ROWS + EDGE)
    to_east = copy(pack, wide.at[0, own, :], 0, (east, lat))
    to_west = copy(pack, wide.at[1, own, :], 1, (west, lat))
    to_north = copy(x.at[:, 0, ROWS:EDGE + ROWS, :], x.at[:, 0, 0:EDGE, :], 2, (lon, lat + 1))
    to_ne = copy(pack.at[ROWS - EDGE:ROWS, :], wide.at[0, 0:EDGE, :], 3, (east, lat + 1))
    to_nw = copy(pack.at[ROWS - EDGE:ROWS, :], wide.at[1, 0:EDGE, :], 4, (west, lat + 1))
    to_south = copy(x.at[:, 0, EDGE:2 * EDGE, :], x.at[:, 0, top_rows, :], 5, (lon, lat - 1))
    to_se = copy(pack.at[0:EDGE, :], wide.at[0, top_rows, :], 6, (east, lat - 1))
    to_sw = copy(pack.at[0:EDGE, :], wide.at[1, top_rows, :], 7, (west, lat - 1))
    to_east3 = copy(pack3, wide3.at[0], 8, (east, lat))
    to_west3 = copy(pack3, wide3.at[1], 9, (west, lat))
    to_north3 = copy(
        ts.at[:, :, EDGE + ROWS - 2:EDGE + ROWS, :], ts.at[:, :, EDGE - 2:EDGE, :], 10, (lon, lat + 1)
    )
    to_south3 = copy(
        ts.at[:, :, EDGE:EDGE + 2, :], ts.at[:, :, EDGE + ROWS:EDGE + ROWS + 2, :], 11, (lon, lat - 1)
    )
    north_sends = (to_north, to_ne, to_nw)
    south_sends = (to_south, to_se, to_sw)

    def spread(src, dst, sem, devs):
        for dev in devs:
            pltpu.make_async_remote_copy(
                src_ref=src, dst_ref=dst, send_sem=group_send.at[sem], recv_sem=group_recv.at[sem],
                device_id=dev, device_id_type=MESH,
            ).start()

    def settle(ref, sem):
        pltpu.make_async_copy(ref, ref, sem).wait()

    @pl.when(is_top)
    def _():
        spread(own2.at[0:FOLD2, :], fold2.at[lon, 0:FOLD2, :], 0, ring)

    to_east.start()
    to_west.start()

    @pl.when(not_top)
    def _():
        for send in north_sends:
            send.start()

    @pl.when(not_low)
    def _():
        for send in south_sends:
            send.start()

    to_east3.start()
    to_west3.start()

    @pl.when(not_top)
    def _():
        to_north3.start()

    @pl.when(not_low)
    def _():
        to_south3.start()

    @pl.when(is_top)
    def _():
        spread(own3, fold3.at[lon], 1, ring)

    to_east.wait_recv()
    to_west.wait_recv()

    @pl.when(not_low)
    def _():
        for send in north_sends:
            send.wait_recv()

    @pl.when(not_top)
    def _():
        for send in south_sends:
            send.wait_recv()

    lanes_w = lane_iota(EDGE + ROWS + EDGE)
    eastern = lax.rem(lanes_w, SPAN2) < 5
    merged = jnp.where(eastern, wide[0], wide[1])
    for f in range(5):
        x[f, 1] = pltpu.roll(merged, LANES - (SPAN2 * f + 5), 1)

    @pl.when(is_low)
    def _():
        for f in range(5):
            x[f, 1, 0:EDGE, :] = jnp.zeros((EDGE, LANES), jnp.float32)

    lanes_e = lane_iota(EDGE)
    first = opp[0]
    slot = lax.div(first, LANES)
    offset = first - slot * LANES
    slot_p = lax.rem(slot + 1, NLON)
    slot_m = lax.rem(slot + NLON - 1, NLON)
    slot_mm = lax.rem(slot + NLON - 2, NLON)
    index = (offset - lanes_e) & (LANES - 1)

    def turn(tile):
        return jnp.take_along_axis(tile, index, axis=1)

    @pl.when(is_top)
    def _():
        settle(fold2.at[0:NLON - 1, 0:FOLD2, :], group_recv.at[0])
        kept = lanes_e <= offset
        near_half = index < LANES // 2
        mine, aside = [], []
        for tile in range(3):
            part = slice(EDGE * tile, EDGE * (tile + 1))
            b_p, b_0, b_m, b_mm = (fold2[s, part, :] for s in (slot_p, slot, slot_m, slot_mm))
            mine.append(turn(jnp.where(kept, b_0, b_m)))
            right = jnp.where(kept, b_m, b_mm)
            left = jnp.where(kept, b_p, b_0)
            aside.append(turn(jnp.where(near_half, right, left)))
        for half, tiles in ((0, mine), (1, aside)):
            x[0, half, EDGE + ROWS:EDGE + ROWS + 5, :] = tiles[0][0:5]
            x[1, half, EDGE + ROWS:EDGE + ROWS + 3, :] = tiles[0][5:8]
            x[2, half, EDGE + ROWS:EDGE + ROWS + 4, :] = tiles[1][0:4]
            x[3, half, EDGE + ROWS:EDGE + ROWS + 4, :] = tiles[1][4:8]
            x[4, half, EDGE + ROWS:EDGE + ROWS + 4, :] = tiles[2][0:4]

    full = EDGE + ROWS + EDGE
    first_lane = lanes_w == 0
    last_lane = lanes_w == LANES - 1

    def plus_east(a, b):
        return (
            pltpu.roll(jnp.where(first_lane, b, a), LANES - 1, 1),
            pltpu.roll(jnp.where(first_lane, a, b), LANES - 1, 1),
        )

    def plus_west(a, b):
        return (
            pltpu.roll(jnp.where(last_lane, b, a), 1, 1),
            pltpu.roll(jnp.where(last_lane, a, b), 1, 1),
        )

    def north_of(a):
        return pltpu.roll(a, full - 1, 0)

    def south_of(a):
        return pltpu.roll(a, 1, 0)

    scale2 = (x[3, 0], x[3, 1])
    wet2 = (scale2[0] > 0.0, scale2[1] > 0.0)
    q2 = (x[0, 0], x[0, 1])
    q_e = plus_east(*q2)
    q_w = plus_west(*q2)
    flow_e, flow_n = [], []
    for h in range(2):
        flow_e.append(jnp.where(wet2[h], x[1, h] - 0.05 * (q_e[h] - q_w[h]), 0.0))
        flow_n.append(jnp.where(wet2[h], x[2, h] - 0.05 * (north_of(q2[h]) - south_of(q2[h])), 0.0))
    f_e = plus_east(*flow_e)
    f_w = plus_west(*flow_e)
    basis = []
    v = tuple(
        x[4, h] - scale2[h] * (0.5 * (f_e[h] - f_w[h] + north_of(flow_n[h]) - south_of(flow_n[h])))
        for h in range(2)
    )
    basis.append(v[0][EDGE:EDGE + ROWS])
    for _ in range(3):
        v_e = plus_east(*v)
        v_w = plus_west(*v)
        v = tuple(scale2[h] * (v_e[h] + v_w[h] + north_of(v[h]) + south_of(v[h])) for h in range(2))
        basis.append(v[0][EDGE:EDGE + ROWS])

    for i in range(3):
        press[i, own, :] = basis[i]
    sub = lax.broadcasted_iota(jnp.int32, (EDGE, LANES), 0)
    table = jnp.zeros((EDGE, LANES), jnp.float32)
    for j, (l, r) in enumerate(((0, 0), (0, 1), (1, 1), (1, 2), (2, 2), (2, 3))):
        product = (diagonal * basis[l]) * basis[r]
        line = jnp.sum(product.reshape(ROWS // EDGE, EDGE, LANES), axis=0)
        line = jnp.sum(line, axis=0, keepdims=True)
        table = jnp.where(sub == j, line, table)
    table = jnp.sum(table, axis=1, keepdims=True)
    message = jnp.sum(jnp.where(sub == lanes_e, table, 0.0), axis=0, keepdims=True)
    vec[0:1, :] = message
    mine1 = lon_x * NLAT + lat
    sums1[pl.ds(mine1, 1), :] = message
    spread(vec.at[0:1, :], sums1.at[pl.ds(mine1, 1), :], 2, near)

    to_east3.wait_recv()
    to_west3.wait_recv()

    @pl.when(not_low)
    def _():
        to_north3.wait_recv()

    @pl.when(not_top)
    def _():
        to_south3.wait_recv()

    @pl.when(is_top)
    def _():
        settle(fold3.at[0:NLON - 1], group_recv.at[1])
        kept = lanes_e <= offset
        for tile in range(FOLD3 // EDGE):
            part = slice(EDGE * tile, EDGE * (tile + 1))
            turned = turn(jnp.where(kept, fold3[slot, part, :], fold3[slot_m, part, :]))
            for i in range(EDGE):
                q, r = (EDGE * tile + i) // 2, (EDGE * tile + i) % 2
                ts[q // LEVELS, q % LEVELS, EDGE + ROWS + 1 - r:EDGE + ROWS + 2 - r, :] = turned[i:i + 1]

    merged3 = jnp.where((lanes & 2) == 0, wide3[0], wide3[1])
    below = jnp.zeros((full, LANES), jnp.float32)
    below_side = zero
    tracer_out = (nt, ns)
    for k in range(LEVELS):
        span = spans[k]
        u = uv[0, k]
        w = uv[1, k]
        sides = []
        for f in range(2):
            side = pltpu.roll(merged3, LANES - (SPAN3 * (f * LEVELS + k) + 2), 1)
            sides.append(side)
            c = ts[f, k, EDGE:EDGE + ROWS, :]
            e1 = pltpu.roll(jnp.where(lanes == 0, side, c), LANES - 1, 1)
            e2 = pltpu.roll(jnp.where(lanes < 2, side, c), LANES - 2, 1)
            w1 = pltpu.roll(jnp.where(lanes == LANES - 1, side, c), 1, 1)
            w2 = pltpu.roll(jnp.where(lanes >= LANES - 2, side, c), 2, 1)
            n1 = ts[f, k, EDGE + 1:EDGE + ROWS + 1, :]
            n2 = ts[f, k, EDGE + 2:EDGE + ROWS + 2, :]
            s1 = ts[f, k, EDGE - 1:EDGE + ROWS - 1, :]
            s2 = ts[f, k, EDGE - 2:EDGE + ROWS - 2, :]
            grad_e = (8.0 * (e1 - w1) - (e2 - w2)) * (1.0 / 12.0)
            grad_n = (8.0 * (n1 - s1) - (n2 - s2)) * (1.0 / 12.0)
            laplace = e1 + w1 + n1 + s1 - 4.0 * c
            tracer_out[f][k] = c + wetness * (-0.1 * (u * grad_e + w * grad_n) + 0.1 * laplace)
        layer = density(ts[0, k], ts[1, k]) * span
        level = below + 0.5 * layer
        below = below + layer
        layer_side = density(sides[0], sides[1]) * span
        level_side = below_side + 0.5 * layer_side
        below_side = below_side + layer_side
        centre = level[EDGE:EDGE + ROWS]
        p_e = pltpu.roll(jnp.where(lanes == 0, level_side, centre), LANES - 1, 1)
        p_w = pltpu.roll(jnp.where(lanes == LANES - 1, level_side, centre), 1, 1)
        p_n = north_of(level)[EDGE:EDGE + ROWS]
        p_s = south_of(level)[EDGE:EDGE + ROWS]
        nu[k] = wetness * (u - 0.05 * (p_e - p_w))
        nv[k] = wetness * (w - 0.05 * (p_n - p_s))

    settle(sums1.at[0:NX * NLAT - 1, :], group_recv.at[2])
    total = jnp.sum(sums1[...], axis=0, keepdims=True)
    mine2 = lax.div(lon, NX)
    vec[EDGE:EDGE + 1, :] = total
    sums2[pl.ds(mine2, 1), :] = total
    spread(vec.at[EDGE:EDGE + 1, :], sums2.at[pl.ds(mine2, 1), :], 3, far)
    settle(sums2.at[0:NZ - 1, :], group_recv.at[3])
    total = jnp.sum(sums2[...], axis=0, keepdims=True)
    mu = [total[:, j:j + 1] for j in range(6)]

    def gram(a, b, shift):
        out = None
        for i, ai in enumerate(a):
            for j, bj in enumerate(b):
                term = ai * bj * mu[i + j + shift]
                out = term if out is None else out + term
        return out

    one = jnp.ones((1, 1), jnp.float32)
    res, dire, sol = [one], [one], [0.0 * one] * 3
    rz = mu[0]
    for step in range(3):
        alpha = rz / (gram(dire, dire, 0) - gram(dire, dire, 1))
        sol = [sol[i] + alpha * dire[i] if i < len(dire) else sol[i] for i in range(3)]
        if step < 2:
            image = [
                (dire[i] if i < len(dire) else 0.0) - (dire[i - 1] if i else 0.0) for i in range(len(dire) + 1)
            ]
            res = [(res[i] if i < len(res) else 0.0) - alpha * image[i] for i in range(len(image))]
            new = gram(res, res, 0)
            beta = new / rz
            dire = [res[i] + (beta * dire[i] if i < len(dire) else 0.0) for i in range(len(res))]
            rz = new
    surf[...] = sol[0] * press[0, own, :] + sol[1] * press[1, own, :] + sol[2] * press[2, own, :]

    to_east.wait_send()
    to_west.wait_send()
    to_east3.wait_send()
    to_west3.wait_send()

    @pl.when(not_top)
    def _():
        for send in north_sends:
            send.wait_send()
        to_north3.wait_send()

    @pl.when(not_low)
    def _():
        for send in south_sends:
            send.wait_send()
        to_south3.wait_send()

    @pl.when(is_top)
    def _():
        settle(fold2.at[0:NLON - 1, 0:FOLD2, :], group_send.at[0])
        settle(fold3.at[0:NLON - 1], group_send.at[1])

    settle(sums1.at[0:NX * NLAT - 1, :], group_send.at[2])
    settle(sums2.at[0:NZ - 1, :], group_send.at[3])


def store(*refs):
    ins, outs, sem = refs[:5], refs[5:10], refs[10]
    copies = [pltpu.make_async_copy(i, o, sem.at[n]) for n, (i, o) in enumerate(zip(ins, outs))]
    for c in copies:
        c.start()
    for c in copies:
        c.wait()


def body(t, s, u, v, spans, water, opp, weights, anomaly):
    hbm = pl.BlockSpec(memory_space=pltpu.HBM)
    smem = pl.BlockSpec(memory_space=pltpu.SMEM)
    vmem = pl.BlockSpec(memory_space=pltpu.VMEM)
    f32 = jnp.float32
    shapes = [jax.ShapeDtypeStruct((LEVELS, ROWS, LANES), f32)] * 4 + [jax.ShapeDtypeStruct((ROWS, LANES), f32)]
    full = ROWS + 2 * EDGE
    results = pl.pallas_call(
        kernel,
        out_shape=shapes,
        in_specs=[hbm] * 7 + [smem] * 2,
        out_specs=[vmem] * 5,
        scratch_shapes=[
            pltpu.VMEM((2, LEVELS, full, LANES), f32),
            pltpu.VMEM((2, LEVELS, ROWS, LANES), f32),
            pltpu.VMEM((ROWS, LANES), jnp.int32),
            pltpu.VMEM((2, ROWS, LANES), f32),
            pltpu.VMEM((5, 2, full, LANES), f32),
            pltpu.VMEM((ROWS, LANES), f32),
            pltpu.VMEM((2, full, LANES), f32),
            pltpu.VMEM((ROWS, LANES), f32),
            pltpu.VMEM((2, ROWS, LANES), f32),
            pltpu.VMEM((24, LANES), f32),
            pltpu.VMEM((NLON, 24, LANES), f32),
            pltpu.VMEM((FOLD3, LANES), f32),
            pltpu.VMEM((NLON, FOLD3, LANES), f32),
            pltpu.VMEM((3, full, LANES), f32),
            pltpu.VMEM((2 * EDGE, LANES), f32),
            pltpu.VMEM((NX * NLAT, LANES), f32),
            pltpu.VMEM((NZ, LANES), f32),
            pltpu.SemaphoreType.DMA((7,)),
            pltpu.SemaphoreType.DMA((12,)),
            pltpu.SemaphoreType.DMA((12,)),
            pltpu.SemaphoreType.DMA((4,)),
            pltpu.SemaphoreType.DMA((4,)),
        ],
        compiler_params=pltpu.CompilerParams(
            collective_id=0, has_side_effects=True, vmem_limit_bytes=40 * 1024 * 1024
        ),
    )(t, s, u, v, water, weights, anomaly, spans, opp)
    anyspec = pl.BlockSpec(memory_space=pl.ANY)
    return pl.pallas_call(
        store,
        out_shape=shapes,
        in_specs=[anyspec] * 5,
        out_specs=[anyspec] * 5,
        scratch_shapes=[pltpu.SemaphoreType.DMA((5,))],
    )(*results)


def solution(mesh):
    deep = P(None, "lat", "lon")
    flat = P("lat", "lon")
    return jax.shard_map(
        body,
        mesh=mesh,
        in_specs=(deep, deep, deep, deep, P(), flat, P("lon"), flat, flat),
        out_specs=(deep, deep, deep, deep, flat),
        check_vma=False,
    )
```

```python
import functools

import jax
import jax.numpy as jnp
from jax import lax
from jax.experimental import pallas as pl
from jax.experimental.pallas import tpu as pltpu
from jax.sharding import PartitionSpec as P

MESH = pl.DeviceIdType.MESH
LEVELS = 10
ROWS = 64
LANES = 128
EDGE = 8
NLON = 32
NLAT = 8
NX = 4
NZ = 8
SPAN2 = 10
SPAN3 = 4
FOLD2 = 20
FOLD3 = 4 * LEVELS


def density(t, s):
    return -t - 0.15 * t * t + 0.8 * s - 0.2 * t * s


def lane_iota(rows):
    return lax.broadcasted_iota(jnp.int32, (rows, LANES), 1)


def kernel(
    t_hbm, s_hbm, u_hbm, v_hbm, w_hbm, e_hbm, a_hbm, spans, opp,
    nt, ns, nu, nv, surf,
    ts, uv, wbuf, ebuf, x, pack, wide, pack3, wide3, own2, fold2, own3, fold3, press, vec, sums1, sums2,
    in_sem, side_send, side_recv, group_send, group_recv,
):
    lon = lax.axis_index("lon")
    lat = lax.axis_index("lat")
    lon_x = lax.rem(lon, NX)
    east = lax.rem(lon + 1, NLON)
    west = lax.rem(lon + NLON - 1, NLON)
    is_top = lat == NLAT - 1
    is_low = lat == 0
    not_top = lat < NLAT - 1
    not_low = lat > 0

    loads = [
        pltpu.make_async_copy(w_hbm, wbuf, in_sem.at[0]),
        pltpu.make_async_copy(e_hbm, ebuf.at[0], in_sem.at[1]),
        pltpu.make_async_copy(a_hbm, ebuf.at[1], in_sem.at[2]),
        pltpu.make_async_copy(t_hbm, ts.at[0, :, EDGE:EDGE + ROWS, :], in_sem.at[3]),
        pltpu.make_async_copy(s_hbm, ts.at[1, :, EDGE:EDGE + ROWS, :], in_sem.at[4]),
        pltpu.make_async_copy(u_hbm, uv.at[0], in_sem.at[5]),
        pltpu.make_async_copy(v_hbm, uv.at[1], in_sem.at[6]),
    ]
    for load in loads:
        load.start()

    barrier = pltpu.get_barrier_semaphore()

    def greet(dev):
        pl.semaphore_signal(barrier, inc=1, device_id=dev, device_id_type=MESH)

    near = []
    for dx in range(NX):
        for dy in range(NLAT):
            if dx or dy:
                near.append((lon - lon_x + lax.rem(lon_x + dx, NX), lax.rem(lat + dy, NLAT)))
    far = [(lax.rem(lon + NX * k, NLON), lat) for k in range(1, NZ)]
    ring = [(lax.rem(lon + k, NLON), lat) for k in range(1, NLON)]
    for dev in near + far + [(east, lat), (west, lat)]:
        greet(dev)

    @pl.when(not_top)
    def _():
        greet((east, lat + 1))
        greet((west, lat + 1))

    @pl.when(not_low)
    def _():
        greet((east, lat - 1))
        greet((west, lat - 1))

    @pl.when(is_top)
    def _():
        for dev in ring:
            greet(dev)

    for load in loads[:3]:
        load.wait()
    own = slice(EDGE, EDGE + ROWS)
    weights = ebuf[0]
    diagonal = 4.0 + weights
    wetness = wbuf[...].astype(jnp.float32)
    scale = wetness / diagonal
    x[3, 0, own, :] = scale
    x[4, 0, own, :] = scale * (weights * ebuf[1])

    for load in loads[3:]:
        load.wait()
    zero = jnp.zeros((ROWS, LANES), jnp.float32)
    below, press_sum, east_sum, north_sum = zero, zero, zero, zero
    for k in range(LEVELS):
        span = spans[k]
        layer = density(ts[0, k, own, :], ts[1, k, own, :]) * span
        press_sum = press_sum + span * (below + 0.5 * layer)
        below = below + layer
        east_sum = east_sum + span * uv[0, k]
        north_sum = north_sum + span * uv[1, k]
    x[0, 0, own, :] = press_sum
    x[1, 0, own, :] = east_sum
    x[2, 0, own, :] = north_sum

    lanes = lane_iota(ROWS)
    packed = zero
    for f in range(5):
        moved = pltpu.roll(x[f, 0, own, :], SPAN2 * f + 5, 1)
        packed = jnp.where((lanes >= SPAN2 * f) & (lanes < SPAN2 * (f + 1)), moved, packed)
    pack[...] = packed
    packed = zero
    for q in range(2 * LEVELS):
        moved = pltpu.roll(ts[q // LEVELS, q % LEVELS, own, :], SPAN3 * q + 2, 1)
        packed = jnp.where((lanes >= SPAN3 * q) & (lanes < SPAN3 * (q + 1)), moved, packed)
    pack3[...] = packed

    @pl.when(is_top)
    def _():
        row = 0
        for f, count in ((0, 5), (1, 3), (2, 4), (3, 4), (4, 4)):
            for r in range(count):
                last = EDGE + ROWS - 1 - r
                line = x[f, 0, last:last + 1, :]
                own2[row:row + 1, :] = -line if f in (1, 2) else line
                row += 1
        fold2[lon, 0:FOLD2, :] = own2[0:FOLD2, :]
        for q in range(2 * LEVELS):
            own3[2 * q:2 * q + 2, :] = ts[q // LEVELS, q % LEVELS, EDGE + ROWS - 2:EDGE + ROWS, :]
        fold3[lon] = own3[...]
        for f in range(5):
            x[f, 0, EDGE + ROWS:, :] = jnp.zeros((EDGE, LANES), jnp.float32)

    @pl.when(is_low)
    def _():
        for f in range(5):
            x[f, 0, 0:EDGE, :] = jnp.zeros((EDGE, LANES), jnp.float32)
        for q in range(2 * LEVELS):
            ts[q // LEVELS, q % LEVELS, 0:EDGE, :] = jnp.zeros((EDGE, LANES), jnp.float32)

    base = 31 + 7 + 2

    @pl.when(is_top)
    def _():
        pl.semaphore_wait(barrier, base + 2 + NLON - 1)

    @pl.when(is_low)
    def _():
        pl.semaphore_wait(barrier, base + 2)

    @pl.when(not_top & not_low)
    def _():
        pl.semaphore_wait(barrier, base + 4)

    def copy(src, dst, sem, dev):
        return pltpu.make_async_remote_copy(
            src_ref=src, dst_ref=dst, send_sem=side_send.at[sem], recv_sem=side_recv.at[sem],
            device_id=dev, device_id_type=MESH,
        )

    top_rows = slice(EDGE + ROWS, EDGE + ROWS + EDGE)
    to_east = copy(pack, wide.at[0, own, :], 0, (east, lat))
    to_west = copy(pack, wide.at[1, own, :], 1, (west, lat))
    to_north = copy(x.at[:, 0, ROWS:EDGE + ROWS, :], x.at[:, 0, 0:EDGE, :], 2, (lon, lat + 1))
    to_ne = copy(pack.at[ROWS - EDGE:ROWS, :], wide.at[0, 0:EDGE, :], 3, (east, lat + 1))
    to_nw = copy(pack.at[ROWS - EDGE:ROWS, :], wide.at[1, 0:EDGE, :], 4, (west, lat + 1))
    to_south = copy(x.at[:, 0, EDGE:2 * EDGE, :], x.at[:, 0, top_rows, :], 5, (lon, lat - 1))
    to_se = copy(pack.at[0:EDGE, :], wide.at[0, top_rows, :], 6, (east, lat - 1))
    to_sw = copy(pack.at[0:EDGE, :], wide.at[1, top_rows, :], 7, (west, lat - 1))
    to_east3 = copy(pack3, wide3.at[0], 8, (east, lat))
    to_west3 = copy(pack3, wide3.at[1], 9, (west, lat))
    to_north3 = copy(
        ts.at[:, :, EDGE + ROWS - 2:EDGE + ROWS, :], ts.at[:, :, EDGE - 2:EDGE, :], 10, (lon, lat + 1)
    )
    to_south3 = copy(
        ts.at[:, :, EDGE:EDGE + 2, :], ts.at[:, :, EDGE + ROWS:EDGE + ROWS + 2, :], 11, (lon, lat - 1)
    )
    north_sends = (to_north, to_ne, to_nw)
    south_sends = (to_south, to_se, to_sw)

    def spread(src, dst, sem, devs):
        for dev in devs:
            pltpu.make_async_remote_copy(
                src_ref=src, dst_ref=dst, send_sem=group_send.at[sem], recv_sem=group_recv.at[sem],
                device_id=dev, device_id_type=MESH,
            ).start()

    def settle(ref, sem):
        pltpu.make_async_copy(ref, ref, sem).wait()

    @pl.when(is_top)
    def _():
        spread(own2.at[0:FOLD2, :], fold2.at[lon, 0:FOLD2, :], 0, ring)

    to_east.start()
    to_west.start()

    @pl.when(not_top)
    def _():
        for send in north_sends:
            send.start()

    @pl.when(not_low)
    def _():
        for send in south_sends:
            send.start()

    to_east3.start()
    to_west3.start()

    @pl.when(not_top)
    def _():
        to_north3.start()

    @pl.when(not_low)
    def _():
        to_south3.start()

    @pl.when(is_top)
    def _():
        spread(own3, fold3.at[lon], 1, ring)

    to_east.wait_recv()
    to_west.wait_recv()

    @pl.when(not_low)
    def _():
        for send in north_sends:
            send.wait_recv()

    @pl.when(not_top)
    def _():
        for send in south_sends:
            send.wait_recv()

    lanes_w = lane_iota(EDGE + ROWS + EDGE)
    eastern = lax.rem(lanes_w, SPAN2) < 5
    merged = jnp.where(eastern, wide[0], wide[1])
    for f in range(5):
        x[f, 1] = pltpu.roll(merged, LANES - (SPAN2 * f + 5), 1)

    @pl.when(is_low)
    def _():
        for f in range(5):
            x[f, 1, 0:EDGE, :] = jnp.zeros((EDGE, LANES), jnp.float32)

    lanes_e = lane_iota(EDGE)
    first = opp[0]
    slot = lax.div(first, LANES)
    offset = first - slot * LANES
    slot_p = lax.rem(slot + 1, NLON)
    slot_m = lax.rem(slot + NLON - 1, NLON)
    slot_mm = lax.rem(slot + NLON - 2, NLON)
    index = (offset - lanes_e) & (LANES - 1)

    def turn(tile):
        return jnp.take_along_axis(tile, index, axis=1)

    @pl.when(is_top)
    def _():
        settle(fold2.at[0:NLON - 1, 0:FOLD2, :], group_recv.at[0])
        kept = lanes_e <= offset
        near_half = index < LANES // 2
        mine, aside = [], []
        for tile in range(3):
            part = slice(EDGE * tile, EDGE * (tile + 1))
            b_p, b_0, b_m, b_mm = (fold2[s, part, :] for s in (slot_p, slot, slot_m, slot_mm))
            mine.append(turn(jnp.where(kept, b_0, b_m)))
            right = jnp.where(kept, b_m, b_mm)
            left = jnp.where(kept, b_p, b_0)
            aside.append(turn(jnp.where(near_half, right, left)))
        for half, tiles in ((0, mine), (1, aside)):
            x[0, half, EDGE + ROWS:EDGE + ROWS + 5, :] = tiles[0][0:5]
            x[1, half, EDGE + ROWS:EDGE + ROWS + 3, :] = tiles[0][5:8]
            x[2, half, EDGE + ROWS:EDGE + ROWS + 4, :] = tiles[1][0:4]
            x[3, half, EDGE + ROWS:EDGE + ROWS + 4, :] = tiles[1][4:8]
            x[4, half, EDGE + ROWS:EDGE + ROWS + 4, :] = tiles[2][0:4]

    full = EDGE + ROWS + EDGE
    first_lane = lanes_w == 0
    last_lane = lanes_w == LANES - 1

    def plus_east(a, b):
        return (
            pltpu.roll(jnp.where(first_lane, b, a), LANES - 1, 1),
            pltpu.roll(jnp.where(first_lane, a, b), LANES - 1, 1),
        )

    def plus_west(a, b):
        return (
            pltpu.roll(jnp.where(last_lane, b, a), 1, 1),
            pltpu.roll(jnp.where(last_lane, a, b), 1, 1),
        )

    def north_of(a):
        return pltpu.roll(a, full - 1, 0)

    def south_of(a):
        return pltpu.roll(a, 1, 0)

    scale2 = (x[3, 0], x[3, 1])
    wet2 = (scale2[0] > 0.0, scale2[1] > 0.0)
    q2 = (x[0, 0], x[0, 1])
    q_e = plus_east(*q2)
    q_w = plus_west(*q2)
    flow_e, flow_n = [], []
    for h in range(2):
        flow_e.append(jnp.where(wet2[h], x[1, h] - 0.05 * (q_e[h] - q_w[h]), 0.0))
        flow_n.append(jnp.where(wet2[h], x[2, h] - 0.05 * (north_of(q2[h]) - south_of(q2[h])), 0.0))
    f_e = plus_east(*flow_e)
    f_w = plus_west(*flow_e)
    basis = []
    v = tuple(
        x[4, h] - scale2[h] * (0.5 * (f_e[h] - f_w[h] + north_of(flow_n[h]) - south_of(flow_n[h])))
        for h in range(2)
    )
    basis.append(v[0][EDGE:EDGE + ROWS])
    for _ in range(3):
        v_e = plus_east(*v)
        v_w = plus_west(*v)
        v = tuple(scale2[h] * (v_e[h] + v_w[h] + north_of(v[h]) + south_of(v[h])) for h in range(2))
        basis.append(v[0][EDGE:EDGE + ROWS])

    for i in range(3):
        press[i, own, :] = basis[i]
    sub = lax.broadcasted_iota(jnp.int32, (EDGE, LANES), 0)
    table = jnp.zeros((EDGE, LANES), jnp.float32)
    for j, (l, r) in enumerate(((0, 0), (0, 1), (1, 1), (1, 2), (2, 2), (2, 3))):
        product = (diagonal * basis[l]) * basis[r]
        line = jnp.sum(product.reshape(ROWS // EDGE, EDGE, LANES), axis=0)
        line = jnp.sum(line, axis=0, keepdims=True)
        table = jnp.where(sub == j, line, table)
    table = jnp.sum(table, axis=1, keepdims=True)
    message = jnp.sum(jnp.where(sub == lanes_e, table, 0.0), axis=0, keepdims=True)
    vec[0:1, :] = message
    mine1 = lon_x * NLAT + lat
    sums1[pl.ds(mine1, 1), :] = message
    spread(vec.at[0:1, :], sums1.at[pl.ds(mine1, 1), :], 2, near)

    to_east3.wait_recv()
    to_west3.wait_recv()

    @pl.when(not_low)
    def _():
        to_north3.wait_recv()

    @pl.when(not_top)
    def _():
        to_south3.wait_recv()

    @pl.when(is_top)
    def _():
        settle(fold3.at[0:NLON - 1], group_recv.at[1])
        kept = lanes_e <= offset
        for tile in range(FOLD3 // EDGE):
            part = slice(EDGE * tile, EDGE * (tile + 1))
            turned = turn(jnp.where(kept, fold3[slot, part, :], fold3[slot_m, part, :]))
            for i in range(EDGE):
                q, r = (EDGE * tile + i) // 2, (EDGE * tile + i) % 2
                ts[q // LEVELS, q % LEVELS, EDGE + ROWS + 1 - r:EDGE + ROWS + 2 - r, :] = turned[i:i + 1]

    merged3 = jnp.where((lanes & 2) == 0, wide3[0], wide3[1])
    below = jnp.zeros((full, LANES), jnp.float32)
    below_side = zero
    tracer_out = (nt, ns)
    for k in range(LEVELS):
        span = spans[k]
        u = uv[0, k]
        w = uv[1, k]
        sides = []
        for f in range(2):
            side = pltpu.roll(merged3, LANES - (SPAN3 * (f * LEVELS + k) + 2), 1)
            sides.append(side)
            c = ts[f, k, EDGE:EDGE + ROWS, :]
            e1 = pltpu.roll(jnp.where(lanes == 0, side, c), LANES - 1, 1)
            e2 = pltpu.roll(jnp.where(lanes < 2, side, c), LANES - 2, 1)
            w1 = pltpu.roll(jnp.where(lanes == LANES - 1, side, c), 1, 1)
            w2 = pltpu.roll(jnp.where(lanes >= LANES - 2, side, c), 2, 1)
            n1 = ts[f, k, EDGE + 1:EDGE + ROWS + 1, :]
            n2 = ts[f, k, EDGE + 2:EDGE + ROWS + 2, :]
            s1 = ts[f, k, EDGE - 1:EDGE + ROWS - 1, :]
            s2 = ts[f, k, EDGE - 2:EDGE + ROWS - 2, :]
            grad_e = (8.0 * (e1 - w1) - (e2 - w2)) * (1.0 / 12.0)
            grad_n = (8.0 * (n1 - s1) - (n2 - s2)) * (1.0 / 12.0)
            laplace = e1 + w1 + n1 + s1 - 4.0 * c
            tracer_out[f][k] = c + wetness * (-0.1 * (u * grad_e + w * grad_n) + 0.1 * laplace)
        layer = density(ts[0, k], ts[1, k]) * span
        level = below + 0.5 * layer
        below = below + layer
        layer_side = density(sides[0], sides[1]) * span
        level_side = below_side + 0.5 * layer_side
        below_side = below_side + layer_side
        centre = level[EDGE:EDGE + ROWS]
        p_e = pltpu.roll(jnp.where(lanes == 0, level_side, centre), LANES - 1, 1)
        p_w = pltpu.roll(jnp.where(lanes == LANES - 1, level_side, centre), 1, 1)
        p_n = north_of(level)[EDGE:EDGE + ROWS]
        p_s = south_of(level)[EDGE:EDGE + ROWS]
        nu[k] = wetness * (u - 0.05 * (p_e - p_w))
        nv[k] = wetness * (w - 0.05 * (p_n - p_s))

    settle(sums1.at[0:NX * NLAT - 1, :], group_recv.at[2])
    total = jnp.sum(sums1[...], axis=0, keepdims=True)
    mine2 = lax.div(lon, NX)
    vec[EDGE:EDGE + 1, :] = total
    sums2[pl.ds(mine2, 1), :] = total
    spread(vec.at[EDGE:EDGE + 1, :], sums2.at[pl.ds(mine2, 1), :], 3, far)
    settle(sums2.at[0:NZ - 1, :], group_recv.at[3])
    total = jnp.sum(sums2[...], axis=0, keepdims=True)
    mu = [total[:, j:j + 1] for j in range(6)]

    def gram(a, b, shift):
        out = None
        for i, ai in enumerate(a):
            for j, bj in enumerate(b):
                term = ai * bj * mu[i + j + shift]
                out = term if out is None else out + term
        return out

    one = jnp.ones((1, 1), jnp.float32)
    res, dire, sol = [one], [one], [0.0 * one] * 3
    rz = mu[0]
    for step in range(3):
        alpha = rz / (gram(dire, dire, 0) - gram(dire, dire, 1))
        sol = [sol[i] + alpha * dire[i] if i < len(dire) else sol[i] for i in range(3)]
        if step < 2:
            image = [
                (dire[i] if i < len(dire) else 0.0) - (dire[i - 1] if i else 0.0) for i in range(len(dire) + 1)
            ]
            res = [(res[i] if i < len(res) else 0.0) - alpha * image[i] for i in range(len(image))]
            new = gram(res, res, 0)
            beta = new / rz
            dire = [res[i] + (beta * dire[i] if i < len(dire) else 0.0) for i in range(len(res))]
            rz = new
    surf[...] = sol[0] * press[0, own, :] + sol[1] * press[1, own, :] + sol[2] * press[2, own, :]

    to_east.wait_send()
    to_west.wait_send()
    to_east3.wait_send()
    to_west3.wait_send()

    @pl.when(not_top)
    def _():
        for send in north_sends:
            send.wait_send()
        to_north3.wait_send()

    @pl.when(not_low)
    def _():
        for send in south_sends:
            send.wait_send()
        to_south3.wait_send()

    @pl.when(is_top)
    def _():
        settle(fold2.at[0:NLON - 1, 0:FOLD2, :], group_send.at[0])
        settle(fold3.at[0:NLON - 1], group_send.at[1])

    settle(sums1.at[0:NX * NLAT - 1, :], group_send.at[2])
    settle(sums2.at[0:NZ - 1, :], group_send.at[3])


def store(*refs):
    ins, outs, sem = refs[:5], refs[5:10], refs[10]
    copies = [pltpu.make_async_copy(i, o, sem.at[n]) for n, (i, o) in enumerate(zip(ins, outs))]
    for c in copies:
        c.start()
    for c in copies:
        c.wait()


def body(t, s, u, v, spans, water, opp, weights, anomaly):
    t, s, u, v, water, weights, anomaly, spans, opp = (
        pltpu.with_memory_space_constraint(r, pltpu.HBM) for r in (t, s, u, v, water, weights, anomaly, spans, opp)
    )
    hbm = pl.BlockSpec(memory_space=pltpu.HBM)
    smem = pl.BlockSpec(memory_space=pltpu.SMEM)
    vmem = pl.BlockSpec(memory_space=pltpu.VMEM)
    f32 = jnp.float32
    shapes = [jax.ShapeDtypeStruct((LEVELS, ROWS, LANES), f32)] * 4 + [jax.ShapeDtypeStruct((ROWS, LANES), f32)]
    full = ROWS + 2 * EDGE
    results = pl.pallas_call(
        kernel,
        out_shape=shapes,
        in_specs=[hbm] * 7 + [smem] * 2,
        out_specs=[vmem] * 5,
        scratch_shapes=[
            pltpu.VMEM((2, LEVELS, full, LANES), f32),
            pltpu.VMEM((2, LEVELS, ROWS, LANES), f32),
            pltpu.VMEM((ROWS, LANES), jnp.int32),
            pltpu.VMEM((2, ROWS, LANES), f32),
            pltpu.VMEM((5, 2, full, LANES), f32),
            pltpu.VMEM((ROWS, LANES), f32),
            pltpu.VMEM((2, full, LANES), f32),
            pltpu.VMEM((ROWS, LANES), f32),
            pltpu.VMEM((2, ROWS, LANES), f32),
            pltpu.VMEM((24, LANES), f32),
            pltpu.VMEM((NLON, 24, LANES), f32),
            pltpu.VMEM((FOLD3, LANES), f32),
            pltpu.VMEM((NLON, FOLD3, LANES), f32),
            pltpu.VMEM((3, full, LANES), f32),
            pltpu.VMEM((2 * EDGE, LANES), f32),
            pltpu.VMEM((NX * NLAT, LANES), f32),
            pltpu.VMEM((NZ, LANES), f32),
            pltpu.SemaphoreType.DMA((7,)),
            pltpu.SemaphoreType.DMA((12,)),
            pltpu.SemaphoreType.DMA((12,)),
            pltpu.SemaphoreType.DMA((4,)),
            pltpu.SemaphoreType.DMA((4,)),
        ],
        compiler_params=pltpu.CompilerParams(
            collective_id=0, has_side_effects=True, vmem_limit_bytes=40 * 1024 * 1024
        ),
    )(t, s, u, v, water, weights, anomaly, spans, opp)
    anyspec = pl.BlockSpec(memory_space=pl.ANY)
    return pl.pallas_call(
        store,
        out_shape=shapes,
        in_specs=[anyspec] * 5,
        out_specs=[anyspec] * 5,
        scratch_shapes=[pltpu.SemaphoreType.DMA((5,))],
        compiler_params=pltpu.CompilerParams(vmem_limit_bytes=8 * 1024 * 1024),
    )(*results)


def solution(mesh):
    deep = P(None, "lat", "lon")
    flat = P("lat", "lon")
    return jax.shard_map(
        body,
        mesh=mesh,
        in_specs=(deep, deep, deep, deep, P(), flat, P("lon"), flat, flat),
        out_specs=(deep, deep, deep, deep, flat),
        check_vma=False,
    )
```

```python
import functools

import jax
import jax.numpy as jnp
from jax import lax
from jax.experimental import pallas as pl
from jax.experimental.pallas import tpu as pltpu
from jax.sharding import PartitionSpec as P

MESH = pl.DeviceIdType.MESH
LEVELS = 10
ROWS = 64
LANES = 128
EDGE = 8
NLON = 32
NLAT = 8
NX = 4
NZ = 8
SPAN2 = 10
SPAN3 = 4
FOLD2 = 13
FOLD3 = 4 * LEVELS


def density(t, s):
    return -t - 0.15 * t * t + 0.8 * s - 0.2 * t * s


def lane_iota(rows):
    return lax.broadcasted_iota(jnp.int32, (rows, LANES), 1)


def kernel(
    t_hbm, s_hbm, u_hbm, v_hbm, w_hbm, e_hbm, a_hbm, spans, opp,
    nt, ns, nu, nv, surf,
    ts, uv, wbuf, ebuf, x, pack, wide, pack3, wide3, own2, fold2, own3, foldz, own3x, foldx, press, vec, sums1, sums2,
    in_sem, side_send, side_recv, group_send, group_recv,
):
    lon = lax.axis_index("lon")
    lat = lax.axis_index("lat")
    lon_x = lax.rem(lon, NX)
    lon_z = lax.div(lon, NX)
    east = lax.rem(lon + 1, NLON)
    west = lax.rem(lon + NLON - 1, NLON)
    is_top = lat == NLAT - 1
    is_low = lat == 0
    not_top = lat < NLAT - 1
    not_low = lat > 0

    loads = [
        pltpu.make_async_copy(w_hbm, wbuf, in_sem.at[0]),
        pltpu.make_async_copy(e_hbm, ebuf.at[0], in_sem.at[1]),
        pltpu.make_async_copy(a_hbm, ebuf.at[1], in_sem.at[2]),
        pltpu.make_async_copy(t_hbm, ts.at[0, :, EDGE:EDGE + ROWS, :], in_sem.at[3]),
        pltpu.make_async_copy(s_hbm, ts.at[1, :, EDGE:EDGE + ROWS, :], in_sem.at[4]),
        pltpu.make_async_copy(u_hbm, uv.at[0], in_sem.at[5]),
        pltpu.make_async_copy(v_hbm, uv.at[1], in_sem.at[6]),
    ]
    for load in loads:
        load.start()

    barrier = pltpu.get_barrier_semaphore()

    def greet(dev):
        pl.semaphore_signal(barrier, inc=1, device_id=dev, device_id_type=MESH)

    near = []
    for dx in range(NX):
        for dy in range(NLAT):
            if dx or dy:
                near.append((lon - lon_x + lax.rem(lon_x + dx, NX), lax.rem(lat + dy, NLAT)))
    far = [(lax.rem(lon + NX * k, NLON), lat) for k in range(1, NZ)]
    ring = [(lax.rem(lon + k, NLON), lat) for k in range(1, NLON)]
    for dev in near + far + [(east, lat), (west, lat)]:
        greet(dev)

    @pl.when(not_top)
    def _():
        greet((east, lat + 1))
        greet((west, lat + 1))

    @pl.when(not_low)
    def _():
        greet((east, lat - 1))
        greet((west, lat - 1))

    @pl.when(is_top)
    def _():
        for dev in ring:
            greet(dev)

    for load in loads[:3]:
        load.wait()
    own = slice(EDGE, EDGE + ROWS)
    weights = ebuf[0]
    diagonal = 4.0 + weights
    wetness = wbuf[...].astype(jnp.float32)
    scale = wetness / diagonal
    x[3, 0, own, :] = scale
    x[4, 0, own, :] = scale * (weights * ebuf[1])

    for load in loads[3:]:
        load.wait()
    zero = jnp.zeros((ROWS, LANES), jnp.float32)
    below, press_sum, east_sum, north_sum = zero, zero, zero, zero
    for k in range(LEVELS):
        span = spans[k]
        layer = density(ts[0, k, own, :], ts[1, k, own, :]) * span
        press_sum = press_sum + span * (below + 0.5 * layer)
        below = below + layer
        east_sum = east_sum + span * uv[0, k]
        north_sum = north_sum + span * uv[1, k]
    x[0, 0, own, :] = press_sum
    x[1, 0, own, :] = east_sum
    x[2, 0, own, :] = north_sum

    lanes = lane_iota(ROWS)
    packed = zero
    for f in range(5):
        moved = pltpu.roll(x[f, 0, own, :], SPAN2 * f + 5, 1)
        packed = jnp.where((lanes >= SPAN2 * f) & (lanes < SPAN2 * (f + 1)), moved, packed)
    pack[...] = packed
    packed = zero
    for q in range(2 * LEVELS):
        moved = pltpu.roll(ts[q // LEVELS, q % LEVELS, own, :], SPAN3 * q + 2, 1)
        packed = jnp.where((lanes >= SPAN3 * q) & (lanes < SPAN3 * (q + 1)), moved, packed)
    pack3[...] = packed

    @pl.when(is_top)
    def _():
        last = EDGE + ROWS - 1
        up = x[0, 0, last - 2:last + 1, :]
        down = x[0, 0, last - 4:last - 1, :]
        inner = slice(last - 3, last)
        flow = jnp.where(x[3, 0, inner, :] > 0.0, x[2, 0, inner, :] - 0.05 * (up - down), 0.0)
        for r in range(3):
            row = last - r
            own2[r:r + 1, :] = x[0, 0, row:row + 1, :]
            own2[3 + r:4 + r, :] = -x[1, 0, row:row + 1, :]
            half = 0.5 * x[3, 0, row:row + 1, :]
            own2[7 + r:8 + r, :] = x[3, 0, row:row + 1, :]
            inside = flow[2 - r:3 - r] if r < 2 else flow[0:1] - flow[2:3]
            own2[10 + r:11 + r, :] = x[4, 0, row:row + 1, :] + half * inside
        own2[6:7, :] = -x[2, 0, last:last + 1, :]
        fold2[lon, 0:FOLD2, :] = own2[0:FOLD2, :]
        for q in range(2 * LEVELS):
            own3[2 * q:2 * q + 2, :] = ts[q // LEVELS, q % LEVELS, EDGE + ROWS - 2:EDGE + ROWS, :]
        foldz[lon_z] = own3[...]
        for f in range(5):
            x[f, 0, EDGE + ROWS:, :] = jnp.zeros((EDGE, LANES), jnp.float32)

    @pl.when(is_low)
    def _():
        for f in range(5):
            x[f, 0, 0:EDGE, :] = jnp.zeros((EDGE, LANES), jnp.float32)
        for q in range(2 * LEVELS):
            ts[q // LEVELS, q % LEVELS, 0:EDGE, :] = jnp.zeros((EDGE, LANES), jnp.float32)

    base = 31 + 7 + 2

    @pl.when(is_top)
    def _():
        pl.semaphore_wait(barrier, base + 2 + NLON - 1)

    @pl.when(is_low)
    def _():
        pl.semaphore_wait(barrier, base + 2)

    @pl.when(not_top & not_low)
    def _():
        pl.semaphore_wait(barrier, base + 4)

    def copy(src, dst, sem, dev):
        return pltpu.make_async_remote_copy(
            src_ref=src, dst_ref=dst, send_sem=side_send.at[sem], recv_sem=side_recv.at[sem],
            device_id=dev, device_id_type=MESH,
        )

    top_rows = slice(EDGE + ROWS, EDGE + ROWS + EDGE)
    to_east = copy(pack, wide.at[0, own, :], 0, (east, lat))
    to_west = copy(pack, wide.at[1, own, :], 1, (west, lat))
    to_north = copy(x.at[:, 0, ROWS:EDGE + ROWS, :], x.at[:, 0, 0:EDGE, :], 2, (lon, lat + 1))
    to_ne = copy(pack.at[ROWS - EDGE:ROWS, :], wide.at[0, 0:EDGE, :], 3, (east, lat + 1))
    to_nw = copy(pack.at[ROWS - EDGE:ROWS, :], wide.at[1, 0:EDGE, :], 4, (west, lat + 1))
    to_south = copy(x.at[:, 0, EDGE:2 * EDGE, :], x.at[:, 0, top_rows, :], 5, (lon, lat - 1))
    to_se = copy(pack.at[0:EDGE, :], wide.at[0, top_rows, :], 6, (east, lat - 1))
    to_sw = copy(pack.at[0:EDGE, :], wide.at[1, top_rows, :], 7, (west, lat - 1))
    to_east3 = copy(pack3, wide3.at[0], 8, (east, lat))
    to_west3 = copy(pack3, wide3.at[1], 9, (west, lat))
    to_north3 = copy(
        ts.at[:, :, EDGE + ROWS - 2:EDGE + ROWS, :], ts.at[:, :, EDGE - 2:EDGE, :], 10, (lon, lat + 1)
    )
    to_south3 = copy(
        ts.at[:, :, EDGE:EDGE + 2, :], ts.at[:, :, EDGE + ROWS:EDGE + ROWS + 2, :], 11, (lon, lat - 1)
    )
    north_sends = (to_north, to_ne, to_nw)
    south_sends = (to_south, to_se, to_sw)

    def spread(src, dst, sem, devs):
        for dev in devs:
            pltpu.make_async_remote_copy(
                src_ref=src, dst_ref=dst, send_sem=group_send.at[sem], recv_sem=group_recv.at[sem],
                device_id=dev, device_id_type=MESH,
            ).start()

    def settle(ref, sem):
        pltpu.make_async_copy(ref, ref, sem).wait()

    @pl.when(is_top)
    def _():
        spread(own2.at[0:FOLD2, :], fold2.at[lon, 0:FOLD2, :], 0, ring)

    to_east.start()
    to_west.start()

    @pl.when(not_top)
    def _():
        for send in north_sends:
            send.start()

    @pl.when(not_low)
    def _():
        for send in south_sends:
            send.start()

    to_east3.start()
    to_west3.start()

    @pl.when(not_top)
    def _():
        to_north3.start()

    @pl.when(not_low)
    def _():
        to_south3.start()

    to_east.wait_recv()
    to_west.wait_recv()

    @pl.when(not_low)
    def _():
        for send in north_sends:
            send.wait_recv()

    @pl.when(not_top)
    def _():
        for send in south_sends:
            send.wait_recv()

    lanes_w = lane_iota(EDGE + ROWS + EDGE)
    eastern = lax.rem(lanes_w, SPAN2) < 5
    merged = jnp.where(eastern, wide[0], wide[1])
    for f in range(5):
        x[f, 1] = pltpu.roll(merged, LANES - (SPAN2 * f + 5), 1)

    @pl.when(is_low)
    def _():
        for f in range(5):
            x[f, 1, 0:EDGE, :] = jnp.zeros((EDGE, LANES), jnp.float32)

    lanes_e = lane_iota(EDGE)
    first = opp[0]
    slot = lax.div(first, LANES)
    offset = first - slot * LANES
    slot_p = lax.rem(slot + 1, NLON)
    slot_m = lax.rem(slot + NLON - 1, NLON)
    slot_mm = lax.rem(slot + NLON - 2, NLON)
    index = (offset - lanes_e) & (LANES - 1)

    def turn(tile):
        return jnp.take_along_axis(tile, index, axis=1)

    @pl.when(is_top)
    def _():
        settle(fold2.at[0:NLON - 1, 0:FOLD2, :], group_recv.at[0])
        kept = lanes_e <= offset
        near_half = index < LANES // 2
        mine, aside = [], []
        for tile in range(2):
            part = slice(EDGE * tile, EDGE * (tile + 1))
            b_p, b_0, b_m, b_mm = (fold2[s, part, :] for s in (slot_p, slot, slot_m, slot_mm))
            mine.append(turn(jnp.where(kept, b_0, b_m)))
            right = jnp.where(kept, b_m, b_mm)
            left = jnp.where(kept, b_p, b_0)
            aside.append(turn(jnp.where(near_half, right, left)))
        for half, tiles in ((0, mine), (1, aside)):
            north = EDGE + ROWS
            x[0, half, north:north + 3, :] = tiles[0][0:3]
            x[1, half, north:north + 3, :] = tiles[0][3:6]
            x[2, half, north:north + 1, :] = tiles[0][6:7]
            x[3, half, north:north + 1, :] = tiles[0][7:8]
            x[3, half, north + 1:north + 3, :] = tiles[1][0:2]
            x[4, half, north:north + 3, :] = tiles[1][2:5]

    full = EDGE + ROWS + EDGE
    first_lane = lanes_w == 0
    last_lane = lanes_w == LANES - 1

    def plus_east(a, b):
        return (
            pltpu.roll(jnp.where(first_lane, b, a), LANES - 1, 1),
            pltpu.roll(jnp.where(first_lane, a, b), LANES - 1, 1),
        )

    def plus_west(a, b):
        return (
            pltpu.roll(jnp.where(last_lane, b, a), 1, 1),
            pltpu.roll(jnp.where(last_lane, a, b), 1, 1),
        )

    def north_of(a):
        return pltpu.roll(a, full - 1, 0)

    def south_of(a):
        return pltpu.roll(a, 1, 0)

    scale2 = (x[3, 0], x[3, 1])
    wet2 = (scale2[0] > 0.0, scale2[1] > 0.0)
    q2 = (x[0, 0], x[0, 1])
    q_e = plus_east(*q2)
    q_w = plus_west(*q2)
    flow_e, flow_n = [], []
    rows_w = lax.broadcasted_iota(jnp.int32, (full, LANES), 0)
    rows_end = jnp.where(is_top, EDGE + ROWS, full)
    for h in range(2):
        flow_e.append(jnp.where(wet2[h], x[1, h] - 0.05 * (q_e[h] - q_w[h]), 0.0))
        flow_n.append(jnp.where(wet2[h] & (rows_w <= rows_end), x[2, h] - 0.05 * (north_of(q2[h]) - south_of(q2[h])), 0.0))
    f_e = plus_east(*flow_e)
    f_w = plus_west(*flow_e)
    basis = []
    v = tuple(
        x[4, h] - scale2[h] * (0.5 * (f_e[h] - f_w[h] + north_of(flow_n[h]) - south_of(flow_n[h])))
        for h in range(2)
    )
    basis.append(v[0][EDGE:EDGE + ROWS])
    for _ in range(3):
        v_e = plus_east(*v)
        v_w = plus_west(*v)
        v = tuple(scale2[h] * (v_e[h] + v_w[h] + north_of(v[h]) + south_of(v[h])) for h in range(2))
        basis.append(v[0][EDGE:EDGE + ROWS])

    for i in range(3):
        press[i, own, :] = basis[i]
    sub = lax.broadcasted_iota(jnp.int32, (EDGE, LANES), 0)
    table = jnp.zeros((EDGE, LANES), jnp.float32)
    for j, (l, r) in enumerate(((0, 0), (0, 1), (1, 1), (1, 2), (2, 2), (2, 3))):
        product = (diagonal * basis[l]) * basis[r]
        line = jnp.sum(product.reshape(ROWS // EDGE, EDGE, LANES), axis=0)
        line = jnp.sum(line, axis=0, keepdims=True)
        table = jnp.where(sub == j, line, table)
    table = jnp.sum(table, axis=1, keepdims=True)
    message = jnp.sum(jnp.where(sub == lanes_e, table, 0.0), axis=0, keepdims=True)
    vec[0:1, :] = message
    mine1 = lon_x * NLAT + lat
    sums1[pl.ds(mine1, 1), :] = message
    spread(vec.at[0:1, :], sums1.at[pl.ds(mine1, 1), :], 2, near)

    @pl.when(is_top)
    def _():
        spread(own3, foldz.at[lon_z], 1, far)

    to_east3.wait_recv()
    to_west3.wait_recv()

    @pl.when(not_low)
    def _():
        to_north3.wait_recv()

    @pl.when(not_top)
    def _():
        to_south3.wait_recv()

    def update(low, rows, parts):
        lane = lane_iota(rows)
        part = slice(low, low + rows)
        wet = wbuf[part, :].astype(jnp.float32)
        joined = jnp.where((lane & 2) == 0, wide3[0, part, :], wide3[1, part, :])
        below = jnp.zeros((rows + 2 * EDGE, LANES), jnp.float32)
        below_side = jnp.zeros((rows, LANES), jnp.float32)
        mid = slice(EDGE, EDGE + rows)
        for k in range(LEVELS):
            span = spans[k]
            u = uv[0, k, part, :]
            w = uv[1, k, part, :]
            sides = []
            for f in range(2):
                side = pltpu.roll(joined, LANES - (SPAN3 * (f * LEVELS + k) + 2), 1)
                sides.append(side)
                at = EDGE + low
                c = ts[f, k, at:at + rows, :]
                e1 = pltpu.roll(jnp.where(lane == 0, side, c), LANES - 1, 1)
                e2 = pltpu.roll(jnp.where(lane < 2, side, c), LANES - 2, 1)
                w1 = pltpu.roll(jnp.where(lane == LANES - 1, side, c), 1, 1)
                w2 = pltpu.roll(jnp.where(lane >= LANES - 2, side, c), 2, 1)
                n1 = ts[f, k, at + 1:at + rows + 1, :]
                n2 = ts[f, k, at + 2:at + rows + 2, :]
                s1 = ts[f, k, at - 1:at + rows - 1, :]
                s2 = ts[f, k, at - 2:at + rows - 2, :]
                grad_e = (8.0 * (e1 - w1) - (e2 - w2)) * (1.0 / 12.0)
                grad_n = (8.0 * (n1 - s1) - (n2 - s2)) * (1.0 / 12.0)
                laplace = e1 + w1 + n1 + s1 - 4.0 * c
                out = (nt, ns)[f]
                out[k, part, :] = c + wet * (-0.1 * (u * grad_e + w * grad_n) + 0.1 * laplace)
            reach = slice(low, low + rows + 2 * EDGE)
            layer = density(ts[0, k, reach, :], ts[1, k, reach, :]) * span
            level = below + 0.5 * layer
            below = below + layer
            p_n = pltpu.roll(level, rows + 2 * EDGE - 1, 0)[mid]
            p_s = pltpu.roll(level, 1, 0)[mid]
            nv[k, part, :] = wet * (w - 0.05 * (p_n - p_s))
            if parts > 1:
                layer_side = density(sides[0], sides[1]) * span
                level_side = below_side + 0.5 * layer_side
                below_side = below_side + layer_side
                centre = level[mid]
                p_e = pltpu.roll(jnp.where(lane == 0, level_side, centre), LANES - 1, 1)
                p_w = pltpu.roll(jnp.where(lane == LANES - 1, level_side, centre), 1, 1)
                nu[k, part, :] = wet * (u - 0.05 * (p_e - p_w))

    update(0, ROWS, 2)

    settle(sums1.at[0:NX * NLAT - 1, :], group_recv.at[2])
    total = jnp.sum(sums1[...], axis=0, keepdims=True)
    mine2 = lon_z
    vec[EDGE:EDGE + 1, :] = total
    sums2[pl.ds(mine2, 1), :] = total
    spread(vec.at[EDGE:EDGE + 1, :], sums2.at[pl.ds(mine2, 1), :], 3, far)

    beside = [(lon - lon_x + lax.rem(lon_x + k, NX), lat) for k in range(1, NX)]
    kept = lane_iota(FOLD3) <= offset

    @pl.when(is_top)
    def _():
        settle(foldz.at[0:NZ - 1], group_recv.at[1])
        base_slot = slot + lon_x + NLON
        row_0 = lax.div(lax.rem(base_slot - (slot & (NX - 1)), NLON), NX)
        row_1 = lax.div(lax.rem(base_slot - 1 - ((slot + NX - 1) & (NX - 1)), NLON), NX)
        joint = jnp.where(kept, foldz[row_0], foldz[row_1])
        own3x[...] = joint
        foldx[lon_x] = joint
        spread(own3x, foldx.at[lon_x], 4, beside)

    settle(sums2.at[0:NZ - 1, :], group_recv.at[3])
    total = jnp.sum(sums2[...], axis=0, keepdims=True)
    mu = [total[:, j:j + 1] for j in range(6)]

    def gram(a, b, shift):
        out = None
        for i, ai in enumerate(a):
            for j, bj in enumerate(b):
                term = ai * bj * mu[i + j + shift]
                out = term if out is None else out + term
        return out

    one = jnp.ones((1, 1), jnp.float32)
    res, dire, sol = [one], [one], [0.0 * one] * 3
    rz = mu[0]
    for step in range(3):
        alpha = rz / (gram(dire, dire, 0) - gram(dire, dire, 1))
        sol = [sol[i] + alpha * dire[i] if i < len(dire) else sol[i] for i in range(3)]
        if step < 2:
            image = [
                (dire[i] if i < len(dire) else 0.0) - (dire[i - 1] if i else 0.0) for i in range(len(dire) + 1)
            ]
            res = [(res[i] if i < len(res) else 0.0) - alpha * image[i] for i in range(len(image))]
            new = gram(res, res, 0)
            beta = new / rz
            dire = [res[i] + (beta * dire[i] if i < len(dire) else 0.0) for i in range(len(res))]
            rz = new
    surf[...] = sol[0] * press[0, own, :] + sol[1] * press[1, own, :] + sol[2] * press[2, own, :]

    @pl.when(is_top)
    def _():
        settle(foldx.at[0:NX - 1], group_recv.at[4])
        side_0 = slot & (NX - 1)
        side_1 = (slot + NX - 1) & (NX - 1)
        for tile in range(FOLD3 // EDGE):
            part = slice(EDGE * tile, EDGE * (tile + 1))
            turned = turn(jnp.where(kept[part], foldx[side_0, part, :], foldx[side_1, part, :]))
            for i in range(EDGE):
                q, r = (EDGE * tile + i) // 2, (EDGE * tile + i) % 2
                ts[q // LEVELS, q % LEVELS, EDGE + ROWS + 1 - r:EDGE + ROWS + 2 - r, :] = turned[i:i + 1]
        update(ROWS - EDGE, EDGE, 1)

    to_east.wait_send()
    to_west.wait_send()
    to_east3.wait_send()
    to_west3.wait_send()

    @pl.when(not_top)
    def _():
        for send in north_sends:
            send.wait_send()
        to_north3.wait_send()

    @pl.when(not_low)
    def _():
        for send in south_sends:
            send.wait_send()
        to_south3.wait_send()

    @pl.when(is_top)
    def _():
        settle(fold2.at[0:NLON - 1, 0:FOLD2, :], group_send.at[0])
        settle(foldz.at[0:NZ - 1], group_send.at[1])
        settle(foldx.at[0:NX - 1], group_send.at[4])

    settle(sums1.at[0:NX * NLAT - 1, :], group_send.at[2])
    settle(sums2.at[0:NZ - 1, :], group_send.at[3])


def store(*refs):
    ins, outs, sem = refs[:5], refs[5:10], refs[10]
    copies = [pltpu.make_async_copy(i, o, sem.at[n]) for n, (i, o) in enumerate(zip(ins, outs))]
    for c in copies:
        c.start()
    for c in copies:
        c.wait()


def body(t, s, u, v, spans, water, opp, weights, anomaly):
    t, s, u, v, water, weights, anomaly, spans, opp = (
        pltpu.with_memory_space_constraint(r, pltpu.HBM) for r in (t, s, u, v, water, weights, anomaly, spans, opp)
    )
    hbm = pl.BlockSpec(memory_space=pltpu.HBM)
    smem = pl.BlockSpec(memory_space=pltpu.SMEM)
    vmem = pl.BlockSpec(memory_space=pltpu.VMEM)
    f32 = jnp.float32
    shapes = [jax.ShapeDtypeStruct((LEVELS, ROWS, LANES), f32)] * 4 + [jax.ShapeDtypeStruct((ROWS, LANES), f32)]
    full = ROWS + 2 * EDGE
    results = pl.pallas_call(
        kernel,
        out_shape=shapes,
        in_specs=[hbm] * 7 + [smem] * 2,
        out_specs=[vmem] * 5,
        scratch_shapes=[
            pltpu.VMEM((2, LEVELS, full, LANES), f32),
            pltpu.VMEM((2, LEVELS, ROWS, LANES), f32),
            pltpu.VMEM((ROWS, LANES), jnp.int32),
            pltpu.VMEM((2, ROWS, LANES), f32),
            pltpu.VMEM((5, 2, full, LANES), f32),
            pltpu.VMEM((ROWS, LANES), f32),
            pltpu.VMEM((2, full, LANES), f32),
            pltpu.VMEM((ROWS, LANES), f32),
            pltpu.VMEM((2, ROWS, LANES), f32),
            pltpu.VMEM((16, LANES), f32),
            pltpu.VMEM((NLON, 16, LANES), f32),
            pltpu.VMEM((FOLD3, LANES), f32),
            pltpu.VMEM((NZ, FOLD3, LANES), f32),
            pltpu.VMEM((FOLD3, LANES), f32),
            pltpu.VMEM((NX, FOLD3, LANES), f32),
            pltpu.VMEM((3, full, LANES), f32),
            pltpu.VMEM((2 * EDGE, LANES), f32),
            pltpu.VMEM((NX * NLAT, LANES), f32),
            pltpu.VMEM((NZ, LANES), f32),
            pltpu.SemaphoreType.DMA((7,)),
            pltpu.SemaphoreType.DMA((12,)),
            pltpu.SemaphoreType.DMA((12,)),
            pltpu.SemaphoreType.DMA((5,)),
            pltpu.SemaphoreType.DMA((5,)),
        ],
        compiler_params=pltpu.CompilerParams(
            collective_id=0, has_side_effects=True, vmem_limit_bytes=40 * 1024 * 1024
        ),
    )(t, s, u, v, water, weights, anomaly, spans, opp)
    anyspec = pl.BlockSpec(memory_space=pl.ANY)
    return pl.pallas_call(
        store,
        out_shape=shapes,
        in_specs=[anyspec] * 5,
        out_specs=[anyspec] * 5,
        scratch_shapes=[pltpu.SemaphoreType.DMA((5,))],
        compiler_params=pltpu.CompilerParams(vmem_limit_bytes=8 * 1024 * 1024),
    )(*results)


def solution(mesh):
    deep = P(None, "lat", "lon")
    flat = P("lat", "lon")
    return jax.shard_map(
        body,
        mesh=mesh,
        in_specs=(deep, deep, deep, deep, P(), flat, P("lon"), flat, flat),
        out_specs=(deep, deep, deep, deep, flat),
        check_vma=False,
    )
```

```python
import itertools

import jax
import jax.numpy as jnp
from jax import lax
from jax.experimental import pallas as pl
from jax.experimental.pallas import tpu as pltpu
from jax.sharding import PartitionSpec as P

MESH = pl.DeviceIdType.MESH
LEVELS = 10
ROWS = 64
LANES = 128
EDGE = 8
NLON = 32
NLAT = 8
NX = 4
NZ = 8
SPAN2 = 10
SPAN3 = 4
FOLD2 = 13
FOLD3 = 4 * LEVELS


def density(t, s):
    return -t - 0.15 * t * t + 0.8 * s - 0.2 * t * s


def lane_iota(rows):
    return lax.broadcasted_iota(jnp.int32, (rows, LANES), 1)


def kernel(
    t_hbm, s_hbm, u_hbm, v_hbm, w_hbm, e_hbm, a_hbm, spans, opp,
    nt, ns, nu, nv, surf,
    ts, uv, wbuf, ebuf, x, pack, wide, pack3, wide3, own2, fold2, own3, foldz, own3x, foldx, press, vec, sums1, sums2,
    in_sem, side_send, side_recv, group_send, group_recv,
):
    lon = lax.axis_index("lon")
    lat = lax.axis_index("lat")
    lon_x = lax.rem(lon, NX)
    lon_z = lax.div(lon, NX)
    east = lax.rem(lon + 1, NLON)
    west = lax.rem(lon + NLON - 1, NLON)
    is_top = lat == NLAT - 1
    is_low = lat == 0
    not_top = lat < NLAT - 1
    not_low = lat > 0

    barrier = pltpu.get_barrier_semaphore()

    def greet(dev):
        pl.semaphore_signal(barrier, inc=1, device_id=dev, device_id_type=MESH)

    def hops(step, size):
        return min(step, size - step)

    lat_y = lax.div(lat, 2)
    lat_c = lat & 1
    zs = [((lon_z + d) & (NZ - 1)) * NX for d in range(NZ)]
    xs = [(lon_x + d) & (NX - 1) for d in range(NX)]
    lats = {(dy, dc): ((lat_y + dy) & (NLAT // 2 - 1)) * 2 + (lat_c ^ dc) for dy in range(NLAT // 2) for dc in range(2)}

    def at(dz, dx, dy, dc):
        return (zs[dz] + xs[dx], lats[dy, dc])

    near = [
        at(0, dx, dy, dc)
        for dx, dy, dc in sorted(
            itertools.product(range(NX), range(NLAT // 2), range(2)),
            key=lambda o: -hops(o[0], NX) - hops(o[1], NLAT // 2) - 0.5 * o[2],
        )
        if dx or dy or dc
    ]
    far = [at(dz, 0, 0, 0) for dz in sorted(range(1, NZ), key=lambda o: -hops(o, NZ))]
    ring = [
        at(dz, dx, 0, 0)
        for dz, dx in sorted(
            itertools.product(range(NZ), range(NX)), key=lambda o: -hops(o[0], NZ) - hops(o[1], NX)
        )
        if dz or dx
    ]

    @pl.when(is_top)
    def _():
        for dev in ring:
            greet(dev)

    for dev in far + near + [(east, lat), (west, lat)]:
        greet(dev)

    @pl.when(not_top)
    def _():
        greet((east, lat + 1))
        greet((west, lat + 1))

    @pl.when(not_low)
    def _():
        greet((east, lat - 1))
        greet((west, lat - 1))

    loads = [
        pltpu.make_async_copy(w_hbm, wbuf, in_sem.at[0]),
        pltpu.make_async_copy(e_hbm, ebuf.at[0], in_sem.at[1]),
        pltpu.make_async_copy(a_hbm, ebuf.at[1], in_sem.at[2]),
        pltpu.make_async_copy(t_hbm, ts.at[0, :, EDGE:EDGE + ROWS, :], in_sem.at[3]),
        pltpu.make_async_copy(s_hbm, ts.at[1, :, EDGE:EDGE + ROWS, :], in_sem.at[4]),
        pltpu.make_async_copy(u_hbm, uv.at[0], in_sem.at[5]),
        pltpu.make_async_copy(v_hbm, uv.at[1], in_sem.at[6]),
    ]
    for load in loads:
        load.start()

    for load in loads[:3]:
        load.wait()
    own = slice(EDGE, EDGE + ROWS)
    weights = ebuf[0]
    diagonal = 4.0 + weights
    wetness = wbuf[...].astype(jnp.float32)
    scale = wetness / diagonal
    x[3, 0, own, :] = scale
    x[4, 0, own, :] = scale * (weights * ebuf[1])

    for load in loads[3:]:
        load.wait()
    zero = jnp.zeros((ROWS, LANES), jnp.float32)
    below, press_sum, east_sum, north_sum = zero, zero, zero, zero
    for k in range(LEVELS):
        span = spans[k]
        layer = density(ts[0, k, own, :], ts[1, k, own, :]) * span
        press_sum = press_sum + span * (below + 0.5 * layer)
        below = below + layer
        east_sum = east_sum + span * uv[0, k]
        north_sum = north_sum + span * uv[1, k]
    x[0, 0, own, :] = press_sum
    x[1, 0, own, :] = east_sum
    x[2, 0, own, :] = north_sum

    lanes = lane_iota(ROWS)
    packed = zero
    for f in range(5):
        moved = pltpu.roll(x[f, 0, own, :], SPAN2 * f + 5, 1)
        packed = jnp.where((lanes >= SPAN2 * f) & (lanes < SPAN2 * (f + 1)), moved, packed)
    pack[...] = packed
    packed = zero
    for q in range(2 * LEVELS):
        moved = pltpu.roll(ts[q // LEVELS, q % LEVELS, own, :], SPAN3 * q + 2, 1)
        packed = jnp.where((lanes >= SPAN3 * q) & (lanes < SPAN3 * (q + 1)), moved, packed)
    pack3[...] = packed

    @pl.when(is_top)
    def _():
        last = EDGE + ROWS - 1
        up = x[0, 0, last - 2:last + 1, :]
        down = x[0, 0, last - 4:last - 1, :]
        inner = slice(last - 3, last)
        flow = jnp.where(x[3, 0, inner, :] > 0.0, x[2, 0, inner, :] - 0.05 * (up - down), 0.0)
        for r in range(3):
            row = last - r
            own2[r:r + 1, :] = x[0, 0, row:row + 1, :]
            own2[3 + r:4 + r, :] = -x[1, 0, row:row + 1, :]
            half = 0.5 * x[3, 0, row:row + 1, :]
            own2[7 + r:8 + r, :] = x[3, 0, row:row + 1, :]
            inside = flow[2 - r:3 - r] if r < 2 else flow[0:1] - flow[2:3]
            own2[10 + r:11 + r, :] = x[4, 0, row:row + 1, :] + half * inside
        own2[6:7, :] = -x[2, 0, last:last + 1, :]
        fold2[lon, 0:FOLD2, :] = own2[0:FOLD2, :]
        for q in range(2 * LEVELS):
            own3[2 * q:2 * q + 2, :] = ts[q // LEVELS, q % LEVELS, EDGE + ROWS - 2:EDGE + ROWS, :]
        foldz[lon_z] = own3[...]
        for f in range(5):
            x[f, 0, EDGE + ROWS:, :] = jnp.zeros((EDGE, LANES), jnp.float32)

    @pl.when(is_low)
    def _():
        for f in range(5):
            x[f, 0, 0:EDGE, :] = jnp.zeros((EDGE, LANES), jnp.float32)
        for q in range(2 * LEVELS):
            ts[q // LEVELS, q % LEVELS, 0:EDGE, :] = jnp.zeros((EDGE, LANES), jnp.float32)

    base = 31 + 7 + 2

    @pl.when(is_top)
    def _():
        pl.semaphore_wait(barrier, base + 2 + NLON - 1)

    @pl.when(is_low)
    def _():
        pl.semaphore_wait(barrier, base + 2)

    @pl.when(not_top & not_low)
    def _():
        pl.semaphore_wait(barrier, base + 4)

    def copy(src, dst, sem, dev):
        return pltpu.make_async_remote_copy(
            src_ref=src, dst_ref=dst, send_sem=side_send.at[sem], recv_sem=side_recv.at[sem],
            device_id=dev, device_id_type=MESH,
        )

    top_rows = slice(EDGE + ROWS, EDGE + ROWS + EDGE)
    to_east = copy(pack, wide.at[0, own, :], 0, (east, lat))
    to_west = copy(pack, wide.at[1, own, :], 1, (west, lat))
    to_north = copy(x.at[:, 0, ROWS:EDGE + ROWS, :], x.at[:, 0, 0:EDGE, :], 2, (lon, lat + 1))
    to_ne = copy(pack.at[ROWS - EDGE:ROWS, :], wide.at[0, 0:EDGE, :], 3, (east, lat + 1))
    to_nw = copy(pack.at[ROWS - EDGE:ROWS, :], wide.at[1, 0:EDGE, :], 4, (west, lat + 1))
    to_south = copy(x.at[:, 0, EDGE:2 * EDGE, :], x.at[:, 0, top_rows, :], 5, (lon, lat - 1))
    to_se = copy(pack.at[0:EDGE, :], wide.at[0, top_rows, :], 6, (east, lat - 1))
    to_sw = copy(pack.at[0:EDGE, :], wide.at[1, top_rows, :], 7, (west, lat - 1))
    to_east3 = copy(pack3, wide3.at[0], 8, (east, lat))
    to_west3 = copy(pack3, wide3.at[1], 9, (west, lat))
    to_north3 = copy(
        ts.at[:, :, EDGE + ROWS - 2:EDGE + ROWS, :], ts.at[:, :, EDGE - 2:EDGE, :], 10, (lon, lat + 1)
    )
    to_south3 = copy(
        ts.at[:, :, EDGE:EDGE + 2, :], ts.at[:, :, EDGE + ROWS:EDGE + ROWS + 2, :], 11, (lon, lat - 1)
    )
    north_sends = (to_north, to_ne, to_nw)
    south_sends = (to_south, to_se, to_sw)

    def spread(src, dst, sem, devs):
        for dev in devs:
            pltpu.make_async_remote_copy(
                src_ref=src, dst_ref=dst, send_sem=group_send.at[sem], recv_sem=group_recv.at[sem],
                device_id=dev, device_id_type=MESH,
            ).start()

    def settle(ref, sem):
        pltpu.make_async_copy(ref, ref, sem).wait()

    @pl.when(is_top)
    def _():
        spread(own2.at[0:FOLD2, :], fold2.at[lon, 0:FOLD2, :], 0, ring)

    to_east.start()
    to_west.start()

    @pl.when(not_top)
    def _():
        for send in north_sends:
            send.start()

    @pl.when(not_low)
    def _():
        for send in south_sends:
            send.start()

    to_east3.start()
    to_west3.start()

    @pl.when(not_top)
    def _():
        to_north3.start()

    @pl.when(not_low)
    def _():
        to_south3.start()

    to_east.wait_recv()
    to_west.wait_recv()

    @pl.when(not_low)
    def _():
        for send in north_sends:
            send.wait_recv()

    @pl.when(not_top)
    def _():
        for send in south_sends:
            send.wait_recv()

    lanes_w = lane_iota(EDGE + ROWS + EDGE)
    eastern = lax.rem(lanes_w, SPAN2) < 5
    merged = jnp.where(eastern, wide[0], wide[1])
    for f in range(5):
        x[f, 1] = pltpu.roll(merged, LANES - (SPAN2 * f + 5), 1)

    @pl.when(is_low)
    def _():
        for f in range(5):
            x[f, 1, 0:EDGE, :] = jnp.zeros((EDGE, LANES), jnp.float32)

    lanes_e = lane_iota(EDGE)
    first = opp[0]
    slot = lax.div(first, LANES)
    offset = first - slot * LANES
    slot_p = lax.rem(slot + 1, NLON)
    slot_m = lax.rem(slot + NLON - 1, NLON)
    slot_mm = lax.rem(slot + NLON - 2, NLON)
    index = (offset - lanes_e) & (LANES - 1)

    def turn(tile):
        return jnp.take_along_axis(tile, index, axis=1)

    @pl.when(is_top)
    def _():
        settle(fold2.at[0:NLON - 1, 0:FOLD2, :], group_recv.at[0])
        kept = lanes_e <= offset
        near_half = index < LANES // 2
        mine, aside = [], []
        for tile in range(2):
            part = slice(EDGE * tile, EDGE * (tile + 1))
            b_p, b_0, b_m, b_mm = (fold2[s, part, :] for s in (slot_p, slot, slot_m, slot_mm))
            mine.append(turn(jnp.where(kept, b_0, b_m)))
            right = jnp.where(kept, b_m, b_mm)
            left = jnp.where(kept, b_p, b_0)
            aside.append(turn(jnp.where(near_half, right, left)))
        for half, tiles in ((0, mine), (1, aside)):
            north = EDGE + ROWS
            x[0, half, north:north + 3, :] = tiles[0][0:3]
            x[1, half, north:north + 3, :] = tiles[0][3:6]
            x[2, half, north:north + 1, :] = tiles[0][6:7]
            x[3, half, north:north + 1, :] = tiles[0][7:8]
            x[3, half, north + 1:north + 3, :] = tiles[1][0:2]
            x[4, half, north:north + 3, :] = tiles[1][2:5]

    full = EDGE + ROWS + EDGE
    first_lane = lanes_w == 0
    last_lane = lanes_w == LANES - 1

    def plus_east(a, b):
        return (
            pltpu.roll(jnp.where(first_lane, b, a), LANES - 1, 1),
            pltpu.roll(jnp.where(first_lane, a, b), LANES - 1, 1),
        )

    def plus_west(a, b):
        return (
            pltpu.roll(jnp.where(last_lane, b, a), 1, 1),
            pltpu.roll(jnp.where(last_lane, a, b), 1, 1),
        )

    def north_of(a):
        return pltpu.roll(a, full - 1, 0)

    def south_of(a):
        return pltpu.roll(a, 1, 0)

    scale2 = (x[3, 0], x[3, 1])
    wet2 = (scale2[0] > 0.0, scale2[1] > 0.0)
    q2 = (x[0, 0], x[0, 1])
    q_e = plus_east(*q2)
    q_w = plus_west(*q2)
    flow_e, flow_n = [], []
    rows_w = lax.broadcasted_iota(jnp.int32, (full, LANES), 0)
    rows_end = jnp.where(is_top, EDGE + ROWS, full)
    for h in range(2):
        flow_e.append(jnp.where(wet2[h], x[1, h] - 0.05 * (q_e[h] - q_w[h]), 0.0))
        flow_n.append(jnp.where(wet2[h] & (rows_w <= rows_end), x[2, h] - 0.05 * (north_of(q2[h]) - south_of(q2[h])), 0.0))
    f_e = plus_east(*flow_e)
    f_w = plus_west(*flow_e)
    basis = []
    v = tuple(
        x[4, h] - scale2[h] * (0.5 * (f_e[h] - f_w[h] + north_of(flow_n[h]) - south_of(flow_n[h])))
        for h in range(2)
    )
    basis.append(v[0][EDGE:EDGE + ROWS])
    for _ in range(3):
        v_e = plus_east(*v)
        v_w = plus_west(*v)
        v = tuple(scale2[h] * (v_e[h] + v_w[h] + north_of(v[h]) + south_of(v[h])) for h in range(2))
        basis.append(v[0][EDGE:EDGE + ROWS])

    for i in range(3):
        press[i, own, :] = basis[i]
    sub = lax.broadcasted_iota(jnp.int32, (EDGE, LANES), 0)
    table = jnp.zeros((EDGE, LANES), jnp.float32)
    for j, (l, r) in enumerate(((0, 0), (0, 1), (1, 1), (1, 2), (2, 2), (2, 3))):
        product = (diagonal * basis[l]) * basis[r]
        line = jnp.sum(product.reshape(ROWS // EDGE, EDGE, LANES), axis=0)
        line = jnp.sum(line, axis=0, keepdims=True)
        table = jnp.where(sub == j, line, table)
    table = jnp.sum(table, axis=1, keepdims=True)
    message = jnp.sum(jnp.where(sub == lanes_e, table, 0.0), axis=0, keepdims=True)
    vec[0:1, :] = message
    mine1 = lon_x * NLAT + lat
    sums1[pl.ds(mine1, 1), :] = message
    spread(vec.at[0:1, :], sums1.at[pl.ds(mine1, 1), :], 2, near)

    @pl.when(is_top)
    def _():
        spread(own3, foldz.at[lon_z], 1, far)

    to_east3.wait_recv()
    to_west3.wait_recv()

    @pl.when(not_low)
    def _():
        to_north3.wait_recv()

    @pl.when(not_top)
    def _():
        to_south3.wait_recv()

    def update(low, rows, parts):
        lane = lane_iota(rows)
        part = slice(low, low + rows)
        wet = wbuf[part, :].astype(jnp.float32)
        joined = jnp.where((lane & 2) == 0, wide3[0, part, :], wide3[1, part, :])
        below = jnp.zeros((rows + 2 * EDGE, LANES), jnp.float32)
        below_side = jnp.zeros((rows, LANES), jnp.float32)
        mid = slice(EDGE, EDGE + rows)
        for k in range(LEVELS):
            span = spans[k]
            u = uv[0, k, part, :]
            w = uv[1, k, part, :]
            sides = []
            for f in range(2):
                side = pltpu.roll(joined, LANES - (SPAN3 * (f * LEVELS + k) + 2), 1)
                sides.append(side)
                at = EDGE + low
                c = ts[f, k, at:at + rows, :]
                e1 = pltpu.roll(jnp.where(lane == 0, side, c), LANES - 1, 1)
                e2 = pltpu.roll(jnp.where(lane < 2, side, c), LANES - 2, 1)
                w1 = pltpu.roll(jnp.where(lane == LANES - 1, side, c), 1, 1)
                w2 = pltpu.roll(jnp.where(lane >= LANES - 2, side, c), 2, 1)
                n1 = ts[f, k, at + 1:at + rows + 1, :]
                n2 = ts[f, k, at + 2:at + rows + 2, :]
                s1 = ts[f, k, at - 1:at + rows - 1, :]
                s2 = ts[f, k, at - 2:at + rows - 2, :]
                grad_e = (8.0 * (e1 - w1) - (e2 - w2)) * (1.0 / 12.0)
                grad_n = (8.0 * (n1 - s1) - (n2 - s2)) * (1.0 / 12.0)
                laplace = e1 + w1 + n1 + s1 - 4.0 * c
                out = (nt, ns)[f]
                out[k, part, :] = c + wet * (-0.1 * (u * grad_e + w * grad_n) + 0.1 * laplace)
            reach = slice(low, low + rows + 2 * EDGE)
            layer = density(ts[0, k, reach, :], ts[1, k, reach, :]) * span
            level = below + 0.5 * layer
            below = below + layer
            p_n = pltpu.roll(level, rows + 2 * EDGE - 1, 0)[mid]
            p_s = pltpu.roll(level, 1, 0)[mid]
            nv[k, part, :] = wet * (w - 0.05 * (p_n - p_s))
            if parts > 1:
                layer_side = density(sides[0], sides[1]) * span
                level_side = below_side + 0.5 * layer_side
                below_side = below_side + layer_side
                centre = level[mid]
                p_e = pltpu.roll(jnp.where(lane == 0, level_side, centre), LANES - 1, 1)
                p_w = pltpu.roll(jnp.where(lane == LANES - 1, level_side, centre), 1, 1)
                nu[k, part, :] = wet * (u - 0.05 * (p_e - p_w))

    update(0, ROWS, 2)

    settle(sums1.at[0:NX * NLAT - 1, :], group_recv.at[2])
    total = jnp.sum(sums1[...], axis=0, keepdims=True)
    mine2 = lon_z
    vec[EDGE:EDGE + 1, :] = total
    sums2[pl.ds(mine2, 1), :] = total
    spread(vec.at[EDGE:EDGE + 1, :], sums2.at[pl.ds(mine2, 1), :], 3, far)

    beside = [(lon - lon_x + lax.rem(lon_x + k, NX), lat) for k in range(1, NX)]
    kept = lane_iota(FOLD3) <= offset

    @pl.when(is_top)
    def _():
        settle(foldz.at[0:NZ - 1], group_recv.at[1])
        base_slot = slot + lon_x + NLON
        row_0 = lax.div(lax.rem(base_slot - (slot & (NX - 1)), NLON), NX)
        row_1 = lax.div(lax.rem(base_slot - 1 - ((slot + NX - 1) & (NX - 1)), NLON), NX)
        joint = jnp.where(kept, foldz[row_0], foldz[row_1])
        own3x[...] = joint
        foldx[lon_x] = joint
        spread(own3x, foldx.at[lon_x], 4, beside)

    settle(sums2.at[0:NZ - 1, :], group_recv.at[3])
    total = jnp.sum(sums2[...], axis=0, keepdims=True)
    mu = [total[:, j:j + 1] for j in range(6)]

    def gram(a, b, shift):
        out = None
        for i, ai in enumerate(a):
            for j, bj in enumerate(b):
                term = ai * bj * mu[i + j + shift]
                out = term if out is None else out + term
        return out

    one = jnp.ones((1, 1), jnp.float32)
    res, dire, sol = [one], [one], [0.0 * one] * 3
    rz = mu[0]
    for step in range(3):
        alpha = rz / (gram(dire, dire, 0) - gram(dire, dire, 1))
        sol = [sol[i] + alpha * dire[i] if i < len(dire) else sol[i] for i in range(3)]
        if step < 2:
            image = [
                (dire[i] if i < len(dire) else 0.0) - (dire[i - 1] if i else 0.0) for i in range(len(dire) + 1)
            ]
            res = [(res[i] if i < len(res) else 0.0) - alpha * image[i] for i in range(len(image))]
            new = gram(res, res, 0)
            beta = new / rz
            dire = [res[i] + (beta * dire[i] if i < len(dire) else 0.0) for i in range(len(res))]
            rz = new
    surf[...] = sol[0] * press[0, own, :] + sol[1] * press[1, own, :] + sol[2] * press[2, own, :]

    @pl.when(is_top)
    def _():
        settle(foldx.at[0:NX - 1], group_recv.at[4])
        side_0 = slot & (NX - 1)
        side_1 = (slot + NX - 1) & (NX - 1)
        for tile in range(FOLD3 // EDGE):
            part = slice(EDGE * tile, EDGE * (tile + 1))
            turned = turn(jnp.where(kept[part], foldx[side_0, part, :], foldx[side_1, part, :]))
            for i in range(EDGE):
                q, r = (EDGE * tile + i) // 2, (EDGE * tile + i) % 2
                ts[q // LEVELS, q % LEVELS, EDGE + ROWS + 1 - r:EDGE + ROWS + 2 - r, :] = turned[i:i + 1]
        update(ROWS - EDGE, EDGE, 1)

    to_east.wait_send()
    to_west.wait_send()
    to_east3.wait_send()
    to_west3.wait_send()

    @pl.when(not_top)
    def _():
        for send in north_sends:
            send.wait_send()
        to_north3.wait_send()

    @pl.when(not_low)
    def _():
        for send in south_sends:
            send.wait_send()
        to_south3.wait_send()

    @pl.when(is_top)
    def _():
        settle(fold2.at[0:NLON - 1, 0:FOLD2, :], group_send.at[0])
        settle(foldz.at[0:NZ - 1], group_send.at[1])
        settle(foldx.at[0:NX - 1], group_send.at[4])

    settle(sums1.at[0:NX * NLAT - 1, :], group_send.at[2])
    settle(sums2.at[0:NZ - 1, :], group_send.at[3])


def store(*refs):
    ins, outs, sem = refs[:5], refs[5:10], refs[10]
    copies = [pltpu.make_async_copy(i, o, sem.at[n]) for n, (i, o) in enumerate(zip(ins, outs))]
    for c in copies:
        c.start()
    for c in copies:
        c.wait()


def body(t, s, u, v, spans, water, opp, weights, anomaly):
    t, s, u, v, water, weights, anomaly, spans, opp = (
        pltpu.with_memory_space_constraint(r, pltpu.HBM) for r in (t, s, u, v, water, weights, anomaly, spans, opp)
    )
    hbm = pl.BlockSpec(memory_space=pltpu.HBM)
    smem = pl.BlockSpec(memory_space=pltpu.SMEM)
    vmem = pl.BlockSpec(memory_space=pltpu.VMEM)
    f32 = jnp.float32
    shapes = [jax.ShapeDtypeStruct((LEVELS, ROWS, LANES), f32)] * 4 + [jax.ShapeDtypeStruct((ROWS, LANES), f32)]
    full = ROWS + 2 * EDGE
    results = pl.pallas_call(
        kernel,
        out_shape=shapes,
        in_specs=[hbm] * 7 + [smem] * 2,
        out_specs=[vmem] * 5,
        scratch_shapes=[
            pltpu.VMEM((2, LEVELS, full, LANES), f32),
            pltpu.VMEM((2, LEVELS, ROWS, LANES), f32),
            pltpu.VMEM((ROWS, LANES), jnp.int32),
            pltpu.VMEM((2, ROWS, LANES), f32),
            pltpu.VMEM((5, 2, full, LANES), f32),
            pltpu.VMEM((ROWS, LANES), f32),
            pltpu.VMEM((2, full, LANES), f32),
            pltpu.VMEM((ROWS, LANES), f32),
            pltpu.VMEM((2, ROWS, LANES), f32),
            pltpu.VMEM((16, LANES), f32),
            pltpu.VMEM((NLON, 16, LANES), f32),
            pltpu.VMEM((FOLD3, LANES), f32),
            pltpu.VMEM((NZ, FOLD3, LANES), f32),
            pltpu.VMEM((FOLD3, LANES), f32),
            pltpu.VMEM((NX, FOLD3, LANES), f32),
            pltpu.VMEM((3, full, LANES), f32),
            pltpu.VMEM((2 * EDGE, LANES), f32),
            pltpu.VMEM((NX * NLAT, LANES), f32),
            pltpu.VMEM((NZ, LANES), f32),
            pltpu.SemaphoreType.DMA((7,)),
            pltpu.SemaphoreType.DMA((12,)),
            pltpu.SemaphoreType.DMA((12,)),
            pltpu.SemaphoreType.DMA((5,)),
            pltpu.SemaphoreType.DMA((5,)),
        ],
        compiler_params=pltpu.CompilerParams(
            collective_id=0, has_side_effects=True, vmem_limit_bytes=40 * 1024 * 1024
        ),
    )(t, s, u, v, water, weights, anomaly, spans, opp)
    anyspec = pl.BlockSpec(memory_space=pl.ANY)
    return pl.pallas_call(
        store,
        out_shape=shapes,
        in_specs=[anyspec] * 5,
        out_specs=[anyspec] * 5,
        scratch_shapes=[pltpu.SemaphoreType.DMA((5,))],
        compiler_params=pltpu.CompilerParams(vmem_limit_bytes=8 * 1024 * 1024),
    )(*results)


def solution(mesh):
    deep = P(None, "lat", "lon")
    flat = P("lat", "lon")
    return jax.shard_map(
        body,
        mesh=mesh,
        in_specs=(deep, deep, deep, deep, P(), flat, P("lon"), flat, flat),
        out_specs=(deep, deep, deep, deep, flat),
        check_vma=False,
    )
```

```python
import itertools

import jax
import jax.numpy as jnp
from jax import lax
from jax.experimental import pallas as pl
from jax.experimental.pallas import tpu as pltpu
from jax.sharding import PartitionSpec as P

MESH = pl.DeviceIdType.MESH
LEVELS = 10
ROWS = 64
LANES = 128
EDGE = 8
NLON = 32
NLAT = 8
NX = 4
NZ = 8
SPAN2 = 10
SPAN3 = 4
FOLD2 = 13
FOLD3 = 4 * LEVELS


def density(t, s):
    return -t - 0.15 * t * t + 0.8 * s - 0.2 * t * s


def lane_iota(rows):
    return lax.broadcasted_iota(jnp.int32, (rows, LANES), 1)


def kernel(
    t_hbm, s_hbm, u_hbm, v_hbm, w_hbm, e_hbm, a_hbm, spans_hbm, opp_hbm,
    nt, ns, nu, nv, surf,
    ts, uv, wbuf, ebuf, x, pack, slim, heard, wide, pack3, wide3, own2, fold2, own3, foldz, own3x, foldx, press, vec, sums1, sums2,
    spans, opp, in_sem, side_send, side_recv, group_send, group_recv,
):
    lon = lax.axis_index("lon")
    lat = lax.axis_index("lat")
    lon_x = lax.rem(lon, NX)
    lon_z = lax.div(lon, NX)
    east = lax.rem(lon + 1, NLON)
    west = lax.rem(lon + NLON - 1, NLON)
    is_top = lat == NLAT - 1
    is_low = lat == 0
    not_top = lat < NLAT - 1
    not_low = lat > 0

    barrier = pltpu.get_barrier_semaphore()

    def greet(dev):
        pl.semaphore_signal(barrier, inc=1, device_id=dev, device_id_type=MESH)

    def hops(step, size):
        return min(step, size - step)

    lat_y = lax.div(lat, 2)
    lat_c = lat & 1
    zs = [((lon_z + d) & (NZ - 1)) * NX for d in range(NZ)]
    xs = [(lon_x + d) & (NX - 1) for d in range(NX)]
    lats = {(dy, dc): ((lat_y + dy) & (NLAT // 2 - 1)) * 2 + (lat_c ^ dc) for dy in range(NLAT // 2) for dc in range(2)}

    def at(dz, dx, dy, dc):
        return (zs[dz] + xs[dx], lats[dy, dc])

    near = [
        at(0, dx, dy, dc)
        for dx, dy, dc in sorted(
            itertools.product(range(NX), range(NLAT // 2), range(2)),
            key=lambda o: -hops(o[0], NX) - hops(o[1], NLAT // 2) - 0.5 * o[2],
        )
        if dx or dy or dc
    ]
    far = [at(dz, 0, 0, 0) for dz in sorted(range(1, NZ), key=lambda o: -hops(o, NZ))]
    ring = [
        at(dz, dx, 0, 0)
        for dz, dx in sorted(
            itertools.product(range(NZ), range(NX)), key=lambda o: -hops(o[0], NZ) - hops(o[1], NX)
        )
        if dz or dx
    ]

    @pl.when(is_top)
    def _():
        for dev in ring:
            greet(dev)

    for dev in far + near + [(east, lat), (west, lat)]:
        greet(dev)

    @pl.when(not_top)
    def _():
        greet((east, lat + 1))
        greet((west, lat + 1))

    @pl.when(not_low)
    def _():
        greet((east, lat - 1))
        greet((west, lat - 1))

    loads = [
        pltpu.make_async_copy(w_hbm, wbuf, in_sem.at[0]),
        pltpu.make_async_copy(e_hbm, ebuf.at[0], in_sem.at[1]),
        pltpu.make_async_copy(a_hbm, ebuf.at[1], in_sem.at[2]),
        pltpu.make_async_copy(t_hbm, ts.at[0, :, EDGE:EDGE + ROWS, :], in_sem.at[3]),
        pltpu.make_async_copy(s_hbm, ts.at[1, :, EDGE:EDGE + ROWS, :], in_sem.at[4]),
        pltpu.make_async_copy(u_hbm, uv.at[0], in_sem.at[5]),
        pltpu.make_async_copy(v_hbm, uv.at[1], in_sem.at[6]),
        pltpu.make_async_copy(spans_hbm, spans, in_sem.at[7]),
        pltpu.make_async_copy(opp_hbm, opp, in_sem.at[8]),
    ]
    for load in loads:
        load.start()

    for load in loads[:3]:
        load.wait()
    own = slice(EDGE, EDGE + ROWS)
    weights = ebuf[0]
    diagonal = 4.0 + weights
    wetness = wbuf[...].astype(jnp.float32)
    scale = wetness / diagonal
    x[3, 0, own, :] = scale
    x[4, 0, own, :] = scale * (weights * ebuf[1])

    for load in loads[3:]:
        load.wait()
    zero = jnp.zeros((ROWS, LANES), jnp.float32)
    below, press_sum, east_sum, north_sum = zero, zero, zero, zero
    for k in range(LEVELS):
        span = spans[k]
        layer = density(ts[0, k, own, :], ts[1, k, own, :]) * span
        press_sum = press_sum + span * (below + 0.5 * layer)
        below = below + layer
        east_sum = east_sum + span * uv[0, k]
        north_sum = north_sum + span * uv[1, k]
    x[0, 0, own, :] = press_sum
    x[1, 0, own, :] = east_sum
    x[2, 0, own, :] = north_sum

    lanes = lane_iota(ROWS)
    packed = zero
    for f in range(5):
        moved = pltpu.roll(x[f, 0, own, :], SPAN2 * f + 5, 1)
        packed = jnp.where((lanes >= SPAN2 * f) & (lanes < SPAN2 * (f + 1)), moved, packed)
    pack[...] = packed
    half = ROWS // 2
    quarter = ROWS // 4
    lanes_h = lane_iota(half)
    lanes_q = lane_iota(quarter)
    eastern = lax.rem(lanes_h, SPAN2) < 5
    for side, turned in ((0, SPAN2 - 5), (1, LANES - 5)):
        lower = pltpu.roll(packed[half:], turned, 1)
        folded = jnp.where(eastern, packed[:half], lower) if side == 0 else jnp.where(eastern, lower, packed[:half])
        slim[side] = jnp.where(lanes_q < LANES // 2, folded[:quarter], pltpu.roll(folded[quarter:], LANES // 2, 1))
    packed = zero
    for q in range(2 * LEVELS):
        moved = pltpu.roll(ts[q // LEVELS, q % LEVELS, own, :], SPAN3 * q + 2, 1)
        packed = jnp.where((lanes >= SPAN3 * q) & (lanes < SPAN3 * (q + 1)), moved, packed)
    outer = (lanes_h & 2) == 0
    pack3[0] = jnp.where(outer, packed[:half], pltpu.roll(packed[half:], 2, 1))
    pack3[1] = jnp.where(outer, pltpu.roll(packed[half:], LANES - 2, 1), packed[:half])

    @pl.when(is_top)
    def _():
        last = EDGE + ROWS - 1
        up = x[0, 0, last - 2:last + 1, :]
        down = x[0, 0, last - 4:last - 1, :]
        inner = slice(last - 3, last)
        flow = jnp.where(x[3, 0, inner, :] > 0.0, x[2, 0, inner, :] - 0.05 * (up - down), 0.0)
        for r in range(3):
            row = last - r
            own2[r:r + 1, :] = x[0, 0, row:row + 1, :]
            own2[3 + r:4 + r, :] = -x[1, 0, row:row + 1, :]
            half = 0.5 * x[3, 0, row:row + 1, :]
            own2[7 + r:8 + r, :] = x[3, 0, row:row + 1, :]
            inside = flow[2 - r:3 - r] if r < 2 else flow[0:1] - flow[2:3]
            own2[10 + r:11 + r, :] = x[4, 0, row:row + 1, :] + half * inside
        own2[6:7, :] = -x[2, 0, last:last + 1, :]
        fold2[lon, 0:FOLD2, :] = own2[0:FOLD2, :]
        for q in range(2 * LEVELS):
            own3[2 * q:2 * q + 2, :] = ts[q // LEVELS, q % LEVELS, EDGE + ROWS - 2:EDGE + ROWS, :]
        foldz[lon_z] = own3[...]
        for f in range(5):
            x[f, 0, EDGE + ROWS:, :] = jnp.zeros((EDGE, LANES), jnp.float32)

    @pl.when(is_low)
    def _():
        for f in range(5):
            x[f, 0, 0:EDGE, :] = jnp.zeros((EDGE, LANES), jnp.float32)
        for q in range(2 * LEVELS):
            ts[q // LEVELS, q % LEVELS, 0:EDGE, :] = jnp.zeros((EDGE, LANES), jnp.float32)

    base = 31 + 7 + 2

    @pl.when(is_top)
    def _():
        pl.semaphore_wait(barrier, base + 2 + NLON - 1)

    @pl.when(is_low)
    def _():
        pl.semaphore_wait(barrier, base + 2)

    @pl.when(not_top & not_low)
    def _():
        pl.semaphore_wait(barrier, base + 4)

    def copy(src, dst, sem, dev):
        return pltpu.make_async_remote_copy(
            src_ref=src, dst_ref=dst, send_sem=side_send.at[sem], recv_sem=side_recv.at[sem],
            device_id=dev, device_id_type=MESH,
        )

    top_rows = slice(EDGE + ROWS, EDGE + ROWS + EDGE)
    to_east = copy(slim.at[0], heard.at[0], 0, (east, lat))
    to_west = copy(slim.at[1], heard.at[1], 1, (west, lat))
    to_north = copy(x.at[:, 0, ROWS:EDGE + ROWS, :], x.at[:, 0, 0:EDGE, :], 2, (lon, lat + 1))
    to_ne = copy(pack.at[ROWS - EDGE:ROWS, :], wide.at[0, 0], 3, (east, lat + 1))
    to_nw = copy(pack.at[ROWS - EDGE:ROWS, :], wide.at[1, 0], 4, (west, lat + 1))
    to_south = copy(x.at[:, 0, EDGE:2 * EDGE, :], x.at[:, 0, top_rows, :], 5, (lon, lat - 1))
    to_se = copy(pack.at[0:EDGE, :], wide.at[0, 1], 6, (east, lat - 1))
    to_sw = copy(pack.at[0:EDGE, :], wide.at[1, 1], 7, (west, lat - 1))
    to_east3 = copy(pack3.at[0], wide3.at[0], 8, (east, lat))
    to_west3 = copy(pack3.at[1], wide3.at[1], 9, (west, lat))
    to_north3 = copy(
        ts.at[:, :, EDGE + ROWS - 2:EDGE + ROWS, :], ts.at[:, :, EDGE - 2:EDGE, :], 10, (lon, lat + 1)
    )
    to_south3 = copy(
        ts.at[:, :, EDGE:EDGE + 2, :], ts.at[:, :, EDGE + ROWS:EDGE + ROWS + 2, :], 11, (lon, lat - 1)
    )
    north_sends = (to_north, to_ne, to_nw)
    south_sends = (to_south, to_se, to_sw)

    def spread(src, dst, sem, devs):
        for dev in devs:
            pltpu.make_async_remote_copy(
                src_ref=src, dst_ref=dst, send_sem=group_send.at[sem], recv_sem=group_recv.at[sem],
                device_id=dev, device_id_type=MESH,
            ).start()

    def settle(ref, sem):
        pltpu.make_async_copy(ref, ref, sem).wait()

    @pl.when(is_top)
    def _():
        spread(own2.at[0:FOLD2, :], fold2.at[lon, 0:FOLD2, :], 0, ring)

    to_east.start()
    to_west.start()

    @pl.when(not_top)
    def _():
        for send in north_sends:
            send.start()

    @pl.when(not_low)
    def _():
        for send in south_sends:
            send.start()

    to_east3.start()
    to_west3.start()

    @pl.when(not_top)
    def _():
        to_north3.start()

    @pl.when(not_low)
    def _():
        to_south3.start()

    to_east.wait_recv()
    to_west.wait_recv()

    @pl.when(not_low)
    def _():
        for send in north_sends:
            send.wait_recv()

    @pl.when(not_top)
    def _():
        for send in south_sends:
            send.wait_recv()

    lanes_w = lane_iota(EDGE + ROWS + EDGE)
    from_west, from_east = (
        jnp.concatenate([heard[side], pltpu.roll(heard[side], LANES // 2, 1)], axis=0) for side in range(2)
    )
    upper = jnp.where(eastern, from_west, from_east)
    lower = jnp.where(eastern, pltpu.roll(from_west, LANES - 5, 1), pltpu.roll(from_east, 5, 1))
    eastern_e = lax.rem(lane_iota(EDGE), SPAN2) < 5
    corners = [jnp.where(eastern_e, wide[0, c], wide[1, c]) for c in range(2)]
    merged = jnp.concatenate([corners[0], upper, lower, corners[1]], axis=0)
    for f in range(5):
        x[f, 1] = pltpu.roll(merged, LANES - (SPAN2 * f + 5), 1)

    @pl.when(is_low)
    def _():
        for f in range(5):
            x[f, 1, 0:EDGE, :] = jnp.zeros((EDGE, LANES), jnp.float32)

    lanes_e = lane_iota(EDGE)
    first = opp[0]
    slot = lax.div(first, LANES)
    offset = first - slot * LANES
    slot_p = lax.rem(slot + 1, NLON)
    slot_m = lax.rem(slot + NLON - 1, NLON)
    slot_mm = lax.rem(slot + NLON - 2, NLON)
    index = (offset - lanes_e) & (LANES - 1)

    def turn(tile):
        return jnp.take_along_axis(tile, index, axis=1)

    @pl.when(is_top)
    def _():
        settle(fold2.at[0:NLON - 1, 0:FOLD2, :], group_recv.at[0])
        kept = lanes_e <= offset
        near_half = index < LANES // 2
        mine, aside = [], []
        for tile in range(2):
            part = slice(EDGE * tile, EDGE * (tile + 1))
            b_p, b_0, b_m, b_mm = (fold2[s, part, :] for s in (slot_p, slot, slot_m, slot_mm))
            mine.append(turn(jnp.where(kept, b_0, b_m)))
            right = jnp.where(kept, b_m, b_mm)
            left = jnp.where(kept, b_p, b_0)
            aside.append(turn(jnp.where(near_half, right, left)))
        for half, tiles in ((0, mine), (1, aside)):
            north = EDGE + ROWS
            x[0, half, north:north + 3, :] = tiles[0][0:3]
            x[1, half, north:north + 3, :] = tiles[0][3:6]
            x[2, half, north:north + 1, :] = tiles[0][6:7]
            x[3, half, north:north + 1, :] = tiles[0][7:8]
            x[3, half, north + 1:north + 3, :] = tiles[1][0:2]
            x[4, half, north:north + 3, :] = tiles[1][2:5]

    full = EDGE + ROWS + EDGE
    first_lane = lanes_w == 0
    last_lane = lanes_w == LANES - 1

    def plus_east(a, b):
        return (
            pltpu.roll(jnp.where(first_lane, b, a), LANES - 1, 1),
            pltpu.roll(jnp.where(first_lane, a, b), LANES - 1, 1),
        )

    def plus_west(a, b):
        return (
            pltpu.roll(jnp.where(last_lane, b, a), 1, 1),
            pltpu.roll(jnp.where(last_lane, a, b), 1, 1),
        )

    def north_of(a):
        return pltpu.roll(a, full - 1, 0)

    def south_of(a):
        return pltpu.roll(a, 1, 0)

    scale2 = (x[3, 0], x[3, 1])
    wet2 = (scale2[0] > 0.0, scale2[1] > 0.0)
    q2 = (x[0, 0], x[0, 1])
    q_e = plus_east(*q2)
    q_w = plus_west(*q2)
    flow_e, flow_n = [], []
    rows_w = lax.broadcasted_iota(jnp.int32, (full, LANES), 0)
    rows_end = jnp.where(is_top, EDGE + ROWS, full)
    for h in range(2):
        flow_e.append(jnp.where(wet2[h], x[1, h] - 0.05 * (q_e[h] - q_w[h]), 0.0))
        flow_n.append(jnp.where(wet2[h] & (rows_w <= rows_end), x[2, h] - 0.05 * (north_of(q2[h]) - south_of(q2[h])), 0.0))
    f_e = plus_east(*flow_e)
    f_w = plus_west(*flow_e)
    basis = []
    v = tuple(
        x[4, h] - scale2[h] * (0.5 * (f_e[h] - f_w[h] + north_of(flow_n[h]) - south_of(flow_n[h])))
        for h in range(2)
    )
    basis.append(v[0][EDGE:EDGE + ROWS])
    for _ in range(3):
        v_e = plus_east(*v)
        v_w = plus_west(*v)
        v = tuple(scale2[h] * (v_e[h] + v_w[h] + north_of(v[h]) + south_of(v[h])) for h in range(2))
        basis.append(v[0][EDGE:EDGE + ROWS])

    for i in range(3):
        press[i, own, :] = basis[i]
    sub = lax.broadcasted_iota(jnp.int32, (EDGE, LANES), 0)
    table = jnp.zeros((EDGE, LANES), jnp.float32)
    for j, (l, r) in enumerate(((0, 0), (0, 1), (1, 1), (1, 2), (2, 2), (2, 3))):
        product = (diagonal * basis[l]) * basis[r]
        line = jnp.sum(product.reshape(ROWS // EDGE, EDGE, LANES), axis=0)
        line = jnp.sum(line, axis=0, keepdims=True)
        table = jnp.where(sub == j, line, table)
    table = jnp.sum(table, axis=1, keepdims=True)
    message = jnp.sum(jnp.where(sub == lanes_e, table, 0.0), axis=0, keepdims=True)
    vec[0:1, :] = message
    mine1 = lon_x * NLAT + lat
    sums1[pl.ds(mine1, 1), :] = message
    spread(vec.at[0:1, :], sums1.at[pl.ds(mine1, 1), :], 2, near)

    @pl.when(is_top)
    def _():
        spread(own3, foldz.at[lon_z], 1, far)

    to_east3.wait_recv()
    to_west3.wait_recv()

    @pl.when(not_low)
    def _():
        to_north3.wait_recv()

    @pl.when(not_top)
    def _():
        to_south3.wait_recv()

    def update(low, rows, parts):
        lane = lane_iota(rows)
        part = slice(low, low + rows)
        wet = wbuf[part, :].astype(jnp.float32)
        rows_3 = []
        if low < ROWS // 2:
            rows_3.append(jnp.where(outer, wide3[0], wide3[1]))
        cut = max(low - ROWS // 2, 0)
        low_w = pltpu.roll(wide3[0, cut:, :], LANES - 2, 1)
        low_e = pltpu.roll(wide3[1, cut:, :], 2, 1)
        rows_3.append(jnp.where(outer[cut:], low_w, low_e))
        joined = jnp.concatenate(rows_3, axis=0)
        below = jnp.zeros((rows + 2 * EDGE, LANES), jnp.float32)
        below_side = jnp.zeros((rows, LANES), jnp.float32)
        mid = slice(EDGE, EDGE + rows)
        for k in range(LEVELS):
            span = spans[k]
            u = uv[0, k, part, :]
            w = uv[1, k, part, :]
            sides = []
            for f in range(2):
                side = pltpu.roll(joined, LANES - (SPAN3 * (f * LEVELS + k) + 2), 1)
                sides.append(side)
                at = EDGE + low
                c = ts[f, k, at:at + rows, :]
                e1 = pltpu.roll(jnp.where(lane == 0, side, c), LANES - 1, 1)
                e2 = pltpu.roll(jnp.where(lane < 2, side, c), LANES - 2, 1)
                w1 = pltpu.roll(jnp.where(lane == LANES - 1, side, c), 1, 1)
                w2 = pltpu.roll(jnp.where(lane >= LANES - 2, side, c), 2, 1)
                n1 = ts[f, k, at + 1:at + rows + 1, :]
                n2 = ts[f, k, at + 2:at + rows + 2, :]
                s1 = ts[f, k, at - 1:at + rows - 1, :]
                s2 = ts[f, k, at - 2:at + rows - 2, :]
                grad_e = (8.0 * (e1 - w1) - (e2 - w2)) * (1.0 / 12.0)
                grad_n = (8.0 * (n1 - s1) - (n2 - s2)) * (1.0 / 12.0)
                laplace = e1 + w1 + n1 + s1 - 4.0 * c
                out = (nt, ns)[f]
                out[k, part, :] = c + wet * (-0.1 * (u * grad_e + w * grad_n) + 0.1 * laplace)
            reach = slice(low, low + rows + 2 * EDGE)
            layer = density(ts[0, k, reach, :], ts[1, k, reach, :]) * span
            level = below + 0.5 * layer
            below = below + layer
            p_n = pltpu.roll(level, rows + 2 * EDGE - 1, 0)[mid]
            p_s = pltpu.roll(level, 1, 0)[mid]
            nv[k, part, :] = wet * (w - 0.05 * (p_n - p_s))
            if parts > 1:
                layer_side = density(sides[0], sides[1]) * span
                level_side = below_side + 0.5 * layer_side
                below_side = below_side + layer_side
                centre = level[mid]
                p_e = pltpu.roll(jnp.where(lane == 0, level_side, centre), LANES - 1, 1)
                p_w = pltpu.roll(jnp.where(lane == LANES - 1, level_side, centre), 1, 1)
                nu[k, part, :] = wet * (u - 0.05 * (p_e - p_w))

    update(0, ROWS, 2)

    settle(sums1.at[0:NX * NLAT - 1, :], group_recv.at[2])
    total = jnp.sum(sums1[...], axis=0, keepdims=True)
    mine2 = lon_z
    vec[EDGE:EDGE + 1, :] = total
    sums2[pl.ds(mine2, 1), :] = total
    spread(vec.at[EDGE:EDGE + 1, :], sums2.at[pl.ds(mine2, 1), :], 3, far)

    beside = [(lon - lon_x + lax.rem(lon_x + k, NX), lat) for k in range(1, NX)]
    kept = lane_iota(FOLD3) <= offset

    @pl.when(is_top)
    def _():
        settle(foldz.at[0:NZ - 1], group_recv.at[1])
        base_slot = slot + lon_x + NLON
        row_0 = lax.div(lax.rem(base_slot - (slot & (NX - 1)), NLON), NX)
        row_1 = lax.div(lax.rem(base_slot - 1 - ((slot + NX - 1) & (NX - 1)), NLON), NX)
        joint = jnp.where(kept, foldz[row_0], foldz[row_1])
        own3x[...] = joint
        foldx[lon_x] = joint
        spread(own3x, foldx.at[lon_x], 4, beside)

    settle(sums2.at[0:NZ - 1, :], group_recv.at[3])
    total = jnp.sum(sums2[...], axis=0, keepdims=True)
    mu = [total[:, j:j + 1] for j in range(6)]

    def gram(a, b, shift):
        out = None
        for i, ai in enumerate(a):
            for j, bj in enumerate(b):
                term = ai * bj * mu[i + j + shift]
                out = term if out is None else out + term
        return out

    one = jnp.ones((1, 1), jnp.float32)
    res, dire, sol = [one], [one], [0.0 * one] * 3
    rz = mu[0]
    for step in range(3):
        alpha = rz / (gram(dire, dire, 0) - gram(dire, dire, 1))
        sol = [sol[i] + alpha * dire[i] if i < len(dire) else sol[i] for i in range(3)]
        if step < 2:
            image = [
                (dire[i] if i < len(dire) else 0.0) - (dire[i - 1] if i else 0.0) for i in range(len(dire) + 1)
            ]
            res = [(res[i] if i < len(res) else 0.0) - alpha * image[i] for i in range(len(image))]
            new = gram(res, res, 0)
            beta = new / rz
            dire = [res[i] + (beta * dire[i] if i < len(dire) else 0.0) for i in range(len(res))]
            rz = new
    surf[...] = sol[0] * press[0, own, :] + sol[1] * press[1, own, :] + sol[2] * press[2, own, :]

    @pl.when(is_top)
    def _():
        settle(foldx.at[0:NX - 1], group_recv.at[4])
        side_0 = slot & (NX - 1)
        side_1 = (slot + NX - 1) & (NX - 1)
        for tile in range(FOLD3 // EDGE):
            part = slice(EDGE * tile, EDGE * (tile + 1))
            turned = turn(jnp.where(kept[part], foldx[side_0, part, :], foldx[side_1, part, :]))
            for i in range(EDGE):
                q, r = (EDGE * tile + i) // 2, (EDGE * tile + i) % 2
                ts[q // LEVELS, q % LEVELS, EDGE + ROWS + 1 - r:EDGE + ROWS + 2 - r, :] = turned[i:i + 1]
        update(ROWS - EDGE, EDGE, 1)

    to_east.wait_send()
    to_west.wait_send()
    to_east3.wait_send()
    to_west3.wait_send()

    @pl.when(not_top)
    def _():
        for send in north_sends:
            send.wait_send()
        to_north3.wait_send()

    @pl.when(not_low)
    def _():
        for send in south_sends:
            send.wait_send()
        to_south3.wait_send()

    @pl.when(is_top)
    def _():
        settle(fold2.at[0:NLON - 1, 0:FOLD2, :], group_send.at[0])
        settle(foldz.at[0:NZ - 1], group_send.at[1])
        settle(foldx.at[0:NX - 1], group_send.at[4])

    settle(sums1.at[0:NX * NLAT - 1, :], group_send.at[2])
    settle(sums2.at[0:NZ - 1, :], group_send.at[3])


def store(*refs):
    ins, outs, sem = refs[:5], refs[5:10], refs[10]
    copies = [pltpu.make_async_copy(i, o, sem.at[n]) for n, (i, o) in enumerate(zip(ins, outs))]
    for c in copies:
        c.start()
    for c in copies:
        c.wait()


def body(t, s, u, v, spans, water, opp, weights, anomaly):
    t, s, u, v, water, weights, anomaly, spans, opp = (
        pltpu.with_memory_space_constraint(r, pltpu.HBM) for r in (t, s, u, v, water, weights, anomaly, spans, opp)
    )
    hbm = pl.BlockSpec(memory_space=pltpu.HBM)
    vmem = pl.BlockSpec(memory_space=pltpu.VMEM)
    f32 = jnp.float32
    shapes = [jax.ShapeDtypeStruct((LEVELS, ROWS, LANES), f32)] * 4 + [jax.ShapeDtypeStruct((ROWS, LANES), f32)]
    full = ROWS + 2 * EDGE
    results = pl.pallas_call(
        kernel,
        out_shape=shapes,
        in_specs=[hbm] * 9,
        out_specs=[vmem] * 5,
        scratch_shapes=[
            pltpu.VMEM((2, LEVELS, full, LANES), f32),
            pltpu.VMEM((2, LEVELS, ROWS, LANES), f32),
            pltpu.VMEM((ROWS, LANES), jnp.int32),
            pltpu.VMEM((2, ROWS, LANES), f32),
            pltpu.VMEM((5, 2, full, LANES), f32),
            pltpu.VMEM((ROWS, LANES), f32),
            pltpu.VMEM((2, ROWS // 4, LANES), f32),
            pltpu.VMEM((2, ROWS // 4, LANES), f32),
            pltpu.VMEM((2, 2, EDGE, LANES), f32),
            pltpu.VMEM((2, ROWS // 2, LANES), f32),
            pltpu.VMEM((2, ROWS // 2, LANES), f32),
            pltpu.VMEM((16, LANES), f32),
            pltpu.VMEM((NLON, 16, LANES), f32),
            pltpu.VMEM((FOLD3, LANES), f32),
            pltpu.VMEM((NZ, FOLD3, LANES), f32),
            pltpu.VMEM((FOLD3, LANES), f32),
            pltpu.VMEM((NX, FOLD3, LANES), f32),
            pltpu.VMEM((3, full, LANES), f32),
            pltpu.VMEM((2 * EDGE, LANES), f32),
            pltpu.VMEM((NX * NLAT, LANES), f32),
            pltpu.VMEM((NZ, LANES), f32),
            pltpu.SMEM((LEVELS,), f32),
            pltpu.SMEM((LANES,), jnp.int32),
            pltpu.SemaphoreType.DMA((9,)),
            pltpu.SemaphoreType.DMA((12,)),
            pltpu.SemaphoreType.DMA((12,)),
            pltpu.SemaphoreType.DMA((5,)),
            pltpu.SemaphoreType.DMA((5,)),
        ],
        compiler_params=pltpu.CompilerParams(
            collective_id=0, has_side_effects=True, vmem_limit_bytes=40 * 1024 * 1024
        ),
    )(t, s, u, v, water, weights, anomaly, spans, opp)
    anyspec = pl.BlockSpec(memory_space=pl.ANY)
    return pl.pallas_call(
        store,
        out_shape=shapes,
        in_specs=[anyspec] * 5,
        out_specs=[anyspec] * 5,
        scratch_shapes=[pltpu.SemaphoreType.DMA((5,))],
        compiler_params=pltpu.CompilerParams(vmem_limit_bytes=8 * 1024 * 1024),
    )(*results)


def solution(mesh):
    deep = P(None, "lat", "lon")
    flat = P("lat", "lon")
    return jax.shard_map(
        body,
        mesh=mesh,
        in_specs=(deep, deep, deep, deep, P(), flat, P("lon"), flat, flat),
        out_specs=(deep, deep, deep, deep, flat),
        check_vma=False,
    )
```

```python
import itertools

import jax
import jax.numpy as jnp
from jax import lax
from jax.experimental import pallas as pl
from jax.experimental.pallas import tpu as pltpu
from jax.sharding import PartitionSpec as P

MESH = pl.DeviceIdType.MESH
LEVELS = 10
ROWS = 64
LANES = 128
EDGE = 8
NLON = 32
NLAT = 8
NX = 4
NZ = 8
EARLY = 2
SPAN2 = 10
SPAN3 = 4
FOLD2 = 13
FOLD3 = 4 * LEVELS


def density(t, s):
    return -t - 0.15 * t * t + 0.8 * s - 0.2 * t * s


def lane_iota(rows):
    return lax.broadcasted_iota(jnp.int32, (rows, LANES), 1)


def kernel(
    t_hbm, s_hbm, u_hbm, v_hbm, w_hbm, e_hbm, a_hbm, spans_hbm, opp_hbm,
    nt, ns, nu, nv, surf,
    ts, uv, wbuf, ebuf, x, pack, slim, heard, wide, pack3, wide3, own2, fold2, own3, foldz, own3x, foldx, press, rim, vec, sums1, sums2, late1, crown, wide_sent,
    spans, opp, in_sem, side_send, side_recv, group_send, group_recv,
):
    lon = lax.axis_index("lon")
    lat = lax.axis_index("lat")
    lon_x = lax.rem(lon, NX)
    lon_z = lax.div(lon, NX)
    east = lax.rem(lon + 1, NLON)
    west = lax.rem(lon + NLON - 1, NLON)
    is_top = lat == NLAT - 1
    is_low = lat == 0
    not_top = lat < NLAT - 1
    not_low = lat > 0

    barrier = pltpu.get_barrier_semaphore()

    def greet(dev):
        pl.semaphore_signal(barrier, inc=1, device_id=dev, device_id_type=MESH)

    def hops(step, size):
        return min(step, size - step)

    lat_y = lax.div(lat, 2)
    lat_c = lat & 1
    zs = [((lon_z + d) & (NZ - 1)) * NX for d in range(NZ)]
    xs = [(lon_x + d) & (NX - 1) for d in range(NX)]
    lats = {(dy, dc): ((lat_y + dy) & (NLAT // 2 - 1)) * 2 + (lat_c ^ dc) for dy in range(NLAT // 2) for dc in range(2)}

    def at(dz, dx, dy, dc):
        return (zs[dz] + xs[dx], lats[dy, dc])

    near = [
        at(0, dx, dy, dc)
        for dx, dy, dc in sorted(
            itertools.product(range(NX), range(NLAT // 2), range(2)),
            key=lambda o: -hops(o[0], NX) - hops(o[1], NLAT // 2) - 0.5 * o[2],
        )
        if dx or dy or dc
    ]
    far = [at(dz, 0, 0, 0) for dz in sorted(range(1, NZ), key=lambda o: -hops(o, NZ))]
    ring = [
        at(dz, dx, 0, 0)
        for dz, dx in sorted(
            itertools.product(range(NZ), range(NX)), key=lambda o: -hops(o[0], NZ) - hops(o[1], NX)
        )
        if dz or dx
    ]

    is_early = lon_z < EARLY
    crowns = [
        ((zs[dz] + xs[dx], NLAT - 1), dz or dx) for dz, dx in itertools.product(range(NZ), range(NX))
    ]

    @pl.when(is_top)
    def _():
        for dev in ring:
            greet(dev)

    @pl.when(is_early)
    def _():
        for dev, other in crowns:
            if other:
                greet(dev)

    @pl.when(is_early & not_top)
    def _():
        greet((lon, NLAT - 1))

    for dev in far + near + [(east, lat), (west, lat)]:
        greet(dev)

    @pl.when(not_top)
    def _():
        greet((east, lat + 1))
        greet((west, lat + 1))

    @pl.when(not_low)
    def _():
        greet((east, lat - 1))
        greet((west, lat - 1))

    loads = [
        pltpu.make_async_copy(w_hbm, wbuf, in_sem.at[0]),
        pltpu.make_async_copy(e_hbm, ebuf.at[0], in_sem.at[1]),
        pltpu.make_async_copy(a_hbm, ebuf.at[1], in_sem.at[2]),
        pltpu.make_async_copy(t_hbm, ts.at[0, :, EDGE:EDGE + ROWS, :], in_sem.at[3]),
        pltpu.make_async_copy(s_hbm, ts.at[1, :, EDGE:EDGE + ROWS, :], in_sem.at[4]),
        pltpu.make_async_copy(u_hbm, uv.at[0], in_sem.at[5]),
        pltpu.make_async_copy(v_hbm, uv.at[1], in_sem.at[6]),
        pltpu.make_async_copy(spans_hbm, spans, in_sem.at[7]),
        pltpu.make_async_copy(opp_hbm, opp, in_sem.at[8]),
    ]
    for load in loads:
        load.start()

    for load in loads[:3]:
        load.wait()
    own = slice(EDGE, EDGE + ROWS)
    weights = ebuf[0]
    diagonal = 4.0 + weights
    wetness = wbuf[...].astype(jnp.float32)
    scale = wetness / diagonal
    x[3, 0, own, :] = scale
    x[4, 0, own, :] = scale * (weights * ebuf[1])

    for load in loads[3:]:
        load.wait()
    zero = jnp.zeros((ROWS, LANES), jnp.float32)
    below, press_sum, east_sum, north_sum = zero, zero, zero, zero
    for k in range(LEVELS):
        span = spans[k]
        layer = density(ts[0, k, own, :], ts[1, k, own, :]) * span
        press_sum = press_sum + span * (below + 0.5 * layer)
        below = below + layer
        east_sum = east_sum + span * uv[0, k]
        north_sum = north_sum + span * uv[1, k]
    x[0, 0, own, :] = press_sum
    x[1, 0, own, :] = east_sum
    x[2, 0, own, :] = north_sum

    lanes = lane_iota(ROWS)
    packed = zero
    for f in range(5):
        moved = pltpu.roll(x[f, 0, own, :], SPAN2 * f + 5, 1)
        packed = jnp.where((lanes >= SPAN2 * f) & (lanes < SPAN2 * (f + 1)), moved, packed)
    pack[...] = packed
    half = ROWS // 2
    quarter = ROWS // 4
    lanes_h = lane_iota(half)
    lanes_q = lane_iota(quarter)
    eastern = lax.rem(lanes_h, SPAN2) < 5
    for side, turned in ((0, SPAN2 - 5), (1, LANES - 5)):
        lower = pltpu.roll(packed[half:], turned, 1)
        folded = jnp.where(eastern, packed[:half], lower) if side == 0 else jnp.where(eastern, lower, packed[:half])
        slim[side] = jnp.where(lanes_q < LANES // 2, folded[:quarter], pltpu.roll(folded[quarter:], LANES // 2, 1))
    packed = zero
    for q in range(2 * LEVELS):
        moved = pltpu.roll(ts[q // LEVELS, q % LEVELS, own, :], SPAN3 * q + 2, 1)
        packed = jnp.where((lanes >= SPAN3 * q) & (lanes < SPAN3 * (q + 1)), moved, packed)
    outer = (lanes_h & 2) == 0
    pack3[0] = jnp.where(outer, packed[:half], pltpu.roll(packed[half:], 2, 1))
    pack3[1] = jnp.where(outer, pltpu.roll(packed[half:], LANES - 2, 1), packed[:half])

    @pl.when(is_top)
    def _():
        last = EDGE + ROWS - 1
        up = x[0, 0, last - 2:last + 1, :]
        down = x[0, 0, last - 4:last - 1, :]
        inner = slice(last - 3, last)
        flow = jnp.where(x[3, 0, inner, :] > 0.0, x[2, 0, inner, :] - 0.05 * (up - down), 0.0)
        for r in range(3):
            row = last - r
            own2[r:r + 1, :] = x[0, 0, row:row + 1, :]
            own2[3 + r:4 + r, :] = -x[1, 0, row:row + 1, :]
            half = 0.5 * x[3, 0, row:row + 1, :]
            own2[7 + r:8 + r, :] = x[3, 0, row:row + 1, :]
            inside = flow[2 - r:3 - r] if r < 2 else flow[0:1] - flow[2:3]
            own2[10 + r:11 + r, :] = x[4, 0, row:row + 1, :] + half * inside
        own2[6:7, :] = -x[2, 0, last:last + 1, :]
        fold2[lon, 0:FOLD2, :] = own2[0:FOLD2, :]
        for q in range(2 * LEVELS):
            own3[2 * q:2 * q + 2, :] = ts[q // LEVELS, q % LEVELS, EDGE + ROWS - 2:EDGE + ROWS, :]
        foldz[lon_z] = own3[...]
        for f in range(5):
            x[f, 0, EDGE + ROWS:, :] = jnp.zeros((EDGE, LANES), jnp.float32)

    @pl.when(is_low)
    def _():
        for f in range(5):
            x[f, 0, 0:EDGE, :] = jnp.zeros((EDGE, LANES), jnp.float32)
        for q in range(2 * LEVELS):
            ts[q // LEVELS, q % LEVELS, 0:EDGE, :] = jnp.zeros((EDGE, LANES), jnp.float32)

    base = 31 + 7 + 2

    crowned = base + 2 + NLON - 1 + EARLY * NX * NLAT

    @pl.when(is_top & is_early)
    def _():
        pl.semaphore_wait(barrier, crowned - 1)

    @pl.when(is_top & (lon_z >= EARLY))
    def _():
        pl.semaphore_wait(barrier, crowned)

    @pl.when(is_low)
    def _():
        pl.semaphore_wait(barrier, base + 2)

    @pl.when(not_top & not_low)
    def _():
        pl.semaphore_wait(barrier, base + 4)

    def copy(src, dst, sem, dev):
        return pltpu.make_async_remote_copy(
            src_ref=src, dst_ref=dst, send_sem=side_send.at[sem], recv_sem=side_recv.at[sem],
            device_id=dev, device_id_type=MESH,
        )

    top_rows = slice(EDGE + ROWS, EDGE + ROWS + EDGE)
    to_east = copy(slim.at[0], heard.at[0], 0, (east, lat))
    to_west = copy(slim.at[1], heard.at[1], 1, (west, lat))
    to_north = copy(x.at[:, 0, ROWS:EDGE + ROWS, :], x.at[:, 0, 0:EDGE, :], 2, (lon, lat + 1))
    to_ne = copy(pack.at[ROWS - EDGE:ROWS, :], wide.at[0, 0], 3, (east, lat + 1))
    to_nw = copy(pack.at[ROWS - EDGE:ROWS, :], wide.at[1, 0], 4, (west, lat + 1))
    to_south = copy(x.at[:, 0, EDGE:2 * EDGE, :], x.at[:, 0, top_rows, :], 5, (lon, lat - 1))
    to_se = copy(pack.at[0:EDGE, :], wide.at[0, 1], 6, (east, lat - 1))
    to_sw = copy(pack.at[0:EDGE, :], wide.at[1, 1], 7, (west, lat - 1))
    to_east3 = copy(pack3.at[0], wide3.at[0], 8, (east, lat))
    to_west3 = copy(pack3.at[1], wide3.at[1], 9, (west, lat))
    to_north3 = copy(
        ts.at[:, :, EDGE + ROWS - 2:EDGE + ROWS, :], ts.at[:, :, EDGE - 2:EDGE, :], 10, (lon, lat + 1)
    )
    to_south3 = copy(
        ts.at[:, :, EDGE:EDGE + 2, :], ts.at[:, :, EDGE + ROWS:EDGE + ROWS + 2, :], 11, (lon, lat - 1)
    )
    north_sends = (to_north, to_ne, to_nw)
    south_sends = (to_south, to_se, to_sw)

    def spread(src, dst, sem, devs):
        for dev in devs:
            pltpu.make_async_remote_copy(
                src_ref=src, dst_ref=dst, send_sem=group_send.at[sem], recv_sem=group_recv.at[sem],
                device_id=dev, device_id_type=MESH,
            ).start()

    def settle(ref, sem):
        pltpu.make_async_copy(ref, ref, sem).wait()

    to_east.start()
    to_west.start()

    @pl.when(not_top)
    def _():
        for send in north_sends:
            send.start()

    @pl.when(not_low)
    def _():
        for send in south_sends:
            send.start()

    @pl.when(is_top)
    def _():
        spread(own2.at[0:FOLD2, :], fold2.at[lon, 0:FOLD2, :], 0, ring)

    to_east3.start()
    to_west3.start()

    @pl.when(not_top)
    def _():
        to_north3.start()

    @pl.when(not_low)
    def _():
        to_south3.start()

    to_east.wait_recv()
    to_west.wait_recv()

    @pl.when(not_low)
    def _():
        for send in north_sends:
            send.wait_recv()

    @pl.when(not_top)
    def _():
        for send in south_sends:
            send.wait_recv()

    lanes_w = lane_iota(EDGE + ROWS + EDGE)
    from_west, from_east = (
        jnp.concatenate([heard[side], pltpu.roll(heard[side], LANES // 2, 1)], axis=0) for side in range(2)
    )
    upper = jnp.where(eastern, from_west, from_east)
    lower = jnp.where(eastern, pltpu.roll(from_west, LANES - 5, 1), pltpu.roll(from_east, 5, 1))
    eastern_e = lax.rem(lane_iota(EDGE), SPAN2) < 5
    corners = [jnp.where(eastern_e, wide[0, c], wide[1, c]) for c in range(2)]
    merged = jnp.concatenate([corners[0], upper, lower, corners[1]], axis=0)
    for f in range(5):
        x[f, 1] = pltpu.roll(merged, LANES - (SPAN2 * f + 5), 1)

    @pl.when(is_low)
    def _():
        for f in range(5):
            x[f, 1, 0:EDGE, :] = jnp.zeros((EDGE, LANES), jnp.float32)

    lanes_e = lane_iota(EDGE)
    first = opp[0]
    slot = lax.div(first, LANES)
    offset = first - slot * LANES
    slot_p = lax.rem(slot + 1, NLON)
    slot_m = lax.rem(slot + NLON - 1, NLON)
    slot_mm = lax.rem(slot + NLON - 2, NLON)
    index = (offset - lanes_e) & (LANES - 1)

    def turn(tile):
        return jnp.take_along_axis(tile, index, axis=1)

    full = EDGE + ROWS + EDGE
    rows_end = jnp.where(is_top, EDGE + ROWS, full)
    pairs = ((0, 0), (0, 1), (1, 1), (1, 2), (2, 2), (2, 3))

    def north_of(a):
        return pltpu.roll(a, a.shape[0] - 1, 0)

    def south_of(a):
        return pltpu.roll(a, 1, 0)

    def krylov(low, count):
        lane = lane_iota(count)
        first_lane = lane == 0
        last_lane = lane == LANES - 1
        part = slice(low, low + count)

        def plus_east(a, b):
            return (
                pltpu.roll(jnp.where(first_lane, b, a), LANES - 1, 1),
                pltpu.roll(jnp.where(first_lane, a, b), LANES - 1, 1),
            )

        def plus_west(a, b):
            return (
                pltpu.roll(jnp.where(last_lane, b, a), 1, 1),
                pltpu.roll(jnp.where(last_lane, a, b), 1, 1),
            )

        row = lax.broadcasted_iota(jnp.int32, (count, LANES), 0) + low
        scale2 = (x[3, 0, part, :], x[3, 1, part, :])
        q2 = (x[0, 0, part, :], x[0, 1, part, :])
        q_e = plus_east(*q2)
        q_w = plus_west(*q2)
        flow_e, flow_n = [], []
        for h in range(2):
            wet = scale2[h] > 0.0
            flow_e.append(jnp.where(wet, x[1, h, part, :] - 0.05 * (q_e[h] - q_w[h]), 0.0))
            slope = north_of(q2[h]) - south_of(q2[h])
            flow_n.append(jnp.where(wet & (row <= rows_end), x[2, h, part, :] - 0.05 * slope, 0.0))
        f_e = plus_east(*flow_e)
        f_w = plus_west(*flow_e)
        v = tuple(
            x[4, h, part, :]
            - scale2[h] * (0.5 * (f_e[h] - f_w[h] + north_of(flow_n[h]) - south_of(flow_n[h])))
            for h in range(2)
        )
        basis = [v[0]]
        for _ in range(3):
            v_e = plus_east(*v)
            v_w = plus_west(*v)
            v = tuple(scale2[h] * (v_e[h] + v_w[h] + north_of(v[h]) + south_of(v[h])) for h in range(2))
            basis.append(v[0])
        return basis

    basis = [v[own] for v in krylov(0, full)]
    for i in range(3):
        press[i, own, :] = basis[i]
    bulk = []
    for j, (l, r) in enumerate(pairs):
        product = ((diagonal * basis[l]) * basis[r]).reshape(ROWS // EDGE, EDGE, LANES)
        bulk.append(jnp.sum(product[:-1], axis=0))
        rim[j] = product[-1]

    @pl.when(is_top)
    def _():
        settle(fold2.at[0:NLON - 1, 0:FOLD2, :], group_recv.at[0])
        kept = lanes_e <= offset
        near_half = index < LANES // 2
        mine, aside = [], []
        for tile in range(2):
            part = slice(EDGE * tile, EDGE * (tile + 1))
            b_p, b_0, b_m, b_mm = (fold2[s, part, :] for s in (slot_p, slot, slot_m, slot_mm))
            mine.append(turn(jnp.where(kept, b_0, b_m)))
            right = jnp.where(kept, b_m, b_mm)
            left = jnp.where(kept, b_p, b_0)
            aside.append(turn(jnp.where(near_half, right, left)))
        for half, tiles in ((0, mine), (1, aside)):
            north = EDGE + ROWS
            x[0, half, north:north + 3, :] = tiles[0][0:3]
            x[1, half, north:north + 3, :] = tiles[0][3:6]
            x[2, half, north:north + 1, :] = tiles[0][6:7]
            x[3, half, north:north + 1, :] = tiles[0][7:8]
            x[3, half, north + 1:north + 3, :] = tiles[1][0:2]
            x[4, half, north:north + 3, :] = tiles[1][2:5]
        final = slice(EDGE, 2 * EDGE)
        rim_diagonal = 4.0 + ebuf[0, ROWS - EDGE:, :]
        basis = [v[final] for v in krylov(ROWS - EDGE, 3 * EDGE)]
        for i in range(3):
            press[i, ROWS:ROWS + EDGE, :] = basis[i]
        for j, (l, r) in enumerate(pairs):
            rim[j] = (rim_diagonal * basis[l]) * basis[r]

    sub = lax.broadcasted_iota(jnp.int32, (EDGE, LANES), 0)
    table = jnp.zeros((EDGE, LANES), jnp.float32)
    for j in range(len(pairs)):
        line = jnp.sum(bulk[j] + rim[j], axis=0, keepdims=True)
        table = jnp.where(sub == j, line, table)
    table = jnp.sum(table, axis=1, keepdims=True)
    message = jnp.sum(jnp.where(sub == lanes_e, table, 0.0), axis=0, keepdims=True)
    vec[0:1, :] = message
    mine1 = lon_x * (NLAT - 1) + lat

    @pl.when(not_top)
    def _():
        sums1[pl.ds(mine1, 1), :] = message
        spread(vec.at[0:1, :], sums1.at[pl.ds(mine1, 1), :], 2, near)

    @pl.when(is_top)
    def _():
        late1[pl.ds(lon_x, 1), :] = message
        for dz in range(NZ):
            for dx, dy, dc in itertools.product(range(NX), range(NLAT // 2), range(2)):
                if dz or dx or dy or dc:

                    @pl.when(zs[dz] < EARLY * NX)
                    def _(dev=at(dz, dx, dy, dc)):
                        spread(vec.at[0:1, :], crown.at[pl.ds(lon, 1), :], 5, [dev])

        spread(vec.at[0:1, :], late1.at[pl.ds(lon_x, 1), :], 6, near)

    @pl.when(is_top & is_early)
    def _():
        crown[pl.ds(lon, 1), :] = message

    @pl.when(is_top)
    def _():
        spread(own3, foldz.at[lon_z], 1, far)

    to_east3.wait_recv()
    to_west3.wait_recv()

    @pl.when(not_low)
    def _():
        to_north3.wait_recv()

    @pl.when(not_top)
    def _():
        to_south3.wait_recv()

    def update(low, rows, parts):
        lane = lane_iota(rows)
        part = slice(low, low + rows)
        wet = wbuf[part, :].astype(jnp.float32)
        rows_3 = []
        if low < ROWS // 2:
            rows_3.append(jnp.where(outer, wide3[0], wide3[1]))
        cut = max(low - ROWS // 2, 0)
        low_w = pltpu.roll(wide3[0, cut:, :], LANES - 2, 1)
        low_e = pltpu.roll(wide3[1, cut:, :], 2, 1)
        rows_3.append(jnp.where(outer[cut:], low_w, low_e))
        joined = jnp.concatenate(rows_3, axis=0)
        below = jnp.zeros((rows + 2 * EDGE, LANES), jnp.float32)
        below_side = jnp.zeros((rows, LANES), jnp.float32)
        mid = slice(EDGE, EDGE + rows)
        for k in range(LEVELS):
            span = spans[k]
            u = uv[0, k, part, :]
            w = uv[1, k, part, :]
            sides = []
            for f in range(2):
                side = pltpu.roll(joined, LANES - (SPAN3 * (f * LEVELS + k) + 2), 1)
                sides.append(side)
                at = EDGE + low
                c = ts[f, k, at:at + rows, :]
                e1 = pltpu.roll(jnp.where(lane == 0, side, c), LANES - 1, 1)
                e2 = pltpu.roll(jnp.where(lane < 2, side, c), LANES - 2, 1)
                w1 = pltpu.roll(jnp.where(lane == LANES - 1, side, c), 1, 1)
                w2 = pltpu.roll(jnp.where(lane >= LANES - 2, side, c), 2, 1)
                n1 = ts[f, k, at + 1:at + rows + 1, :]
                n2 = ts[f, k, at + 2:at + rows + 2, :]
                s1 = ts[f, k, at - 1:at + rows - 1, :]
                s2 = ts[f, k, at - 2:at + rows - 2, :]
                grad_e = (8.0 * (e1 - w1) - (e2 - w2)) * (1.0 / 12.0)
                grad_n = (8.0 * (n1 - s1) - (n2 - s2)) * (1.0 / 12.0)
                laplace = e1 + w1 + n1 + s1 - 4.0 * c
                out = (nt, ns)[f]
                out[k, part, :] = c + wet * (-0.1 * (u * grad_e + w * grad_n) + 0.1 * laplace)
            reach = slice(low, low + rows + 2 * EDGE)
            layer = density(ts[0, k, reach, :], ts[1, k, reach, :]) * span
            level = below + 0.5 * layer
            below = below + layer
            p_n = pltpu.roll(level, rows + 2 * EDGE - 1, 0)[mid]
            p_s = pltpu.roll(level, 1, 0)[mid]
            nv[k, part, :] = wet * (w - 0.05 * (p_n - p_s))
            if parts > 1:
                layer_side = density(sides[0], sides[1]) * span
                level_side = below_side + 0.5 * layer_side
                below_side = below_side + layer_side
                centre = level[mid]
                p_e = pltpu.roll(jnp.where(lane == 0, level_side, centre), LANES - 1, 1)
                p_w = pltpu.roll(jnp.where(lane == LANES - 1, level_side, centre), 1, 1)
                nu[k, part, :] = wet * (u - 0.05 * (p_e - p_w))

    update(0, ROWS, 2)

    body_rows = NX * (NLAT - 1)

    @pl.when(is_top)
    def _():
        settle(sums1, group_recv.at[2])

    @pl.when(not_top)
    def _():
        settle(sums1.at[0:body_rows - 1, :], group_recv.at[2])

    total = jnp.sum(sums1[...], axis=0, keepdims=True)
    vec[EDGE:EDGE + 1, :] = total

    @pl.when(is_early)
    def _():
        sums2[pl.ds(lon_z, 1), :] = total

    def cross(row, early):
        for dz in sorted(range(1, NZ), key=lambda o: -hops(o, NZ)):
            bound = EARLY * NX

            @pl.when((zs[dz] < bound) if early else (zs[dz] >= bound))
            def _(dev=at(dz, 0, 0, 0)):
                spread(vec.at[row:row + 1, :], sums2.at[pl.ds(lon_z, 1), :], 3, [dev])

    cross(EDGE, True)

    @pl.when(is_top)
    def _():
        settle(late1.at[0:NX - 1, :], group_recv.at[6])

    @pl.when(not_top)
    def _():
        settle(late1, group_recv.at[6])

    total = total + jnp.sum(late1[...], axis=0, keepdims=True)
    vec[EDGE + 1:EDGE + 2, :] = total

    @pl.when(lon_z >= EARLY)
    def _():
        sums2[pl.ds(lon_z, 1), :] = total

    cross(EDGE + 1, False)

    beside = [(lon - lon_x + lax.rem(lon_x + k, NX), lat) for k in range(1, NX)]
    kept = lane_iota(FOLD3) <= offset

    @pl.when(is_top)
    def _():
        settle(foldz.at[0:NZ - 1], group_recv.at[1])
        base_slot = slot + lon_x + NLON
        row_0 = lax.div(lax.rem(base_slot - (slot & (NX - 1)), NLON), NX)
        row_1 = lax.div(lax.rem(base_slot - 1 - ((slot + NX - 1) & (NX - 1)), NLON), NX)
        joint = jnp.where(kept, foldz[row_0], foldz[row_1])
        own3x[...] = joint
        foldx[lon_x] = joint
        spread(own3x, foldx.at[lon_x], 4, beside)

    settle(sums2.at[0:NZ - 1, :], group_recv.at[3])
    vec[EDGE + 2:EDGE + 3, :] = jnp.sum(sums2[...], axis=0, keepdims=True)

    @pl.when(is_early & is_top)
    def _():
        settle(crown.at[0:NLON - 1, :], group_recv.at[5])

    @pl.when(is_early & not_top)
    def _():
        settle(crown, group_recv.at[5])

    @pl.when(is_early)
    def _():
        vec[EDGE + 2:EDGE + 3, :] = vec[EDGE + 2:EDGE + 3, :] + jnp.sum(crown[...], axis=0, keepdims=True)

    total = vec[EDGE + 2:EDGE + 3, :]
    mu = [total[:, j:j + 1] for j in range(6)]

    def gram(a, b, shift):
        out = None
        for i, ai in enumerate(a):
            for j, bj in enumerate(b):
                term = ai * bj * mu[i + j + shift]
                out = term if out is None else out + term
        return out

    one = jnp.ones((1, 1), jnp.float32)
    res, dire, sol = [one], [one], [0.0 * one] * 3
    rz = mu[0]
    for step in range(3):
        alpha = rz / (gram(dire, dire, 0) - gram(dire, dire, 1))
        sol = [sol[i] + alpha * dire[i] if i < len(dire) else sol[i] for i in range(3)]
        if step < 2:
            image = [
                (dire[i] if i < len(dire) else 0.0) - (dire[i - 1] if i else 0.0) for i in range(len(dire) + 1)
            ]
            res = [(res[i] if i < len(res) else 0.0) - alpha * image[i] for i in range(len(image))]
            new = gram(res, res, 0)
            beta = new / rz
            dire = [res[i] + (beta * dire[i] if i < len(dire) else 0.0) for i in range(len(res))]
            rz = new
    surf[...] = sol[0] * press[0, own, :] + sol[1] * press[1, own, :] + sol[2] * press[2, own, :]

    @pl.when(is_top)
    def _():
        settle(foldx.at[0:NX - 1], group_recv.at[4])
        side_0 = slot & (NX - 1)
        side_1 = (slot + NX - 1) & (NX - 1)
        for tile in range(FOLD3 // EDGE):
            part = slice(EDGE * tile, EDGE * (tile + 1))
            turned = turn(jnp.where(kept[part], foldx[side_0, part, :], foldx[side_1, part, :]))
            for i in range(EDGE):
                q, r = (EDGE * tile + i) // 2, (EDGE * tile + i) % 2
                ts[q // LEVELS, q % LEVELS, EDGE + ROWS + 1 - r:EDGE + ROWS + 2 - r, :] = turned[i:i + 1]
        update(ROWS - EDGE, EDGE, 1)

    to_east.wait_send()
    to_west.wait_send()
    to_east3.wait_send()
    to_west3.wait_send()

    @pl.when(not_top)
    def _():
        for send in north_sends:
            send.wait_send()
        to_north3.wait_send()

    @pl.when(not_low)
    def _():
        for send in south_sends:
            send.wait_send()
        to_south3.wait_send()

    @pl.when(is_top)
    def _():
        settle(fold2.at[0:NLON - 1, 0:FOLD2, :], group_send.at[0])
        settle(foldz.at[0:NZ - 1], group_send.at[1])
        settle(foldx.at[0:NX - 1], group_send.at[4])

    @pl.when(is_top & is_early)
    def _():
        settle(wide_sent.at[0:EARLY * NX * NLAT - 1, :], group_send.at[5])

    @pl.when(is_top & (lon_z >= EARLY))
    def _():
        settle(wide_sent, group_send.at[5])

    @pl.when(is_top)
    def _():
        settle(wide_sent.at[0:NX * NLAT - 1, :], group_send.at[6])

    @pl.when(not_top)
    def _():
        settle(wide_sent.at[0:NX * NLAT - 1, :], group_send.at[2])

    settle(sums2.at[0:NZ - 1, :], group_send.at[3])


def store(*refs):
    ins, outs, sem = refs[:5], refs[5:10], refs[10]
    copies = [pltpu.make_async_copy(i, o, sem.at[n]) for n, (i, o) in enumerate(zip(ins, outs))]
    for c in copies:
        c.start()
    for c in copies:
        c.wait()


def body(t, s, u, v, spans, water, opp, weights, anomaly):
    t, s, u, v, water, weights, anomaly, spans, opp = (
        pltpu.with_memory_space_constraint(r, pltpu.HBM) for r in (t, s, u, v, water, weights, anomaly, spans, opp)
    )
    hbm = pl.BlockSpec(memory_space=pltpu.HBM)
    vmem = pl.BlockSpec(memory_space=pltpu.VMEM)
    f32 = jnp.float32
    shapes = [jax.ShapeDtypeStruct((LEVELS, ROWS, LANES), f32)] * 4 + [jax.ShapeDtypeStruct((ROWS, LANES), f32)]
    full = ROWS + 2 * EDGE
    results = pl.pallas_call(
        kernel,
        out_shape=shapes,
        in_specs=[hbm] * 9,
        out_specs=[vmem] * 5,
        scratch_shapes=[
            pltpu.VMEM((2, LEVELS, full, LANES), f32),
            pltpu.VMEM((2, LEVELS, ROWS, LANES), f32),
            pltpu.VMEM((ROWS, LANES), jnp.int32),
            pltpu.VMEM((2, ROWS, LANES), f32),
            pltpu.VMEM((5, 2, full, LANES), f32),
            pltpu.VMEM((ROWS, LANES), f32),
            pltpu.VMEM((2, ROWS // 4, LANES), f32),
            pltpu.VMEM((2, ROWS // 4, LANES), f32),
            pltpu.VMEM((2, 2, EDGE, LANES), f32),
            pltpu.VMEM((2, ROWS // 2, LANES), f32),
            pltpu.VMEM((2, ROWS // 2, LANES), f32),
            pltpu.VMEM((16, LANES), f32),
            pltpu.VMEM((NLON, 16, LANES), f32),
            pltpu.VMEM((FOLD3, LANES), f32),
            pltpu.VMEM((NZ, FOLD3, LANES), f32),
            pltpu.VMEM((FOLD3, LANES), f32),
            pltpu.VMEM((NX, FOLD3, LANES), f32),
            pltpu.VMEM((3, full, LANES), f32),
            pltpu.VMEM((6, EDGE, LANES), f32),
            pltpu.VMEM((2 * EDGE, LANES), f32),
            pltpu.VMEM((NX * (NLAT - 1), LANES), f32),
            pltpu.VMEM((NZ, LANES), f32),
            pltpu.VMEM((NX, LANES), f32),
            pltpu.VMEM((NLON, LANES), f32),
            pltpu.VMEM((EARLY * NX * NLAT, LANES), f32),
            pltpu.SMEM((LEVELS,), f32),
            pltpu.SMEM((LANES,), jnp.int32),
            pltpu.SemaphoreType.DMA((9,)),
            pltpu.SemaphoreType.DMA((12,)),
            pltpu.SemaphoreType.DMA((12,)),
            pltpu.SemaphoreType.DMA((7,)),
            pltpu.SemaphoreType.DMA((7,)),
        ],
        compiler_params=pltpu.CompilerParams(
            collective_id=0, has_side_effects=True, vmem_limit_bytes=40 * 1024 * 1024
        ),
    )(t, s, u, v, water, weights, anomaly, spans, opp)
    anyspec = pl.BlockSpec(memory_space=pl.ANY)
    return pl.pallas_call(
        store,
        out_shape=shapes,
        in_specs=[anyspec] * 5,
        out_specs=[anyspec] * 5,
        scratch_shapes=[pltpu.SemaphoreType.DMA((5,))],
        compiler_params=pltpu.CompilerParams(vmem_limit_bytes=8 * 1024 * 1024),
    )(*results)


def solution(mesh):
    deep = P(None, "lat", "lon")
    flat = P("lat", "lon")
    return jax.shard_map(
        body,
        mesh=mesh,
        in_specs=(deep, deep, deep, deep, P(), flat, P("lon"), flat, flat),
        out_specs=(deep, deep, deep, deep, flat),
        check_vma=False,
    )
```

```python
import itertools

import jax
import jax.numpy as jnp
from jax import lax
from jax.experimental import pallas as pl
from jax.experimental.pallas import tpu as pltpu
from jax.sharding import PartitionSpec as P

MESH = pl.DeviceIdType.MESH
LEVELS = 10
ROWS = 64
LANES = 128
EDGE = 8
NLON = 32
NLAT = 8
NX = 4
NZ = 8
EARLY = 4
SPAN2 = 10
SPAN3 = 4
FOLD2 = 13
FOLD3 = 4 * LEVELS


def density(t, s):
    return -t - 0.15 * t * t + 0.8 * s - 0.2 * t * s


def lane_iota(rows):
    return lax.broadcasted_iota(jnp.int32, (rows, LANES), 1)


def kernel(
    t_hbm, s_hbm, u_hbm, v_hbm, w_hbm, e_hbm, a_hbm, spans_hbm, opp_hbm,
    nt, ns, nu, nv, surf,
    ts, uv, wbuf, ebuf, x, pack, slim, heard, wide, pack3, wide3, own2, fold2, own3, foldz, own3x, foldx, press, rim, vec, sums1, sums2, late1, crown, wide_sent,
    spans, opp, in_sem, side_send, side_recv, group_send, group_recv,
):
    lon = lax.axis_index("lon")
    lat = lax.axis_index("lat")
    lon_x = lax.rem(lon, NX)
    lon_z = lax.div(lon, NX)
    east = lax.rem(lon + 1, NLON)
    west = lax.rem(lon + NLON - 1, NLON)
    is_top = lat == NLAT - 1
    is_low = lat == 0
    not_top = lat < NLAT - 1
    not_low = lat > 0

    barrier = pltpu.get_barrier_semaphore()

    def greet(dev):
        pl.semaphore_signal(barrier, inc=1, device_id=dev, device_id_type=MESH)

    def hops(step, size):
        return min(step, size - step)

    lat_y = lax.div(lat, 2)
    lat_c = lat & 1
    zs = [((lon_z + d) & (NZ - 1)) * NX for d in range(NZ)]
    xs = [(lon_x + d) & (NX - 1) for d in range(NX)]
    lats = {(dy, dc): ((lat_y + dy) & (NLAT // 2 - 1)) * 2 + (lat_c ^ dc) for dy in range(NLAT // 2) for dc in range(2)}

    def at(dz, dx, dy, dc):
        return (zs[dz] + xs[dx], lats[dy, dc])

    near = [
        at(0, dx, dy, dc)
        for dx, dy, dc in sorted(
            itertools.product(range(NX), range(NLAT // 2), range(2)),
            key=lambda o: -hops(o[0], NX) - hops(o[1], NLAT // 2) - 0.5 * o[2],
        )
        if dx or dy or dc
    ]
    far = [at(dz, 0, 0, 0) for dz in sorted(range(1, NZ), key=lambda o: -hops(o, NZ))]
    ring = [
        at(dz, dx, 0, 0)
        for dz, dx in sorted(
            itertools.product(range(NZ), range(NX)), key=lambda o: -hops(o[0], NZ) - hops(o[1], NX)
        )
        if dz or dx
    ]

    is_early = lon_z < EARLY
    crowns = [
        ((zs[dz] + xs[dx], NLAT - 1), dz or dx) for dz, dx in itertools.product(range(NZ), range(NX))
    ]

    @pl.when(is_top)
    def _():
        for dev in ring:
            greet(dev)

    @pl.when(is_early)
    def _():
        for dev, other in crowns:
            if other:
                greet(dev)

    @pl.when(is_early & not_top)
    def _():
        greet((lon, NLAT - 1))

    for dev in far + near + [(east, lat), (west, lat)]:
        greet(dev)

    @pl.when(not_top)
    def _():
        greet((east, lat + 1))
        greet((west, lat + 1))

    @pl.when(not_low)
    def _():
        greet((east, lat - 1))
        greet((west, lat - 1))

    loads = [
        pltpu.make_async_copy(w_hbm, wbuf, in_sem.at[0]),
        pltpu.make_async_copy(e_hbm, ebuf.at[0], in_sem.at[1]),
        pltpu.make_async_copy(a_hbm, ebuf.at[1], in_sem.at[2]),
        pltpu.make_async_copy(t_hbm, ts.at[0, :, EDGE:EDGE + ROWS, :], in_sem.at[3]),
        pltpu.make_async_copy(s_hbm, ts.at[1, :, EDGE:EDGE + ROWS, :], in_sem.at[4]),
        pltpu.make_async_copy(u_hbm, uv.at[0], in_sem.at[5]),
        pltpu.make_async_copy(v_hbm, uv.at[1], in_sem.at[6]),
        pltpu.make_async_copy(spans_hbm, spans, in_sem.at[7]),
        pltpu.make_async_copy(opp_hbm, opp, in_sem.at[8]),
    ]
    for load in loads:
        load.start()

    for load in loads[:3]:
        load.wait()
    own = slice(EDGE, EDGE + ROWS)
    weights = ebuf[0]
    diagonal = 4.0 + weights
    wetness = wbuf[...].astype(jnp.float32)
    scale = wetness / diagonal
    x[3, 0, own, :] = scale
    x[4, 0, own, :] = scale * (weights * ebuf[1])

    for load in loads[3:]:
        load.wait()
    zero = jnp.zeros((ROWS, LANES), jnp.float32)
    below, press_sum, east_sum, north_sum = zero, zero, zero, zero
    for k in range(LEVELS):
        span = spans[k]
        layer = density(ts[0, k, own, :], ts[1, k, own, :]) * span
        press_sum = press_sum + span * (below + 0.5 * layer)
        below = below + layer
        east_sum = east_sum + span * uv[0, k]
        north_sum = north_sum + span * uv[1, k]
    x[0, 0, own, :] = press_sum
    x[1, 0, own, :] = east_sum
    x[2, 0, own, :] = north_sum

    lanes = lane_iota(ROWS)
    packed = zero
    for f in range(5):
        moved = pltpu.roll(x[f, 0, own, :], SPAN2 * f + 5, 1)
        packed = jnp.where((lanes >= SPAN2 * f) & (lanes < SPAN2 * (f + 1)), moved, packed)
    pack[...] = packed
    half = ROWS // 2
    quarter = ROWS // 4
    lanes_h = lane_iota(half)
    lanes_q = lane_iota(quarter)
    eastern = lax.rem(lanes_h, SPAN2) < 5
    for side, turned in ((0, SPAN2 - 5), (1, LANES - 5)):
        lower = pltpu.roll(packed[half:], turned, 1)
        folded = jnp.where(eastern, packed[:half], lower) if side == 0 else jnp.where(eastern, lower, packed[:half])
        slim[side] = jnp.where(lanes_q < LANES // 2, folded[:quarter], pltpu.roll(folded[quarter:], LANES // 2, 1))
    packed = zero
    for q in range(2 * LEVELS):
        moved = pltpu.roll(ts[q // LEVELS, q % LEVELS, own, :], SPAN3 * q + 2, 1)
        packed = jnp.where((lanes >= SPAN3 * q) & (lanes < SPAN3 * (q + 1)), moved, packed)
    outer = (lanes_h & 2) == 0
    pack3[0] = jnp.where(outer, packed[:half], pltpu.roll(packed[half:], 2, 1))
    pack3[1] = jnp.where(outer, pltpu.roll(packed[half:], LANES - 2, 1), packed[:half])

    @pl.when(is_top)
    def _():
        last = EDGE + ROWS - 1
        up = x[0, 0, last - 2:last + 1, :]
        down = x[0, 0, last - 4:last - 1, :]
        inner = slice(last - 3, last)
        flow = jnp.where(x[3, 0, inner, :] > 0.0, x[2, 0, inner, :] - 0.05 * (up - down), 0.0)
        for r in range(3):
            row = last - r
            own2[r:r + 1, :] = x[0, 0, row:row + 1, :]
            own2[3 + r:4 + r, :] = -x[1, 0, row:row + 1, :]
            half = 0.5 * x[3, 0, row:row + 1, :]
            own2[7 + r:8 + r, :] = x[3, 0, row:row + 1, :]
            inside = flow[2 - r:3 - r] if r < 2 else flow[0:1] - flow[2:3]
            own2[10 + r:11 + r, :] = x[4, 0, row:row + 1, :] + half * inside
        own2[6:7, :] = -x[2, 0, last:last + 1, :]
        fold2[lon, 0:FOLD2, :] = own2[0:FOLD2, :]
        for q in range(2 * LEVELS):
            own3[2 * q:2 * q + 2, :] = ts[q // LEVELS, q % LEVELS, EDGE + ROWS - 2:EDGE + ROWS, :]
        foldz[lon_z] = own3[...]
        for f in range(5):
            x[f, 0, EDGE + ROWS:, :] = jnp.zeros((EDGE, LANES), jnp.float32)

    @pl.when(is_low)
    def _():
        for f in range(5):
            x[f, 0, 0:EDGE, :] = jnp.zeros((EDGE, LANES), jnp.float32)
        for q in range(2 * LEVELS):
            ts[q // LEVELS, q % LEVELS, 0:EDGE, :] = jnp.zeros((EDGE, LANES), jnp.float32)

    base = 31 + 7 + 2

    crowned = base + 2 + NLON - 1 + EARLY * NX * NLAT

    @pl.when(is_top & is_early)
    def _():
        pl.semaphore_wait(barrier, crowned - 1)

    @pl.when(is_top & (lon_z >= EARLY))
    def _():
        pl.semaphore_wait(barrier, crowned)

    @pl.when(is_low)
    def _():
        pl.semaphore_wait(barrier, base + 2)

    @pl.when(not_top & not_low)
    def _():
        pl.semaphore_wait(barrier, base + 4)

    def copy(src, dst, sem, dev):
        return pltpu.make_async_remote_copy(
            src_ref=src, dst_ref=dst, send_sem=side_send.at[sem], recv_sem=side_recv.at[sem],
            device_id=dev, device_id_type=MESH,
        )

    top_rows = slice(EDGE + ROWS, EDGE + ROWS + EDGE)
    to_east = copy(slim.at[0], heard.at[0], 0, (east, lat))
    to_west = copy(slim.at[1], heard.at[1], 1, (west, lat))
    to_north = copy(x.at[:, 0, ROWS:EDGE + ROWS, :], x.at[:, 0, 0:EDGE, :], 2, (lon, lat + 1))
    to_ne = copy(pack.at[ROWS - EDGE:ROWS, :], wide.at[0, 0], 3, (east, lat + 1))
    to_nw = copy(pack.at[ROWS - EDGE:ROWS, :], wide.at[1, 0], 4, (west, lat + 1))
    to_south = copy(x.at[:, 0, EDGE:2 * EDGE, :], x.at[:, 0, top_rows, :], 5, (lon, lat - 1))
    to_se = copy(pack.at[0:EDGE, :], wide.at[0, 1], 6, (east, lat - 1))
    to_sw = copy(pack.at[0:EDGE, :], wide.at[1, 1], 7, (west, lat - 1))
    to_east3 = copy(pack3.at[0], wide3.at[0], 8, (east, lat))
    to_west3 = copy(pack3.at[1], wide3.at[1], 9, (west, lat))
    to_north3 = copy(
        ts.at[:, :, EDGE + ROWS - 2:EDGE + ROWS, :], ts.at[:, :, EDGE - 2:EDGE, :], 10, (lon, lat + 1)
    )
    to_south3 = copy(
        ts.at[:, :, EDGE:EDGE + 2, :], ts.at[:, :, EDGE + ROWS:EDGE + ROWS + 2, :], 11, (lon, lat - 1)
    )
    north_sends = (to_north, to_ne, to_nw)
    south_sends = (to_south, to_se, to_sw)

    def spread(src, dst, sem, devs):
        for dev in devs:
            pltpu.make_async_remote_copy(
                src_ref=src, dst_ref=dst, send_sem=group_send.at[sem], recv_sem=group_recv.at[sem],
                device_id=dev, device_id_type=MESH,
            ).start()

    def settle(ref, sem):
        pltpu.make_async_copy(ref, ref, sem).wait()

    to_east.start()
    to_west.start()

    @pl.when(not_top)
    def _():
        for send in north_sends:
            send.start()

    @pl.when(not_low)
    def _():
        for send in south_sends:
            send.start()

    @pl.when(is_top)
    def _():
        spread(own2.at[0:FOLD2, :], fold2.at[lon, 0:FOLD2, :], 0, ring)

    to_east3.start()
    to_west3.start()

    @pl.when(not_top)
    def _():
        to_north3.start()

    @pl.when(not_low)
    def _():
        to_south3.start()

    @pl.when(is_top)
    def _():
        spread(own3, foldz.at[lon_z], 1, far)

    to_east.wait_recv()
    to_west.wait_recv()

    @pl.when(not_low)
    def _():
        for send in north_sends:
            send.wait_recv()

    @pl.when(not_top)
    def _():
        for send in south_sends:
            send.wait_recv()

    lanes_w = lane_iota(EDGE + ROWS + EDGE)
    from_west, from_east = (
        jnp.concatenate([heard[side], pltpu.roll(heard[side], LANES // 2, 1)], axis=0) for side in range(2)
    )
    upper = jnp.where(eastern, from_west, from_east)
    lower = jnp.where(eastern, pltpu.roll(from_west, LANES - 5, 1), pltpu.roll(from_east, 5, 1))
    eastern_e = lax.rem(lane_iota(EDGE), SPAN2) < 5
    corners = [jnp.where(eastern_e, wide[0, c], wide[1, c]) for c in range(2)]
    merged = jnp.concatenate([corners[0], upper, lower, corners[1]], axis=0)
    for f in range(5):
        x[f, 1] = pltpu.roll(merged, LANES - (SPAN2 * f + 5), 1)

    @pl.when(is_low)
    def _():
        for f in range(5):
            x[f, 1, 0:EDGE, :] = jnp.zeros((EDGE, LANES), jnp.float32)

    lanes_e = lane_iota(EDGE)
    first = opp[0]
    slot = lax.div(first, LANES)
    offset = first - slot * LANES
    slot_p = lax.rem(slot + 1, NLON)
    slot_m = lax.rem(slot + NLON - 1, NLON)
    slot_mm = lax.rem(slot + NLON - 2, NLON)
    index = (offset - lanes_e) & (LANES - 1)

    def turn(tile):
        return jnp.take_along_axis(tile, index, axis=1)

    full = EDGE + ROWS + EDGE
    rows_end = jnp.where(is_top, EDGE + ROWS, full)
    pairs = ((0, 0), (0, 1), (1, 1), (1, 2), (2, 2), (2, 3))

    def north_of(a):
        return pltpu.roll(a, a.shape[0] - 1, 0)

    def south_of(a):
        return pltpu.roll(a, 1, 0)

    def krylov(low, count):
        lane = lane_iota(count)
        first_lane = lane == 0
        last_lane = lane == LANES - 1
        part = slice(low, low + count)

        def plus_east(a, b):
            return (
                pltpu.roll(jnp.where(first_lane, b, a), LANES - 1, 1),
                pltpu.roll(jnp.where(first_lane, a, b), LANES - 1, 1),
            )

        def plus_west(a, b):
            return (
                pltpu.roll(jnp.where(last_lane, b, a), 1, 1),
                pltpu.roll(jnp.where(last_lane, a, b), 1, 1),
            )

        row = lax.broadcasted_iota(jnp.int32, (count, LANES), 0) + low
        scale2 = (x[3, 0, part, :], x[3, 1, part, :])
        q2 = (x[0, 0, part, :], x[0, 1, part, :])
        q_e = plus_east(*q2)
        q_w = plus_west(*q2)
        flow_e, flow_n = [], []
        for h in range(2):
            wet = scale2[h] > 0.0
            flow_e.append(jnp.where(wet, x[1, h, part, :] - 0.05 * (q_e[h] - q_w[h]), 0.0))
            slope = north_of(q2[h]) - south_of(q2[h])
            flow_n.append(jnp.where(wet & (row <= rows_end), x[2, h, part, :] - 0.05 * slope, 0.0))
        f_e = plus_east(*flow_e)
        f_w = plus_west(*flow_e)
        v = tuple(
            x[4, h, part, :]
            - scale2[h] * (0.5 * (f_e[h] - f_w[h] + north_of(flow_n[h]) - south_of(flow_n[h])))
            for h in range(2)
        )
        basis = [v[0]]
        for _ in range(3):
            v_e = plus_east(*v)
            v_w = plus_west(*v)
            v = tuple(scale2[h] * (v_e[h] + v_w[h] + north_of(v[h]) + south_of(v[h])) for h in range(2))
            basis.append(v[0])
        return basis

    basis = [v[own] for v in krylov(0, full)]
    for i in range(3):
        press[i, own, :] = basis[i]
    bulk = []
    for j, (l, r) in enumerate(pairs):
        product = ((diagonal * basis[l]) * basis[r]).reshape(ROWS // EDGE, EDGE, LANES)
        bulk.append(jnp.sum(product[:-1], axis=0))
        rim[j] = product[-1]

    @pl.when(is_top)
    def _():
        settle(fold2.at[0:NLON - 1, 0:FOLD2, :], group_recv.at[0])
        kept = lanes_e <= offset
        near_half = index < LANES // 2
        mine, aside = [], []
        for tile in range(2):
            part = slice(EDGE * tile, EDGE * (tile + 1))
            b_p, b_0, b_m, b_mm = (fold2[s, part, :] for s in (slot_p, slot, slot_m, slot_mm))
            mine.append(turn(jnp.where(kept, b_0, b_m)))
            right = jnp.where(kept, b_m, b_mm)
            left = jnp.where(kept, b_p, b_0)
            aside.append(turn(jnp.where(near_half, right, left)))
        for half, tiles in ((0, mine), (1, aside)):
            north = EDGE + ROWS
            x[0, half, north:north + 3, :] = tiles[0][0:3]
            x[1, half, north:north + 3, :] = tiles[0][3:6]
            x[2, half, north:north + 1, :] = tiles[0][6:7]
            x[3, half, north:north + 1, :] = tiles[0][7:8]
            x[3, half, north + 1:north + 3, :] = tiles[1][0:2]
            x[4, half, north:north + 3, :] = tiles[1][2:5]
        final = slice(EDGE, 2 * EDGE)
        rim_diagonal = 4.0 + ebuf[0, ROWS - EDGE:, :]
        basis = [v[final] for v in krylov(ROWS - EDGE, 3 * EDGE)]
        for i in range(3):
            press[i, ROWS:ROWS + EDGE, :] = basis[i]
        for j, (l, r) in enumerate(pairs):
            rim[j] = (rim_diagonal * basis[l]) * basis[r]

    sub = lax.broadcasted_iota(jnp.int32, (EDGE, LANES), 0)
    table = jnp.zeros((EDGE, LANES), jnp.float32)
    for j in range(len(pairs)):
        line = jnp.sum(bulk[j] + rim[j], axis=0, keepdims=True)
        table = jnp.where(sub == j, line, table)
    table = jnp.sum(table, axis=1, keepdims=True)
    message = jnp.sum(jnp.where(sub == lanes_e, table, 0.0), axis=0, keepdims=True)
    vec[0:1, :] = message
    mine1 = lon_x * (NLAT - 1) + lat

    @pl.when(not_top)
    def _():
        sums1[pl.ds(mine1, 1), :] = message
        spread(vec.at[0:1, :], sums1.at[pl.ds(mine1, 1), :], 2, near)

    @pl.when(is_top)
    def _():
        late1[pl.ds(lon_x, 1), :] = message
        for dz in range(NZ):
            for dx, dy, dc in itertools.product(range(NX), range(NLAT // 2), range(2)):
                if dz or dx or dy or dc:

                    @pl.when(zs[dz] < EARLY * NX)
                    def _(dev=at(dz, dx, dy, dc)):
                        spread(vec.at[0:1, :], crown.at[pl.ds(lon, 1), :], 5, [dev])

        spread(vec.at[0:1, :], late1.at[pl.ds(lon_x, 1), :], 6, near)

    @pl.when(is_top & is_early)
    def _():
        crown[pl.ds(lon, 1), :] = message

    def hear_tracers():
        to_east3.wait_recv()
        to_west3.wait_recv()

        @pl.when(not_low)
        def _():
            to_north3.wait_recv()

        @pl.when(not_top)
        def _():
            to_south3.wait_recv()

    def update(low, rows, parts):
        lane = lane_iota(rows)
        part = slice(low, low + rows)
        wet = wbuf[part, :].astype(jnp.float32)
        rows_3 = []
        if low < ROWS // 2:
            rows_3.append(jnp.where(outer, wide3[0], wide3[1]))
        cut = max(low - ROWS // 2, 0)
        low_w = pltpu.roll(wide3[0, cut:, :], LANES - 2, 1)
        low_e = pltpu.roll(wide3[1, cut:, :], 2, 1)
        rows_3.append(jnp.where(outer[cut:], low_w, low_e))
        joined = jnp.concatenate(rows_3, axis=0)
        below = jnp.zeros((rows + 2 * EDGE, LANES), jnp.float32)
        below_side = jnp.zeros((rows, LANES), jnp.float32)
        mid = slice(EDGE, EDGE + rows)
        for k in range(LEVELS):
            span = spans[k]
            u = uv[0, k, part, :]
            w = uv[1, k, part, :]
            sides = []
            for f in range(2):
                side = pltpu.roll(joined, LANES - (SPAN3 * (f * LEVELS + k) + 2), 1)
                sides.append(side)
                at = EDGE + low
                c = ts[f, k, at:at + rows, :]
                e1 = pltpu.roll(jnp.where(lane == 0, side, c), LANES - 1, 1)
                e2 = pltpu.roll(jnp.where(lane < 2, side, c), LANES - 2, 1)
                w1 = pltpu.roll(jnp.where(lane == LANES - 1, side, c), 1, 1)
                w2 = pltpu.roll(jnp.where(lane >= LANES - 2, side, c), 2, 1)
                n1 = ts[f, k, at + 1:at + rows + 1, :]
                n2 = ts[f, k, at + 2:at + rows + 2, :]
                s1 = ts[f, k, at - 1:at + rows - 1, :]
                s2 = ts[f, k, at - 2:at + rows - 2, :]
                grad_e = (8.0 * (e1 - w1) - (e2 - w2)) * (1.0 / 12.0)
                grad_n = (8.0 * (n1 - s1) - (n2 - s2)) * (1.0 / 12.0)
                laplace = e1 + w1 + n1 + s1 - 4.0 * c
                out = (nt, ns)[f]
                out[k, part, :] = c + wet * (-0.1 * (u * grad_e + w * grad_n) + 0.1 * laplace)
            reach = slice(low, low + rows + 2 * EDGE)
            layer = density(ts[0, k, reach, :], ts[1, k, reach, :]) * span
            level = below + 0.5 * layer
            below = below + layer
            p_n = pltpu.roll(level, rows + 2 * EDGE - 1, 0)[mid]
            p_s = pltpu.roll(level, 1, 0)[mid]
            nv[k, part, :] = wet * (w - 0.05 * (p_n - p_s))
            if parts > 1:
                layer_side = density(sides[0], sides[1]) * span
                level_side = below_side + 0.5 * layer_side
                below_side = below_side + layer_side
                centre = level[mid]
                p_e = pltpu.roll(jnp.where(lane == 0, level_side, centre), LANES - 1, 1)
                p_w = pltpu.roll(jnp.where(lane == LANES - 1, level_side, centre), 1, 1)
                nu[k, part, :] = wet * (u - 0.05 * (p_e - p_w))

    @pl.when(not_top)
    def _():
        hear_tracers()
        update(0, ROWS, 2)

    body_rows = NX * (NLAT - 1)

    @pl.when(is_top)
    def _():
        settle(sums1, group_recv.at[2])

    @pl.when(not_top)
    def _():
        settle(sums1.at[0:body_rows - 1, :], group_recv.at[2])

    total = jnp.sum(sums1[...], axis=0, keepdims=True)
    vec[EDGE:EDGE + 1, :] = total

    @pl.when(is_early)
    def _():
        sums2[pl.ds(lon_z, 1), :] = total

    def cross(row, early):
        for dz in sorted(range(1, NZ), key=lambda o: -hops(o, NZ)):
            bound = EARLY * NX

            @pl.when((zs[dz] < bound) if early else (zs[dz] >= bound))
            def _(dev=at(dz, 0, 0, 0)):
                spread(vec.at[row:row + 1, :], sums2.at[pl.ds(lon_z, 1), :], 3, [dev])

    cross(EDGE, True)

    @pl.when(is_top)
    def _():
        settle(late1.at[0:NX - 1, :], group_recv.at[6])

    @pl.when(not_top)
    def _():
        settle(late1, group_recv.at[6])

    total = total + jnp.sum(late1[...], axis=0, keepdims=True)
    vec[EDGE + 1:EDGE + 2, :] = total

    @pl.when(lon_z >= EARLY)
    def _():
        sums2[pl.ds(lon_z, 1), :] = total

    cross(EDGE + 1, False)

    beside = [(lon - lon_x + lax.rem(lon_x + k, NX), lat) for k in range(1, NX)]
    kept = lane_iota(FOLD3) <= offset

    @pl.when(is_top)
    def _():
        settle(foldz.at[0:NZ - 1], group_recv.at[1])
        base_slot = slot + lon_x + NLON
        row_0 = lax.div(lax.rem(base_slot - (slot & (NX - 1)), NLON), NX)
        row_1 = lax.div(lax.rem(base_slot - 1 - ((slot + NX - 1) & (NX - 1)), NLON), NX)
        joint = jnp.where(kept, foldz[row_0], foldz[row_1])
        own3x[...] = joint
        foldx[lon_x] = joint
        spread(own3x, foldx.at[lon_x], 4, beside)
        hear_tracers()
        update(0, ROWS, 2)

    settle(sums2.at[0:NZ - 1, :], group_recv.at[3])
    vec[EDGE + 2:EDGE + 3, :] = jnp.sum(sums2[...], axis=0, keepdims=True)

    @pl.when(is_early & is_top)
    def _():
        settle(crown.at[0:NLON - 1, :], group_recv.at[5])

    @pl.when(is_early & not_top)
    def _():
        settle(crown, group_recv.at[5])

    @pl.when(is_early)
    def _():
        vec[EDGE + 2:EDGE + 3, :] = vec[EDGE + 2:EDGE + 3, :] + jnp.sum(crown[...], axis=0, keepdims=True)

    total = vec[EDGE + 2:EDGE + 3, :]
    mu = [total[:, j:j + 1] for j in range(6)]

    def gram(a, b, shift):
        out = None
        for i, ai in enumerate(a):
            for j, bj in enumerate(b):
                term = ai * bj * mu[i + j + shift]
                out = term if out is None else out + term
        return out

    one = jnp.ones((1, 1), jnp.float32)
    res, dire, sol = [one], [one], [0.0 * one] * 3
    rz = mu[0]
    for step in range(3):
        alpha = rz / (gram(dire, dire, 0) - gram(dire, dire, 1))
        sol = [sol[i] + alpha * dire[i] if i < len(dire) else sol[i] for i in range(3)]
        if step < 2:
            image = [
                (dire[i] if i < len(dire) else 0.0) - (dire[i - 1] if i else 0.0) for i in range(len(dire) + 1)
            ]
            res = [(res[i] if i < len(res) else 0.0) - alpha * image[i] for i in range(len(image))]
            new = gram(res, res, 0)
            beta = new / rz
            dire = [res[i] + (beta * dire[i] if i < len(dire) else 0.0) for i in range(len(res))]
            rz = new
    surf[...] = sol[0] * press[0, own, :] + sol[1] * press[1, own, :] + sol[2] * press[2, own, :]

    @pl.when(is_top)
    def _():
        settle(foldx.at[0:NX - 1], group_recv.at[4])
        side_0 = slot & (NX - 1)
        side_1 = (slot + NX - 1) & (NX - 1)
        for tile in range(FOLD3 // EDGE):
            part = slice(EDGE * tile, EDGE * (tile + 1))
            turned = turn(jnp.where(kept[part], foldx[side_0, part, :], foldx[side_1, part, :]))
            for i in range(EDGE):
                q, r = (EDGE * tile + i) // 2, (EDGE * tile + i) % 2
                ts[q // LEVELS, q % LEVELS, EDGE + ROWS + 1 - r:EDGE + ROWS + 2 - r, :] = turned[i:i + 1]
        update(ROWS - EDGE, EDGE, 1)

    to_east.wait_send()
    to_west.wait_send()
    to_east3.wait_send()
    to_west3.wait_send()

    @pl.when(not_top)
    def _():
        for send in north_sends:
            send.wait_send()
        to_north3.wait_send()

    @pl.when(not_low)
    def _():
        for send in south_sends:
            send.wait_send()
        to_south3.wait_send()

    @pl.when(is_top)
    def _():
        settle(fold2.at[0:NLON - 1, 0:FOLD2, :], group_send.at[0])
        settle(foldz.at[0:NZ - 1], group_send.at[1])
        settle(foldx.at[0:NX - 1], group_send.at[4])

    @pl.when(is_top & is_early)
    def _():
        settle(wide_sent.at[0:EARLY * NX * NLAT - 1, :], group_send.at[5])

    @pl.when(is_top & (lon_z >= EARLY))
    def _():
        settle(wide_sent, group_send.at[5])

    @pl.when(is_top)
    def _():
        settle(wide_sent.at[0:NX * NLAT - 1, :], group_send.at[6])

    @pl.when(not_top)
    def _():
        settle(wide_sent.at[0:NX * NLAT - 1, :], group_send.at[2])

    settle(sums2.at[0:NZ - 1, :], group_send.at[3])


def store(*refs):
    ins, outs, sem = refs[:5], refs[5:10], refs[10]
    copies = [pltpu.make_async_copy(i, o, sem.at[n]) for n, (i, o) in enumerate(zip(ins, outs))]
    for c in copies:
        c.start()
    for c in copies:
        c.wait()


def body(t, s, u, v, spans, water, opp, weights, anomaly):
    t, s, u, v, water, weights, anomaly, spans, opp = (
        pltpu.with_memory_space_constraint(r, pltpu.HBM) for r in (t, s, u, v, water, weights, anomaly, spans, opp)
    )
    hbm = pl.BlockSpec(memory_space=pltpu.HBM)
    vmem = pl.BlockSpec(memory_space=pltpu.VMEM)
    f32 = jnp.float32
    shapes = [jax.ShapeDtypeStruct((LEVELS, ROWS, LANES), f32)] * 4 + [jax.ShapeDtypeStruct((ROWS, LANES), f32)]
    full = ROWS + 2 * EDGE
    results = pl.pallas_call(
        kernel,
        out_shape=shapes,
        in_specs=[hbm] * 9,
        out_specs=[vmem] * 5,
        scratch_shapes=[
            pltpu.VMEM((2, LEVELS, full, LANES), f32),
            pltpu.VMEM((2, LEVELS, ROWS, LANES), f32),
            pltpu.VMEM((ROWS, LANES), jnp.int32),
            pltpu.VMEM((2, ROWS, LANES), f32),
            pltpu.VMEM((5, 2, full, LANES), f32),
            pltpu.VMEM((ROWS, LANES), f32),
            pltpu.VMEM((2, ROWS // 4, LANES), f32),
            pltpu.VMEM((2, ROWS // 4, LANES), f32),
            pltpu.VMEM((2, 2, EDGE, LANES), f32),
            pltpu.VMEM((2, ROWS // 2, LANES), f32),
            pltpu.VMEM((2, ROWS // 2, LANES), f32),
            pltpu.VMEM((16, LANES), f32),
            pltpu.VMEM((NLON, 16, LANES), f32),
            pltpu.VMEM((FOLD3, LANES), f32),
            pltpu.VMEM((NZ, FOLD3, LANES), f32),
            pltpu.VMEM((FOLD3, LANES), f32),
            pltpu.VMEM((NX, FOLD3, LANES), f32),
            pltpu.VMEM((3, full, LANES), f32),
            pltpu.VMEM((6, EDGE, LANES), f32),
            pltpu.VMEM((2 * EDGE, LANES), f32),
            pltpu.VMEM((NX * (NLAT - 1), LANES), f32),
            pltpu.VMEM((NZ, LANES), f32),
            pltpu.VMEM((NX, LANES), f32),
            pltpu.VMEM((NLON, LANES), f32),
            pltpu.VMEM((EARLY * NX * NLAT, LANES), f32),
            pltpu.SMEM((LEVELS,), f32),
            pltpu.SMEM((LANES,), jnp.int32),
            pltpu.SemaphoreType.DMA((9,)),
            pltpu.SemaphoreType.DMA((12,)),
            pltpu.SemaphoreType.DMA((12,)),
            pltpu.SemaphoreType.DMA((7,)),
            pltpu.SemaphoreType.DMA((7,)),
        ],
        compiler_params=pltpu.CompilerParams(
            collective_id=0, has_side_effects=True, vmem_limit_bytes=40 * 1024 * 1024
        ),
    )(t, s, u, v, water, weights, anomaly, spans, opp)
    anyspec = pl.BlockSpec(memory_space=pl.ANY)
    return pl.pallas_call(
        store,
        out_shape=shapes,
        in_specs=[anyspec] * 5,
        out_specs=[anyspec] * 5,
        scratch_shapes=[pltpu.SemaphoreType.DMA((5,))],
        compiler_params=pltpu.CompilerParams(vmem_limit_bytes=8 * 1024 * 1024),
    )(*results)


def solution(mesh):
    deep = P(None, "lat", "lon")
    flat = P("lat", "lon")
    return jax.shard_map(
        body,
        mesh=mesh,
        in_specs=(deep, deep, deep, deep, P(), flat, P("lon"), flat, flat),
        out_specs=(deep, deep, deep, deep, flat),
        check_vma=False,
    )
```

```python
import itertools

import jax
import jax.numpy as jnp
from jax import lax
from jax.experimental import pallas as pl
from jax.experimental.pallas import tpu as pltpu
from jax.sharding import PartitionSpec as P

MESH = pl.DeviceIdType.MESH
LEVELS = 10
ROWS = 64
LANES = 128
EDGE = 8
NLON = 32
NLAT = 8
NX = 4
NZ = 8
EARLY = 4
SPAN2 = 10
SPAN3 = 4
FOLD2 = 13
FOLD3 = 4 * LEVELS


def density(t, s):
    return -t - 0.15 * t * t + 0.8 * s - 0.2 * t * s


def lane_iota(rows):
    return lax.broadcasted_iota(jnp.int32, (rows, LANES), 1)


def kernel(
    t_hbm, s_hbm, u_hbm, v_hbm, w_hbm, e_hbm, a_hbm, spans_hbm, opp_hbm,
    nt, ns, nu, nv, surf,
    ts, uv, wbuf, ebuf, x, pack, slim, heard, wide, pack3, wide3, own2, fold2, own3, foldz, own3x, foldx, press, rim, vec, sums1, sums2, late1, crown, wide_sent,
    spans, opp, in_sem, side_send, side_recv, group_send, group_recv,
):
    lon = lax.axis_index("lon")
    lat = lax.axis_index("lat")
    lon_x = lax.rem(lon, NX)
    lon_z = lax.div(lon, NX)
    east = lax.rem(lon + 1, NLON)
    west = lax.rem(lon + NLON - 1, NLON)
    above = lax.rem(lat + 1, NLAT)
    beneath = lax.rem(lat + NLAT - 1, NLAT)
    is_top = lat == NLAT - 1
    is_low = lat == 0
    not_top = lat < NLAT - 1
    not_low = lat > 0

    barrier = pltpu.get_barrier_semaphore()

    def greet(dev):
        pl.semaphore_signal(barrier, inc=1, device_id=dev, device_id_type=MESH)

    def hops(step, size):
        return min(step, size - step)

    lat_y = lax.div(lat, 2)
    lat_c = lat & 1
    zs = [((lon_z + d) & (NZ - 1)) * NX for d in range(NZ)]
    xs = [(lon_x + d) & (NX - 1) for d in range(NX)]
    lats = {(dy, dc): ((lat_y + dy) & (NLAT // 2 - 1)) * 2 + (lat_c ^ dc) for dy in range(NLAT // 2) for dc in range(2)}

    def at(dz, dx, dy, dc):
        return (zs[dz] + xs[dx], lats[dy, dc])

    near = [
        at(0, dx, dy, dc)
        for dx, dy, dc in sorted(
            itertools.product(range(NX), range(NLAT // 2), range(2)),
            key=lambda o: -hops(o[0], NX) - hops(o[1], NLAT // 2) - 0.5 * o[2],
        )
        if dx or dy or dc
    ]
    far = [at(dz, 0, 0, 0) for dz in sorted(range(1, NZ), key=lambda o: -hops(o, NZ))]
    ring = [
        at(dz, dx, 0, 0)
        for dz, dx in sorted(
            itertools.product(range(NZ), range(NX)), key=lambda o: -hops(o[0], NZ) - hops(o[1], NX)
        )
        if dz or dx
    ]

    is_early = lon_z < EARLY
    crowns = [
        ((zs[dz] + xs[dx], NLAT - 1), dz or dx) for dz, dx in itertools.product(range(NZ), range(NX))
    ]

    @pl.when(is_top)
    def _():
        for dev in ring:
            greet(dev)

    @pl.when(is_early)
    def _():
        for dev, other in crowns:
            if other:
                greet(dev)

    @pl.when(is_early & not_top)
    def _():
        greet((lon, NLAT - 1))

    for dev in far + near + [(east, lat), (west, lat)]:
        greet(dev)

    @pl.when(not_top)
    def _():
        greet((east, above))
        greet((west, above))

    @pl.when(not_low)
    def _():
        greet((east, beneath))
        greet((west, beneath))

    loads = [
        pltpu.make_async_copy(w_hbm, wbuf, in_sem.at[0]),
        pltpu.make_async_copy(e_hbm, ebuf.at[0], in_sem.at[1]),
        pltpu.make_async_copy(a_hbm, ebuf.at[1], in_sem.at[2]),
        pltpu.make_async_copy(t_hbm, ts.at[0, :, EDGE:EDGE + ROWS, :], in_sem.at[3]),
        pltpu.make_async_copy(s_hbm, ts.at[1, :, EDGE:EDGE + ROWS, :], in_sem.at[4]),
        pltpu.make_async_copy(u_hbm, uv.at[0], in_sem.at[5]),
        pltpu.make_async_copy(v_hbm, uv.at[1], in_sem.at[6]),
        pltpu.make_async_copy(spans_hbm, spans, in_sem.at[7]),
        pltpu.make_async_copy(opp_hbm, opp, in_sem.at[8]),
    ]
    for load in loads:
        load.start()

    for load in loads[:3]:
        load.wait()
    own = slice(EDGE, EDGE + ROWS)
    weights = ebuf[0]
    diagonal = 4.0 + weights
    wetness = wbuf[...].astype(jnp.float32)
    scale = wetness / diagonal
    x[3, 0, own, :] = scale
    x[4, 0, own, :] = scale * (weights * ebuf[1])

    for load in loads[3:]:
        load.wait()
    zero = jnp.zeros((ROWS, LANES), jnp.float32)
    below, press_sum, east_sum, north_sum = zero, zero, zero, zero
    for k in range(LEVELS):
        span = spans[k]
        layer = density(ts[0, k, own, :], ts[1, k, own, :]) * span
        press_sum = press_sum + span * (below + 0.5 * layer)
        below = below + layer
        east_sum = east_sum + span * uv[0, k]
        north_sum = north_sum + span * uv[1, k]
    x[0, 0, own, :] = press_sum
    x[1, 0, own, :] = east_sum
    x[2, 0, own, :] = north_sum

    lanes = lane_iota(ROWS)
    packed = zero
    for f in range(5):
        moved = pltpu.roll(x[f, 0, own, :], SPAN2 * f + 5, 1)
        packed = jnp.where((lanes >= SPAN2 * f) & (lanes < SPAN2 * (f + 1)), moved, packed)
    pack[...] = packed
    half = ROWS // 2
    quarter = ROWS // 4
    lanes_h = lane_iota(half)
    lanes_q = lane_iota(quarter)
    eastern = lax.rem(lanes_h, SPAN2) < 5
    for side, turned in ((0, SPAN2 - 5), (1, LANES - 5)):
        lower = pltpu.roll(packed[half:], turned, 1)
        folded = jnp.where(eastern, packed[:half], lower) if side == 0 else jnp.where(eastern, lower, packed[:half])
        slim[side] = jnp.where(lanes_q < LANES // 2, folded[:quarter], pltpu.roll(folded[quarter:], LANES // 2, 1))
    packed = zero
    for q in range(2 * LEVELS):
        moved = pltpu.roll(ts[q // LEVELS, q % LEVELS, own, :], SPAN3 * q + 2, 1)
        packed = jnp.where((lanes >= SPAN3 * q) & (lanes < SPAN3 * (q + 1)), moved, packed)
    outer = (lanes_h & 2) == 0
    pack3[0] = jnp.where(outer, packed[:half], pltpu.roll(packed[half:], 2, 1))
    pack3[1] = jnp.where(outer, pltpu.roll(packed[half:], LANES - 2, 1), packed[:half])

    @pl.when(is_top)
    def _():
        last = EDGE + ROWS - 1
        up = x[0, 0, last - 2:last + 1, :]
        down = x[0, 0, last - 4:last - 1, :]
        inner = slice(last - 3, last)
        flow = jnp.where(x[3, 0, inner, :] > 0.0, x[2, 0, inner, :] - 0.05 * (up - down), 0.0)
        for r in range(3):
            row = last - r
            own2[r:r + 1, :] = x[0, 0, row:row + 1, :]
            own2[3 + r:4 + r, :] = -x[1, 0, row:row + 1, :]
            half = 0.5 * x[3, 0, row:row + 1, :]
            own2[7 + r:8 + r, :] = x[3, 0, row:row + 1, :]
            inside = flow[2 - r:3 - r] if r < 2 else flow[0:1] - flow[2:3]
            own2[10 + r:11 + r, :] = x[4, 0, row:row + 1, :] + half * inside
        own2[6:7, :] = -x[2, 0, last:last + 1, :]
        fold2[lon, 0:FOLD2, :] = own2[0:FOLD2, :]
        for q in range(2 * LEVELS):
            own3[2 * q:2 * q + 2, :] = ts[q // LEVELS, q % LEVELS, EDGE + ROWS - 2:EDGE + ROWS, :]
        foldz[lon_z] = own3[...]
        for f in range(5):
            x[f, 0, EDGE + ROWS:, :] = jnp.zeros((EDGE, LANES), jnp.float32)

    @pl.when(is_low)
    def _():
        for f in range(5):
            x[f, 0, 0:EDGE, :] = jnp.zeros((EDGE, LANES), jnp.float32)
        for q in range(2 * LEVELS):
            ts[q // LEVELS, q % LEVELS, 0:EDGE, :] = jnp.zeros((EDGE, LANES), jnp.float32)

    base = 31 + 7 + 2

    crowned = base + 2 + NLON - 1 + EARLY * NX * NLAT

    @pl.when(is_top & is_early)
    def _():
        pl.semaphore_wait(barrier, crowned - 1)

    @pl.when(is_top & (lon_z >= EARLY))
    def _():
        pl.semaphore_wait(barrier, crowned)

    @pl.when(is_low)
    def _():
        pl.semaphore_wait(barrier, base + 2)

    @pl.when(not_top & not_low)
    def _():
        pl.semaphore_wait(barrier, base + 4)

    def copy(src, dst, sem, dev):
        return pltpu.make_async_remote_copy(
            src_ref=src, dst_ref=dst, send_sem=side_send.at[sem], recv_sem=side_recv.at[sem],
            device_id=dev, device_id_type=MESH,
        )

    top_rows = slice(EDGE + ROWS, EDGE + ROWS + EDGE)
    to_east = copy(slim.at[0], heard.at[0], 0, (east, lat))
    to_west = copy(slim.at[1], heard.at[1], 1, (west, lat))
    to_north = copy(x.at[:, 0, ROWS:EDGE + ROWS, :], x.at[:, 0, 0:EDGE, :], 2, (lon, above))
    to_ne = copy(pack.at[ROWS - EDGE:ROWS, :], wide.at[0, 0], 3, (east, above))
    to_nw = copy(pack.at[ROWS - EDGE:ROWS, :], wide.at[1, 0], 4, (west, above))
    to_south = copy(x.at[:, 0, EDGE:2 * EDGE, :], x.at[:, 0, top_rows, :], 5, (lon, beneath))
    to_se = copy(pack.at[0:EDGE, :], wide.at[0, 1], 6, (east, beneath))
    to_sw = copy(pack.at[0:EDGE, :], wide.at[1, 1], 7, (west, beneath))
    to_east3 = copy(pack3.at[0], wide3.at[0], 8, (east, lat))
    to_west3 = copy(pack3.at[1], wide3.at[1], 9, (west, lat))
    to_north3 = copy(
        ts.at[:, :, EDGE + ROWS - 2:EDGE + ROWS, :], ts.at[:, :, EDGE - 2:EDGE, :], 10, (lon, above)
    )
    to_south3 = copy(
        ts.at[:, :, EDGE:EDGE + 2, :], ts.at[:, :, EDGE + ROWS:EDGE + ROWS + 2, :], 11, (lon, beneath)
    )
    north_sends = (to_north, to_ne, to_nw)
    south_sends = (to_south, to_se, to_sw)

    def spread(src, dst, sem, devs):
        for dev in devs:
            pltpu.make_async_remote_copy(
                src_ref=src, dst_ref=dst, send_sem=group_send.at[sem], recv_sem=group_recv.at[sem],
                device_id=dev, device_id_type=MESH,
            ).start()

    def settle(ref, sem):
        pltpu.make_async_copy(ref, ref, sem).wait()

    to_east.start()
    to_west.start()

    @pl.when(not_top)
    def _():
        for send in north_sends:
            send.start()

    @pl.when(not_low)
    def _():
        for send in south_sends:
            send.start()

    @pl.when(is_top)
    def _():
        spread(own2.at[0:FOLD2, :], fold2.at[lon, 0:FOLD2, :], 0, ring)

    to_east3.start()
    to_west3.start()

    @pl.when(not_top)
    def _():
        to_north3.start()

    @pl.when(not_low)
    def _():
        to_south3.start()

    @pl.when(is_top)
    def _():
        spread(own3, foldz.at[lon_z], 1, far)

    to_east.wait_recv()
    to_west.wait_recv()

    @pl.when(not_low)
    def _():
        for send in north_sends:
            send.wait_recv()

    @pl.when(not_top)
    def _():
        for send in south_sends:
            send.wait_recv()

    lanes_w = lane_iota(EDGE + ROWS + EDGE)
    from_west, from_east = (
        jnp.concatenate([heard[side], pltpu.roll(heard[side], LANES // 2, 1)], axis=0) for side in range(2)
    )
    upper = jnp.where(eastern, from_west, from_east)
    lower = jnp.where(eastern, pltpu.roll(from_west, LANES - 5, 1), pltpu.roll(from_east, 5, 1))
    eastern_e = lax.rem(lane_iota(EDGE), SPAN2) < 5
    corners = [jnp.where(eastern_e, wide[0, c], wide[1, c]) for c in range(2)]
    merged = jnp.concatenate([corners[0], upper, lower, corners[1]], axis=0)
    for f in range(5):
        x[f, 1] = pltpu.roll(merged, LANES - (SPAN2 * f + 5), 1)

    @pl.when(is_low)
    def _():
        for f in range(5):
            x[f, 1, 0:EDGE, :] = jnp.zeros((EDGE, LANES), jnp.float32)

    lanes_e = lane_iota(EDGE)
    first = opp[0]
    slot = lax.div(first, LANES)
    offset = first - slot * LANES
    slot_p = lax.rem(slot + 1, NLON)
    slot_m = lax.rem(slot + NLON - 1, NLON)
    slot_mm = lax.rem(slot + NLON - 2, NLON)
    index = (offset - lanes_e) & (LANES - 1)

    def turn(tile):
        return jnp.take_along_axis(tile, index, axis=1)

    full = EDGE + ROWS + EDGE
    rows_end = jnp.where(is_top, EDGE + ROWS, full)
    pairs = ((0, 0), (0, 1), (1, 1), (1, 2), (2, 2), (2, 3))

    def north_of(a):
        return pltpu.roll(a, a.shape[0] - 1, 0)

    def south_of(a):
        return pltpu.roll(a, 1, 0)

    def krylov(low, count):
        lane = lane_iota(count)
        first_lane = lane == 0
        last_lane = lane == LANES - 1
        part = slice(low, low + count)

        def plus_east(a, b):
            return (
                pltpu.roll(jnp.where(first_lane, b, a), LANES - 1, 1),
                pltpu.roll(jnp.where(first_lane, a, b), LANES - 1, 1),
            )

        def plus_west(a, b):
            return (
                pltpu.roll(jnp.where(last_lane, b, a), 1, 1),
                pltpu.roll(jnp.where(last_lane, a, b), 1, 1),
            )

        row = lax.broadcasted_iota(jnp.int32, (count, LANES), 0) + low
        scale2 = (x[3, 0, part, :], x[3, 1, part, :])
        q2 = (x[0, 0, part, :], x[0, 1, part, :])
        q_e = plus_east(*q2)
        q_w = plus_west(*q2)
        flow_e, flow_n = [], []
        for h in range(2):
            wet = scale2[h] > 0.0
            flow_e.append(jnp.where(wet, x[1, h, part, :] - 0.05 * (q_e[h] - q_w[h]), 0.0))
            slope = north_of(q2[h]) - south_of(q2[h])
            flow_n.append(jnp.where(wet & (row <= rows_end), x[2, h, part, :] - 0.05 * slope, 0.0))
        f_e = plus_east(*flow_e)
        f_w = plus_west(*flow_e)
        v = tuple(
            x[4, h, part, :]
            - scale2[h] * (0.5 * (f_e[h] - f_w[h] + north_of(flow_n[h]) - south_of(flow_n[h])))
            for h in range(2)
        )
        basis = [v[0]]
        for _ in range(3):
            v_e = plus_east(*v)
            v_w = plus_west(*v)
            v = tuple(scale2[h] * (v_e[h] + v_w[h] + north_of(v[h]) + south_of(v[h])) for h in range(2))
            basis.append(v[0])
        return basis

    basis = [v[own] for v in krylov(0, full)]
    for i in range(3):
        press[i, own, :] = basis[i]
    bulk = []
    for j, (l, r) in enumerate(pairs):
        product = ((diagonal * basis[l]) * basis[r]).reshape(ROWS // EDGE, EDGE, LANES)
        bulk.append(jnp.sum(product[:-1], axis=0))
        rim[j] = product[-1]

    @pl.when(is_top)
    def _():
        settle(fold2.at[0:NLON - 1, 0:FOLD2, :], group_recv.at[0])
        kept = lanes_e <= offset
        near_half = index < LANES // 2
        mine, aside = [], []
        for tile in range(2):
            part = slice(EDGE * tile, EDGE * (tile + 1))
            b_p, b_0, b_m, b_mm = (fold2[s, part, :] for s in (slot_p, slot, slot_m, slot_mm))
            mine.append(turn(jnp.where(kept, b_0, b_m)))
            right = jnp.where(kept, b_m, b_mm)
            left = jnp.where(kept, b_p, b_0)
            aside.append(turn(jnp.where(near_half, right, left)))
        for half, tiles in ((0, mine), (1, aside)):
            north = EDGE + ROWS
            x[0, half, north:north + 3, :] = tiles[0][0:3]
            x[1, half, north:north + 3, :] = tiles[0][3:6]
            x[2, half, north:north + 1, :] = tiles[0][6:7]
            x[3, half, north:north + 1, :] = tiles[0][7:8]
            x[3, half, north + 1:north + 3, :] = tiles[1][0:2]
            x[4, half, north:north + 3, :] = tiles[1][2:5]
        final = slice(EDGE, 2 * EDGE)
        rim_diagonal = 4.0 + ebuf[0, ROWS - EDGE:, :]
        basis = [v[final] for v in krylov(ROWS - EDGE, 3 * EDGE)]
        for i in range(3):
            press[i, ROWS:ROWS + EDGE, :] = basis[i]
        for j, (l, r) in enumerate(pairs):
            rim[j] = (rim_diagonal * basis[l]) * basis[r]

    sub = lax.broadcasted_iota(jnp.int32, (EDGE, LANES), 0)
    table = jnp.zeros((EDGE, LANES), jnp.float32)
    for j in range(len(pairs)):
        line = jnp.sum(bulk[j] + rim[j], axis=0, keepdims=True)
        table = jnp.where(sub == j, line, table)
    table = jnp.sum(table, axis=1, keepdims=True)
    message = jnp.sum(jnp.where(sub == lanes_e, table, 0.0), axis=0, keepdims=True)
    vec[0:1, :] = message
    mine1 = lon_x * (NLAT - 1) + lat

    @pl.when(not_top)
    def _():
        sums1[pl.ds(mine1, 1), :] = message
        spread(vec.at[0:1, :], sums1.at[pl.ds(mine1, 1), :], 2, near)

    @pl.when(is_top)
    def _():
        late1[pl.ds(lon_x, 1), :] = message
        for dz in range(NZ):
            for dx, dy, dc in itertools.product(range(NX), range(NLAT // 2), range(2)):
                if dz or dx or dy or dc:

                    @pl.when(zs[dz] < EARLY * NX)
                    def _(dev=at(dz, dx, dy, dc)):
                        spread(vec.at[0:1, :], crown.at[pl.ds(lon, 1), :], 5, [dev])

        spread(vec.at[0:1, :], late1.at[pl.ds(lon_x, 1), :], 6, near)

    @pl.when(is_top & is_early)
    def _():
        crown[pl.ds(lon, 1), :] = message

    def hear_tracers():
        to_east3.wait_recv()
        to_west3.wait_recv()

        @pl.when(not_low)
        def _():
            to_north3.wait_recv()

        @pl.when(not_top)
        def _():
            to_south3.wait_recv()

    def update(low, rows, parts):
        lane = lane_iota(rows)
        part = slice(low, low + rows)
        wet = wbuf[part, :].astype(jnp.float32)
        rows_3 = []
        if low < ROWS // 2:
            rows_3.append(jnp.where(outer, wide3[0], wide3[1]))
        cut = max(low - ROWS // 2, 0)
        low_w = pltpu.roll(wide3[0, cut:, :], LANES - 2, 1)
        low_e = pltpu.roll(wide3[1, cut:, :], 2, 1)
        rows_3.append(jnp.where(outer[cut:], low_w, low_e))
        joined = jnp.concatenate(rows_3, axis=0)
        below = jnp.zeros((rows + 2 * EDGE, LANES), jnp.float32)
        below_side = jnp.zeros((rows, LANES), jnp.float32)
        mid = slice(EDGE, EDGE + rows)
        for k in range(LEVELS):
            span = spans[k]
            u = uv[0, k, part, :]
            w = uv[1, k, part, :]
            sides = []
            for f in range(2):
                side = pltpu.roll(joined, LANES - (SPAN3 * (f * LEVELS + k) + 2), 1)
                sides.append(side)
                at = EDGE + low
                c = ts[f, k, at:at + rows, :]
                e1 = pltpu.roll(jnp.where(lane == 0, side, c), LANES - 1, 1)
                e2 = pltpu.roll(jnp.where(lane < 2, side, c), LANES - 2, 1)
                w1 = pltpu.roll(jnp.where(lane == LANES - 1, side, c), 1, 1)
                w2 = pltpu.roll(jnp.where(lane >= LANES - 2, side, c), 2, 1)
                n1 = ts[f, k, at + 1:at + rows + 1, :]
                n2 = ts[f, k, at + 2:at + rows + 2, :]
                s1 = ts[f, k, at - 1:at + rows - 1, :]
                s2 = ts[f, k, at - 2:at + rows - 2, :]
                grad_e = (8.0 * (e1 - w1) - (e2 - w2)) * (1.0 / 12.0)
                grad_n = (8.0 * (n1 - s1) - (n2 - s2)) * (1.0 / 12.0)
                laplace = e1 + w1 + n1 + s1 - 4.0 * c
                out = (nt, ns)[f]
                out[k, part, :] = c + wet * (-0.1 * (u * grad_e + w * grad_n) + 0.1 * laplace)
            reach = slice(low, low + rows + 2 * EDGE)
            layer = density(ts[0, k, reach, :], ts[1, k, reach, :]) * span
            level = below + 0.5 * layer
            below = below + layer
            p_n = pltpu.roll(level, rows + 2 * EDGE - 1, 0)[mid]
            p_s = pltpu.roll(level, 1, 0)[mid]
            nv[k, part, :] = wet * (w - 0.05 * (p_n - p_s))
            if parts > 1:
                layer_side = density(sides[0], sides[1]) * span
                level_side = below_side + 0.5 * layer_side
                below_side = below_side + layer_side
                centre = level[mid]
                p_e = pltpu.roll(jnp.where(lane == 0, level_side, centre), LANES - 1, 1)
                p_w = pltpu.roll(jnp.where(lane == LANES - 1, level_side, centre), 1, 1)
                nu[k, part, :] = wet * (u - 0.05 * (p_e - p_w))

    @pl.when(not_top)
    def _():
        hear_tracers()
        update(0, ROWS, 2)

    body_rows = NX * (NLAT - 1)

    @pl.when(is_top)
    def _():
        settle(sums1, group_recv.at[2])

    @pl.when(not_top)
    def _():
        settle(sums1.at[0:body_rows - 1, :], group_recv.at[2])

    total = jnp.sum(sums1[...], axis=0, keepdims=True)
    vec[EDGE:EDGE + 1, :] = total

    @pl.when(is_early)
    def _():
        sums2[pl.ds(lon_z, 1), :] = total

    def cross(row, early):
        for dz in sorted(range(1, NZ), key=lambda o: -hops(o, NZ)):
            bound = EARLY * NX

            @pl.when((zs[dz] < bound) if early else (zs[dz] >= bound))
            def _(dev=at(dz, 0, 0, 0)):
                spread(vec.at[row:row + 1, :], sums2.at[pl.ds(lon_z, 1), :], 3, [dev])

    cross(EDGE, True)

    @pl.when(is_top)
    def _():
        settle(late1.at[0:NX - 1, :], group_recv.at[6])

    @pl.when(not_top)
    def _():
        settle(late1, group_recv.at[6])

    total = total + jnp.sum(late1[...], axis=0, keepdims=True)
    vec[EDGE + 1:EDGE + 2, :] = total

    @pl.when(lon_z >= EARLY)
    def _():
        sums2[pl.ds(lon_z, 1), :] = total

    cross(EDGE + 1, False)

    beside = [(lon - lon_x + lax.rem(lon_x + k, NX), lat) for k in range(1, NX)]
    kept = lane_iota(FOLD3) <= offset

    @pl.when(is_top)
    def _():
        settle(foldz.at[0:NZ - 1], group_recv.at[1])
        base_slot = slot + lon_x + NLON
        row_0 = lax.div(lax.rem(base_slot - (slot & (NX - 1)), NLON), NX)
        row_1 = lax.div(lax.rem(base_slot - 1 - ((slot + NX - 1) & (NX - 1)), NLON), NX)
        joint = jnp.where(kept, foldz[row_0], foldz[row_1])
        own3x[...] = joint
        foldx[lon_x] = joint
        spread(own3x, foldx.at[lon_x], 4, beside)
        hear_tracers()
        update(0, ROWS, 2)

    settle(sums2.at[0:NZ - 1, :], group_recv.at[3])
    vec[EDGE + 2:EDGE + 3, :] = jnp.sum(sums2[...], axis=0, keepdims=True)

    @pl.when(is_early & is_top)
    def _():
        settle(crown.at[0:NLON - 1, :], group_recv.at[5])

    @pl.when(is_early & not_top)
    def _():
        settle(crown, group_recv.at[5])

    @pl.when(is_early)
    def _():
        vec[EDGE + 2:EDGE + 3, :] = vec[EDGE + 2:EDGE + 3, :] + jnp.sum(crown[...], axis=0, keepdims=True)

    total = vec[EDGE + 2:EDGE + 3, :]
    mu = [total[:, j:j + 1] for j in range(6)]

    def gram(a, b, shift):
        out = None
        for i, ai in enumerate(a):
            for j, bj in enumerate(b):
                term = ai * bj * mu[i + j + shift]
                out = term if out is None else out + term
        return out

    one = jnp.ones((1, 1), jnp.float32)
    res, dire, sol = [one], [one], [0.0 * one] * 3
    rz = mu[0]
    for step in range(3):
        alpha = rz / (gram(dire, dire, 0) - gram(dire, dire, 1))
        sol = [sol[i] + alpha * dire[i] if i < len(dire) else sol[i] for i in range(3)]
        if step < 2:
            image = [
                (dire[i] if i < len(dire) else 0.0) - (dire[i - 1] if i else 0.0) for i in range(len(dire) + 1)
            ]
            res = [(res[i] if i < len(res) else 0.0) - alpha * image[i] for i in range(len(image))]
            new = gram(res, res, 0)
            beta = new / rz
            dire = [res[i] + (beta * dire[i] if i < len(dire) else 0.0) for i in range(len(res))]
            rz = new
    surf[...] = sol[0] * press[0, own, :] + sol[1] * press[1, own, :] + sol[2] * press[2, own, :]

    @pl.when(is_top)
    def _():
        settle(foldx.at[0:NX - 1], group_recv.at[4])
        side_0 = slot & (NX - 1)
        side_1 = (slot + NX - 1) & (NX - 1)
        for tile in range(FOLD3 // EDGE):
            part = slice(EDGE * tile, EDGE * (tile + 1))
            turned = turn(jnp.where(kept[part], foldx[side_0, part, :], foldx[side_1, part, :]))
            for i in range(EDGE):
                q, r = (EDGE * tile + i) // 2, (EDGE * tile + i) % 2
                ts[q // LEVELS, q % LEVELS, EDGE + ROWS + 1 - r:EDGE + ROWS + 2 - r, :] = turned[i:i + 1]
        update(ROWS - EDGE, EDGE, 1)

    to_east.wait_send()
    to_west.wait_send()
    to_east3.wait_send()
    to_west3.wait_send()

    @pl.when(not_top)
    def _():
        for send in north_sends:
            send.wait_send()
        to_north3.wait_send()

    @pl.when(not_low)
    def _():
        for send in south_sends:
            send.wait_send()
        to_south3.wait_send()

    @pl.when(is_top)
    def _():
        settle(fold2.at[0:NLON - 1, 0:FOLD2, :], group_send.at[0])
        settle(foldz.at[0:NZ - 1], group_send.at[1])
        settle(foldx.at[0:NX - 1], group_send.at[4])

    @pl.when(is_top & is_early)
    def _():
        settle(wide_sent.at[0:EARLY * NX * NLAT - 1, :], group_send.at[5])

    @pl.when(is_top & (lon_z >= EARLY))
    def _():
        settle(wide_sent, group_send.at[5])

    @pl.when(is_top)
    def _():
        settle(wide_sent.at[0:NX * NLAT - 1, :], group_send.at[6])

    @pl.when(not_top)
    def _():
        settle(wide_sent.at[0:NX * NLAT - 1, :], group_send.at[2])

    settle(sums2.at[0:NZ - 1, :], group_send.at[3])


def store(*refs):
    ins, outs, sem = refs[:5], refs[5:10], refs[10]
    copies = [pltpu.make_async_copy(i, o, sem.at[n]) for n, (i, o) in enumerate(zip(ins, outs))]
    for c in copies:
        c.start()
    for c in copies:
        c.wait()


def body(t, s, u, v, spans, water, opp, weights, anomaly):
    t, s, u, v, water, weights, anomaly, spans, opp = (
        pltpu.with_memory_space_constraint(r, pltpu.HBM) for r in (t, s, u, v, water, weights, anomaly, spans, opp)
    )
    hbm = pl.BlockSpec(memory_space=pltpu.HBM)
    vmem = pl.BlockSpec(memory_space=pltpu.VMEM)
    f32 = jnp.float32
    shapes = [jax.ShapeDtypeStruct((LEVELS, ROWS, LANES), f32)] * 4 + [jax.ShapeDtypeStruct((ROWS, LANES), f32)]
    full = ROWS + 2 * EDGE
    results = pl.pallas_call(
        kernel,
        out_shape=shapes,
        in_specs=[hbm] * 9,
        out_specs=[vmem] * 5,
        scratch_shapes=[
            pltpu.VMEM((2, LEVELS, full, LANES), f32),
            pltpu.VMEM((2, LEVELS, ROWS, LANES), f32),
            pltpu.VMEM((ROWS, LANES), jnp.int32),
            pltpu.VMEM((2, ROWS, LANES), f32),
            pltpu.VMEM((5, 2, full, LANES), f32),
            pltpu.VMEM((ROWS, LANES), f32),
            pltpu.VMEM((2, ROWS // 4, LANES), f32),
            pltpu.VMEM((2, ROWS // 4, LANES), f32),
            pltpu.VMEM((2, 2, EDGE, LANES), f32),
            pltpu.VMEM((2, ROWS // 2, LANES), f32),
            pltpu.VMEM((2, ROWS // 2, LANES), f32),
            pltpu.VMEM((16, LANES), f32),
            pltpu.VMEM((NLON, 16, LANES), f32),
            pltpu.VMEM((FOLD3, LANES), f32),
            pltpu.VMEM((NZ, FOLD3, LANES), f32),
            pltpu.VMEM((FOLD3, LANES), f32),
            pltpu.VMEM((NX, FOLD3, LANES), f32),
            pltpu.VMEM((3, full, LANES), f32),
            pltpu.VMEM((6, EDGE, LANES), f32),
            pltpu.VMEM((2 * EDGE, LANES), f32),
            pltpu.VMEM((NX * (NLAT - 1), LANES), f32),
            pltpu.VMEM((NZ, LANES), f32),
            pltpu.VMEM((NX, LANES), f32),
            pltpu.VMEM((NLON, LANES), f32),
            pltpu.VMEM((EARLY * NX * NLAT, LANES), f32),
            pltpu.SMEM((LEVELS,), f32),
            pltpu.SMEM((LANES,), jnp.int32),
            pltpu.SemaphoreType.DMA((9,)),
            pltpu.SemaphoreType.DMA((12,)),
            pltpu.SemaphoreType.DMA((12,)),
            pltpu.SemaphoreType.DMA((7,)),
            pltpu.SemaphoreType.DMA((7,)),
        ],
        compiler_params=pltpu.CompilerParams(
            collective_id=0, has_side_effects=True, vmem_limit_bytes=40 * 1024 * 1024
        ),
    )(t, s, u, v, water, weights, anomaly, spans, opp)
    anyspec = pl.BlockSpec(memory_space=pl.ANY)
    return pl.pallas_call(
        store,
        out_shape=shapes,
        in_specs=[anyspec] * 5,
        out_specs=[anyspec] * 5,
        scratch_shapes=[pltpu.SemaphoreType.DMA((5,))],
        compiler_params=pltpu.CompilerParams(vmem_limit_bytes=8 * 1024 * 1024),
    )(*results)


def solution(mesh):
    deep = P(None, "lat", "lon")
    flat = P("lat", "lon")
    return jax.shard_map(
        body,
        mesh=mesh,
        in_specs=(deep, deep, deep, deep, P(), flat, P("lon"), flat, flat),
        out_specs=(deep, deep, deep, deep, flat),
        check_vma=False,
    )
```
